32 devices in a mesh: dp: 8 (over z, y), mp: 4 (over x, core).
Axes of the slice: x: 2, y: 2, z: 4, core: 2. Of those that a mesh axis runs over, the one named last changes fastest.
Arguments:
- tokens: bfloat16 [16384, 1024], P(('dp', 'mp')), may hold values from -6 to 6
- counts: int32 [8], P('dp'), may hold values from 1024 to 2048, as said below
- gain_attn: float32 [1024], replicated, may hold values from 0.5 to 1.5
- gain_ffn: float32 [1024], replicated, may hold values from 0.5 to 1.5
- w_qkv: bfloat16 [1024, 3, 1024], P(None, None, 'mp'), may hold values from -0.1875 to 0.1875
- w_out: bfloat16 [1024, 1024], P('mp'), may hold values from -2 to 2
- w_gate_up: bfloat16 [1024, 2, 2816], P(None, None, 'mp'), may hold values from -0.1875 to 0.1875
- w_down: bfloat16 [2816, 1024], P('mp'), may hold values from -0.109375 to 0.109375
- cotangent: bfloat16 [16384, 1024], P(('dp', 'mp')), may hold values from -6 to 6
Outputs:
- latents: float32 [16384, 1024], P(('dp', 'mp'))
- grad_tokens: float32 [16384, 1024], P(('dp', 'mp'))
- grad_gain_attn: float32 [1024], replicated
- grad_gain_ffn: float32 [1024], replicated
- grad_w_qkv: float32 [1024, 3, 1024], P(None, None, 'mp')
- grad_w_out: float32 [1024, 1024], P('mp')
- grad_w_gate_up: float32 [1024, 2, 2816], P(None, None, 'mp')
- grad_w_down: float32 [2816, 1024], P('mp')
The draws below stay inside these ranges and needn't reach their ends.
Inputs may be any that keep to these rules, and one draw needn't show every extreme that they name: `counts`: number of real patches of each sequence; the rest of its 2048 slots are padding. Some sequence has exactly 2048 and some exactly 1024.
All inputs are finite; a program needn't handle non-finite values.
Results may differ from the reference program's by a relative error of at most 0.015.
Values may be sent and summed in bfloat16 or wider, within the bound.
No kernel may reach another device: no remote copies, remote signals or barrier semaphores. Data moves between devices by JAX's collectives and lax.ppermute only.
A program may use at most 192 MiB of HBM per device.

```python
import jax
import jax.numpy as jnp
from jax import lax

D = 1024
H = 16
HD = 64
FF = 2816
LEN = 2048
SEQUENCES = 8
TOKENS = 16384


def draw_counts(key, part):
    key = jax.random.fold_in(key, 11)
    first_key, second_key = jax.random.split(key)
    drawn = jax.random.randint(first_key, (SEQUENCES,), LEN // 2, LEN + 1, dtype=jnp.int32)
    order = jax.random.permutation(second_key, SEQUENCES)
    places = jnp.arange(SEQUENCES, dtype=jnp.int32)
    drawn = jnp.where(places == order[0], LEN, drawn)
    drawn = jnp.where(places == order[1], LEN // 2, drawn)
    return drawn.astype(jnp.int32)


def level_of(key, shape, cuts, low, largest):
    loudness, own = 1.0, jax.random.fold_in(key, 6)
    for dim, blocks in cuts:
        steps = jnp.exp(jax.random.uniform(jax.random.fold_in(own, dim), (blocks,), jnp.float32, low / len(cuts), largest / len(cuts)))
        loudness = loudness * jnp.repeat(steps, shape[dim] // blocks).reshape([-1 if axis == dim else 1 for axis in range(len(shape))])
    return loudness


def bell_draw(own_key, dims, scale, reach, shards=(), held_as=jnp.bfloat16):
    entries = jax.random.normal(own_key, dims, jnp.float32) * scale
    if len(shards) > 0:
        entries = level_of(own_key, dims, shards, -0.22, 0.18) * entries
    return jnp.clip(entries, min=-reach, max=reach).astype(held_as)


def setup_inputs(seed: int = 0) -> dict:
    key_list = jax.random.split(jax.random.key(seed), 10)
    tokens = bell_draw(key_list[0], (TOKENS, D), 1.0, 6.0, ((0, 32),))
    counts = draw_counts(jax.random.fold_in(key_list[9], 71), 0)
    gain_attn = jnp.clip(1.0 + 0.1 * jax.random.normal(key_list[2], (D,), jnp.float32), 0.5, 1.5)
    gain_ffn = jnp.clip(1.0 + 0.1 * jax.random.normal(key_list[3], (D,), jnp.float32), 0.5, 1.5)
    w_qkv = bell_draw(key_list[4], (D, 3, D), D ** -0.5, 0.1875, ((2, 4),))
    w_out = bell_draw(key_list[5], (D, D), (max(D // 128, 2)) ** -0.5, 2.0, ((0, 4),))
    w_gate_up = bell_draw(key_list[6], (D, 2, FF), D ** -0.5, 0.1875, ((2, 4),))
    w_down = bell_draw(key_list[7], (FF, D), FF ** -0.5, 0.109375, ((0, 4),))
    cotangent = bell_draw(key_list[8], (TOKENS, D), 1.0, 6.0, ((0, 32),))
    return dict(tokens=tokens, counts=counts, gain_attn=gain_attn, gain_ffn=gain_ffn, w_qkv=w_qkv, w_out=w_out, w_gate_up=w_gate_up, w_down=w_down, cotangent=cotangent)


EPS = 1e-05
HIGH = lax.Precision.HIGHEST

@jax.custom_vjp
def low(v):
    return lax.optimization_barrier(v.astype(jnp.bfloat16)).astype(jnp.float32)

@jax.custom_vjp
def low_back(v):
    return v

def low_keep(v):
    return (low(v), None)

def low_pass(kept, grad):
    return (grad,)

def back_keep(v):
    return (v, None)

def back_low(kept, grad):
    return (low(grad),)
low.defvjp(low_keep, low_pass)
low_back.defvjp(back_keep, back_low)

def product(left, right):
    return jnp.dot(left, right, precision=HIGH, preferred_element_type=jnp.float32)

def rms_scale(values, gain):
    return values * lax.rsqrt(lax.optimization_barrier(jnp.mean(values * values, axis=-1, keepdims=True)) + EPS) * gain

def block_forward(inputs, gain_attn, gain_ffn, w_qkv, w_out, w_gate_up, w_down, patch_count):
    length = inputs.shape[0]
    normed = low(rms_scale(inputs, gain_attn))

    def project(matrix):
        return low(low_back(product(normed, matrix)))

    def heads_first(values):
        return values.reshape(length, H, HD).transpose(1, 0, 2)
    queries = heads_first(project(w_qkv[:, 0, :]))
    keys = heads_first(project(w_qkv[:, 1, :]))
    values = heads_first(project(w_qkv[:, 2, :]))
    positions = jnp.arange(length, dtype=jnp.int32)
    allowed = (positions[None, :] <= positions[:, None]) & (positions[None, :] < patch_count)

    def one_head(triple):
        head_q, head_k, head_v = triple
        scores = low_back(product(head_q, head_k.T) * HD ** (-0.5))
        scores = jnp.where(allowed, scores, -1e+30)
        weights = low(jax.nn.softmax(scores, axis=-1))
        return product(weights, head_v)
    mixed = lax.map(jax.checkpoint(one_head), (queries, keys, values))
    attended = low(low_back(mixed.transpose(1, 0, 2).reshape(length, D)))
    middle = inputs + low_back(product(attended, w_out))
    normed_ffn = low(rms_scale(middle, gain_ffn))
    gate = low_back(product(normed_ffn, w_gate_up[:, 0, :]))
    up = low_back(product(normed_ffn, w_gate_up[:, 1, :]))
    hidden = low(jax.nn.silu(gate) * up)
    return middle + low_back(product(hidden, w_down))

def reference(tokens, counts, gain_attn, gain_ffn, w_qkv, w_out, w_gate_up, w_down, cotangent):
    matrices = (w_qkv.astype(jnp.float32), w_out.astype(jnp.float32), w_gate_up.astype(jnp.float32), w_down.astype(jnp.float32))
    seq_inputs = tokens.astype(jnp.float32).reshape(SEQUENCES, LEN, D)
    seq_grads = cotangent.astype(jnp.float32).reshape(SEQUENCES, LEN, D)

    def one_sequence(totals, item):
        inputs, upstream, patch_count = item

        def forward(values, first_gain, second_gain, mat_a, mat_b, mat_c, mat_d):
            return block_forward(values, first_gain, second_gain, mat_a, mat_b, mat_c, mat_d, patch_count)
        result, pull = jax.vjp(forward, inputs, gain_attn, gain_ffn, matrices[0], matrices[1], matrices[2], matrices[3])
        grads = pull(upstream)
        updated = tuple((total + grad for total, grad in zip(totals, grads[1:])))
        return (updated, (result, grads[0]))
    start = (jnp.zeros_like(gain_attn), jnp.zeros_like(gain_ffn)) + tuple((jnp.zeros_like(m) for m in matrices))
    totals, (results, input_grads) = lax.scan(one_sequence, start, (seq_inputs, seq_grads, counts))
    return (results.reshape(TOKENS, D), input_grads.reshape(TOKENS, D), totals[0], totals[1], totals[2], totals[3], totals[4], totals[5])
```

```python
import functools

import jax
import jax.numpy as jnp
from jax import lax
from jax.experimental import pallas as pl
from jax.experimental.pallas import tpu as pltpu
from jax.sharding import PartitionSpec as P

HD = 64


EPS = 1e-05


def rms_scale(values, gain):
    return values * lax.rsqrt(jnp.mean(values * values, axis=-1, keepdims=True) + EPS) * gain


LANES=128
LOG2E=1.4426950408889634
NT=(((1,),(1,)),((),()))
TN=(((0,),(0,)),((),()))
f32=jnp.float32; bf16=jnp.bfloat16

def dot(a,b,dims=(((1,),(0,)),((),()))):
    return lax.dot_general(a,b,dims,preferred_element_type=f32)

def head_lanes(rows, parity):
    lane=lax.broadcasted_iota(jnp.int32,(rows,LANES),1)
    return (lane//HD)==parity, lane==(1-parity)*HD

def attn_fwd_kernel(count_ref, qkv_ref, o_ref, lse_ref, kaug, *, length, columns, block):
    h=pl.program_id(0)
    parity=lax.rem(h,2)
    col=pl.multiple_of((h//2)*LANES,LANES)
    c=HD**-0.5*LOG2E
    sel,spare=head_lanes(length,parity)
    row=lax.broadcasted_iota(jnp.int32,(length,LANES),0)
    k=qkv_ref[:,pl.ds(columns+col,LANES)].astype(f32)
    bias=jnp.where(row<count_ref[0],0.0,-1e30)
    kaug[...]=jnp.where(sel,k,jnp.where(spare,bias,0.0)).astype(bf16)
    sel_b,spare_b=head_lanes(block,parity)
    ri=lax.broadcasted_iota(jnp.int32,(block,block),0)
    ci=lax.broadcasted_iota(jnp.int32,(block,block),1)
    for i in range(length//block):
        first=i*block; n=first+block
        rows=pl.ds(first,block)
        q=qkv_ref[rows,pl.ds(col,LANES)].astype(f32)
        q=jnp.where(sel_b,q,jnp.where(spare_b,1.0,0.0)).astype(bf16)
        s_d=dot(q,kaug[first:n],NT)
        s_d=jnp.where(ci<=ri,s_d,-1e30)
        m=jnp.max(s_d,axis=1,keepdims=True)
        if first:
            s_o=dot(q,kaug[:first],NT)
            m=jnp.maximum(m,jnp.max(s_o,axis=1,keepdims=True))
        mc=m*c
        p_d=jnp.exp2(s_d*c-mc)
        l=jnp.sum(p_d,axis=1,keepdims=True)
        v=qkv_ref[first:n,pl.ds(2*columns+col,LANES)]
        o=dot(p_d.astype(bf16),v)
        if first:
            p_o=jnp.exp2(s_o*c-mc)
            l=l+jnp.sum(p_o,axis=1,keepdims=True)
            o=o+dot(p_o.astype(bf16),qkv_ref[:first,pl.ds(2*columns+col,LANES)])
        o=(o/l).astype(bf16)
        out=pl.ds(col,LANES)
        prev=o_ref[rows,out]
        o_ref[rows,out]=jnp.where(sel_b,o,prev)
        lse=mc+jnp.log2(l)
        lse_ref[pl.ds(h,1),first:n]=jnp.transpose(jnp.broadcast_to(lse,(block,LANES)))[0:1]

def attn_fwd(count, qkv, block=256):
    length,three=qkv.shape; columns=three//3; heads=columns//HD
    return pl.pallas_call(
        functools.partial(attn_fwd_kernel,length=length,columns=columns,block=block),
        grid=(heads,),
        out_shape=(jax.ShapeDtypeStruct((length,columns),bf16),jax.ShapeDtypeStruct((heads,length),f32)),
        in_specs=[pl.BlockSpec(memory_space=pltpu.SMEM),pl.BlockSpec((length,three),lambda h:(0,0))],
        out_specs=(pl.BlockSpec((length,columns),lambda h:(0,0)),pl.BlockSpec((heads,length),lambda h:(0,0))),
        scratch_shapes=[pltpu.VMEM((length,LANES),bf16)],
        compiler_params=pltpu.CompilerParams(vmem_limit_bytes=50<<20),
        cost_estimate=pl.CostEstimate(flops=4*length*length*columns,bytes_accessed=2*length*columns*4,transcendentals=length*length*heads//2),
        name="attn_fwd",
    )(count,qkv)

def attn_bwd_kernel(count_ref, qkv_ref, do_ref, o_ref, lse_ref, g_ref, kaug, qaug, dom, dq, *, length, columns, block):
    h=pl.program_id(0)
    parity=lax.rem(h,2)
    col=pl.multiple_of((h//2)*LANES,LANES)
    scale=HD**-0.5
    c=scale*LOG2E
    sel,spare=head_lanes(length,parity)
    row=lax.broadcasted_iota(jnp.int32,(length,LANES),0)
    k=qkv_ref[:,pl.ds(columns+col,LANES)].astype(f32)
    bias=jnp.where(row<count_ref[0],0.0,-1e30)
    kaug[...]=jnp.where(sel,k,jnp.where(spare,bias,0.0)).astype(bf16)
    q=qkv_ref[:,pl.ds(col,LANES)].astype(f32)
    qaug[...]=jnp.where(sel,q,jnp.where(spare,1.0,0.0)).astype(bf16)
    do=jnp.where(sel,do_ref[:,pl.ds(col,LANES)].astype(f32),0.0)
    dom[...]=do.astype(bf16)
    prod=do*o_ref[:,pl.ds(col,LANES)].astype(f32)
    hi=prod.astype(bf16)
    lo=(prod-hi.astype(f32)).astype(bf16)
    ones=jnp.ones((8,LANES),bf16)
    delta=(dot(ones,hi,NT)+dot(ones,lo,NT))[0:1]
    lse=lse_ref[pl.ds(h,1),:]
    sel_b,_=head_lanes(block,parity)
    ki=lax.broadcasted_iota(jnp.int32,(block,block),0)
    qi=lax.broadcasted_iota(jnp.int32,(block,block),1)
    dq[...]=jnp.zeros_like(dq)
    for j in range(length//block):
        first=j*block; last=first+block
        kj=kaug[first:last]
        vj=qkv_ref[first:last,pl.ds(2*columns+col,LANES)]
        def part(a,b,diag):
            s=dot(kj,qaug[a:b],NT)
            if diag: s=jnp.where(ki<=qi,s,-1e30)
            p=jnp.exp2(s*c-lse[:,a:b])
            dp=dot(vj,dom[a:b],NT)
            ds=(p*(dp-delta[:,a:b])).astype(bf16)
            pb=p.astype(bf16)
            dv=dot(pb,dom[a:b])
            dk=dot(ds,qaug[a:b])
            dq[a:b]+=dot(ds,kj,TN)
            return dv,dk
        dv,dk=part(first,last,True)
        if last<length:
            dv2,dk2=part(last,length,False)
            dv=dv+dv2; dk=dk+dk2
        for idx,val in ((1,dk*scale),(2,dv)):
            out=pl.ds(idx*columns+col,LANES)
            g_ref[first:last,out]=jnp.where(sel_b,val.astype(bf16),g_ref[first:last,out])
    out=pl.ds(col,LANES)
    g_ref[:,out]=jnp.where(sel,(dq[...]*scale).astype(bf16),g_ref[:,out])

def attn_bwd(count, qkv, do, o, lse, block=256):
    length,three=qkv.shape; columns=three//3; heads=columns//HD
    whole=lambda *s: pl.BlockSpec(s,lambda h:(0,)*len(s))
    return pl.pallas_call(
        functools.partial(attn_bwd_kernel,length=length,columns=columns,block=block),
        grid=(heads,),
        out_shape=jax.ShapeDtypeStruct((length,three),bf16),
        in_specs=[pl.BlockSpec(memory_space=pltpu.SMEM),whole(length,three),whole(length,columns),whole(length,columns),whole(heads,length)],
        out_specs=whole(length,three),
        scratch_shapes=[pltpu.VMEM((length,LANES),bf16)]*3+[pltpu.VMEM((length,LANES),f32)],
        compiler_params=pltpu.CompilerParams(vmem_limit_bytes=50<<20),
        cost_estimate=pl.CostEstimate(flops=10*length*length*columns,bytes_accessed=2*length*columns*8,transcendentals=length*length*heads//2),
        name="attn_bwd",
    )(count,qkv,do,o,lse)


def on_device(tokens, counts, gain_attn, gain_ffn, w_qkv, w_out, w_gate_up, w_down, cotangent):
    width = tokens.shape[1]
    columns = w_qkv.shape[2]
    hidden_cols = w_gate_up.shape[2]
    inputs = tokens.astype(jnp.float32)
    qkv_flat = w_qkv.reshape(width, 3 * columns)
    gate_up_flat = w_gate_up.reshape(width, 2 * hidden_cols)
    normed_attn = lax.all_gather(
        rms_scale(inputs, gain_attn).astype(jnp.bfloat16), "mp", axis=0, tiled=True
    )
    length = normed_attn.shape[0]
    projected = jnp.dot(normed_attn, qkv_flat, preferred_element_type=jnp.float32).astype(
        jnp.bfloat16
    )
    attended, log_totals = attn_fwd(counts, projected)
    piece = attended
    middle = inputs + lax.psum_scatter(
        jnp.dot(piece, w_out, preferred_element_type=jnp.float32),
        "mp",
        scatter_dimension=0,
        tiled=True,
    )
    normed_ffn = lax.all_gather(
        rms_scale(middle, gain_ffn).astype(jnp.bfloat16), "mp", axis=0, tiled=True
    )
    both = jnp.dot(normed_ffn, gate_up_flat, preferred_element_type=jnp.float32)
    gate = both[:, :hidden_cols]
    up = both[:, hidden_cols:]
    hidden = (jax.nn.silu(gate) * up).astype(jnp.bfloat16)
    piece = hidden
    latents = middle + lax.psum_scatter(
        jnp.dot(piece, w_down, preferred_element_type=jnp.float32).astype(jnp.bfloat16),
        "mp",
        scatter_dimension=0,
        tiled=True,
    ).astype(jnp.float32)
    upstream = cotangent.astype(jnp.float32)
    upstream_all = lax.all_gather(cotangent, "mp", axis=0, tiled=True)
    grad_w_down = jnp.einsum("rf,rd->fd", hidden, upstream_all, preferred_element_type=jnp.float32)
    grad_hidden = jnp.einsum("rd,fd->rf", upstream_all, w_down, preferred_element_type=jnp.float32)

    def swiglu(gate_in, up_in):
        return jax.nn.silu(gate_in) * up_in

    unused, swiglu_pull = jax.vjp(swiglu, gate, up)
    grad_gate, grad_up = swiglu_pull(grad_hidden)
    grad_both = jnp.concatenate([grad_gate, grad_up], axis=1).astype(jnp.bfloat16)
    grad_w_gate_up = jnp.einsum(
        "rd,rc->dc", normed_ffn, grad_both, preferred_element_type=jnp.float32
    ).reshape(width, 2, hidden_cols)
    piece = grad_both
    grad_normed_ffn = lax.psum_scatter(
        jnp.einsum("rc,dc->rd", piece, gate_up_flat, preferred_element_type=jnp.float32).astype(
            jnp.bfloat16
        ),
        "mp",
        scatter_dimension=0,
        tiled=True,
    ).astype(jnp.float32)
    unused, norm_pull = jax.vjp(rms_scale, middle, gain_ffn)
    grad_middle_norm, grad_gain_ffn = norm_pull(grad_normed_ffn)
    grad_middle = upstream + grad_middle_norm
    branch_grad = lax.all_gather(grad_middle.astype(jnp.bfloat16), "mp", axis=0, tiled=True)
    grad_w_out = jnp.einsum("rc,rd->cd", attended, branch_grad, preferred_element_type=jnp.float32)
    grad_attended = jnp.einsum("rd,cd->rc", branch_grad, w_out, preferred_element_type=jnp.float32)
    grad_projected = attn_bwd(
        counts, projected, grad_attended.astype(jnp.bfloat16), attended, log_totals
    )
    grad_w_qkv = jnp.einsum(
        "rd,rc->dc", normed_attn, grad_projected, preferred_element_type=jnp.float32
    ).reshape(width, 3, columns)
    piece = grad_projected
    grad_normed_attn = lax.psum_scatter(
        jnp.einsum("rc,dc->rd", piece, qkv_flat, preferred_element_type=jnp.float32).astype(
            jnp.bfloat16
        ),
        "mp",
        scatter_dimension=0,
        tiled=True,
    ).astype(jnp.float32)
    unused, first_pull = jax.vjp(rms_scale, inputs, gain_attn)
    grad_input_norm, grad_gain_attn = first_pull(grad_normed_attn)
    grad_tokens = grad_middle + grad_input_norm
    grad_w_qkv, grad_w_out, grad_w_gate_up, grad_w_down = [
        lax.psum(grad.astype(jnp.bfloat16), "dp").astype(jnp.float32)
        for grad in (grad_w_qkv, grad_w_out, grad_w_gate_up, grad_w_down)
    ]
    grad_gain_attn, grad_gain_ffn = lax.psum((grad_gain_attn, grad_gain_ffn), ("dp", "mp"))
    return (
        latents,
        grad_tokens,
        grad_gain_attn,
        grad_gain_ffn,
        grad_w_qkv,
        grad_w_out,
        grad_w_gate_up,
        grad_w_down,
    )


def solution(mesh):
    placed = (
        P(("dp", "mp"), None),
        P("dp"),
        P(),
        P(),
        P(None, None, "mp"),
        P("mp", None),
        P(None, None, "mp"),
        P("mp", None),
        P(("dp", "mp"), None),
    )
    return jax.shard_map(
        on_device,
        mesh=mesh,
        in_specs=placed,
        out_specs=(
            P(("dp", "mp"), None),
            P(("dp", "mp"), None),
            P(),
            P(),
            P(None, None, "mp"),
            P("mp", None),
            P(None, None, "mp"),
            P("mp", None),
        ),
        check_vma=False,
    )
```

```python
import functools

import jax
import jax.numpy as jnp
from jax import lax
from jax.experimental import pallas as pl
from jax.experimental.pallas import tpu as pltpu
from jax.sharding import PartitionSpec as P

HD = 64
EPS = 1e-05
LANES = 128
LOG2E = 1.4426950408889634
NN = (((1,), (0,)), ((), ()))
NT = (((1,), (1,)), ((), ()))
TN = (((0,), (0,)), ((), ()))
f32 = jnp.float32
bf16 = jnp.bfloat16
VMEM_LIMIT = 56 << 20


def dot(a, b, dims=NN):
    return lax.dot_general(a, b, dims, preferred_element_type=f32)


def whole(*shape):
    return pl.BlockSpec(shape, lambda *_: (0,) * len(shape))


def smem():
    return pl.BlockSpec(memory_space=pltpu.SMEM)


def shaped(shape, dtype):
    return jax.ShapeDtypeStruct(shape, dtype)


def params():
    return pltpu.CompilerParams(vmem_limit_bytes=VMEM_LIMIT)


def cost(flops, bytes_accessed, transcendentals=0):
    return pl.CostEstimate(
        flops=int(flops), bytes_accessed=int(bytes_accessed), transcendentals=int(transcendentals)
    )


def swap(value, bit, axis="mp"):
    size = lax.axis_size(axis)
    return lax.ppermute(value, axis, [(i, i ^ bit) for i in range(size)])


def after(value, *others):
    return lax.optimization_barrier((value,) + others)[0]


def gather_rel(value):
    far = swap(value, 2)
    near = swap(value, 1)
    return [value, near, far, swap(far, 1)]


def exchange_rel(parts):
    return [parts[0]] + [swap(parts[k], k) for k in (1, 2, 3)]


def add_low(a, b):
    return (a.astype(f32) + b.astype(f32)).astype(bf16)


def scatter_rel(parts):
    far = swap(add_low(parts[2], swap(parts[3], 1)), 2)
    return parts[0], swap(parts[1], 1), far


def head_lanes(rows, parity):
    lane = lax.broadcasted_iota(jnp.int32, (rows, LANES), 1)
    return (lane // HD) == parity, lane == (1 - parity) * HD


def project_kernel(a_ref, b_ref, w_ref, oa_ref, ob_ref):
    oa_ref[...] = dot(a_ref[...], w_ref[...]).astype(bf16)
    ob_ref[...] = dot(b_ref[...], w_ref[...]).astype(bf16)


def project(a, b, w):
    rows, width = a.shape
    out = w.shape[1]
    step = 256
    block = pl.BlockSpec((step, width), lambda i: (i, 0))
    block_out = pl.BlockSpec((step, out), lambda i: (i, 0))
    return pl.pallas_call(
        project_kernel,
        grid=(rows // step,),
        in_specs=[block, block, whole(width, out)],
        out_specs=[block_out, block_out],
        out_shape=[shaped((rows, out), bf16)] * 2,
        compiler_params=params(),
        cost_estimate=cost(4 * rows * width * out, 4 * rows * (width + out)),
        name="project",
    )(a, b, w)


def attn_fwd_kernel(me_ref, count_ref, p0_ref, p1_ref, n2_ref, n3_ref, w_ref, qkv_ref, o_ref, lse_ref, a0_ref, a1_ref, a2_ref, a3_ref, kaug, *, length, columns, block):
    h = pl.program_id(0)
    rows_each = length // 4
    me = me_ref[0]

    def spot(k):
        return pl.ds(pl.multiple_of((me ^ k) * rows_each, rows_each), rows_each)

    @pl.when(h == 0)
    def _():
        qkv_ref[spot(0), :] = p0_ref[...]
        qkv_ref[spot(1), :] = p1_ref[...]
        qkv_ref[spot(2), :] = dot(n2_ref[...], w_ref[...]).astype(bf16)
        qkv_ref[spot(3), :] = dot(n3_ref[...], w_ref[...]).astype(bf16)

    parity = lax.rem(h, 2)
    col = pl.multiple_of((h // 2) * LANES, LANES)
    c = HD**-0.5 * LOG2E
    sel, spare = head_lanes(length, parity)
    row = lax.broadcasted_iota(jnp.int32, (length, LANES), 0)
    k = qkv_ref[:, pl.ds(columns + col, LANES)].astype(f32)
    bias = jnp.where(row < count_ref[0], 0.0, -1e30)
    kaug[...] = jnp.where(sel, k, jnp.where(spare, bias, 0.0)).astype(bf16)
    sel_b, spare_b = head_lanes(block, parity)
    ri = lax.broadcasted_iota(jnp.int32, (block, block), 0)
    ci = lax.broadcasted_iota(jnp.int32, (block, block), 1)
    for i in range(length // block):
        first = i * block
        n = first + block
        rows = pl.ds(first, block)
        q = qkv_ref[rows, pl.ds(col, LANES)].astype(f32)
        q = jnp.where(sel_b, q, jnp.where(spare_b, 1.0, 0.0)).astype(bf16)
        s_d = dot(q, kaug[first:n], NT)
        s_d = jnp.where(ci <= ri, s_d, -1e30)
        m = jnp.max(s_d, axis=1, keepdims=True)
        if first:
            s_o = dot(q, kaug[:first], NT)
            m = jnp.maximum(m, jnp.max(s_o, axis=1, keepdims=True))
        mc = m * c
        p_d = jnp.exp2(s_d * c - mc)
        total = jnp.sum(p_d, axis=1, keepdims=True)
        o = dot(p_d.astype(bf16), qkv_ref[first:n, pl.ds(2 * columns + col, LANES)])
        if first:
            p_o = jnp.exp2(s_o * c - mc)
            total = total + jnp.sum(p_o, axis=1, keepdims=True)
            o = o + dot(p_o.astype(bf16), qkv_ref[:first, pl.ds(2 * columns + col, LANES)])
        o = (o / total).astype(bf16)
        out = pl.ds(col, LANES)
        o_ref[rows, out] = jnp.where(sel_b, o, o_ref[rows, out])
        lse = mc + jnp.log2(total)
        lse_ref[pl.ds(h, 1), first:n] = jnp.transpose(jnp.broadcast_to(lse, (block, LANES)))[0:1]

    @pl.when(h == pl.num_programs(0) - 1)
    def _():
        for k, ref in enumerate((a0_ref, a1_ref, a2_ref, a3_ref)):
            ref[...] = o_ref[spot(k), :]


def attn_fwd(me, count, p0, p1, n2, n3, w, block=256):
    each, width = n2.shape
    length = 4 * each
    three = w.shape[1]
    columns = three // 3
    heads = columns // HD
    return pl.pallas_call(
        functools.partial(attn_fwd_kernel, length=length, columns=columns, block=block),
        grid=(heads,),
        out_shape=[shaped((length, three), bf16), shaped((length, columns), bf16), shaped((heads, length), f32)]
        + [shaped((each, columns), bf16)] * 4,
        in_specs=[smem(), smem(), whole(each, three), whole(each, three), whole(each, width), whole(each, width), whole(width, three)],
        out_specs=[whole(length, three), whole(length, columns), whole(heads, length)] + [whole(each, columns)] * 4,
        scratch_shapes=[pltpu.VMEM((length, LANES), bf16)],
        compiler_params=params(),
        cost_estimate=cost(10 * length * length * columns, 2 * length * columns * 8, length * length * heads // 2),
        name="attn_fwd",
    )(me, count, p0, p1, n2, n3, w)


def attn_bwd_kernel(me_ref, count_ref, qkv_ref, d0_ref, d1_ref, d2_ref, d3_ref, o_ref, lse_ref, g_ref, do_all, kaug, qaug, dom, dq, *, length, columns, block):
    h = pl.program_id(0)
    rows_each = length // 4
    me = me_ref[0]

    @pl.when(h == 0)
    def _():
        for k, ref in enumerate((d0_ref, d1_ref, d2_ref, d3_ref)):
            do_all[pl.ds(pl.multiple_of((me ^ k) * rows_each, rows_each), rows_each), :] = ref[...]

    parity = lax.rem(h, 2)
    col = pl.multiple_of((h // 2) * LANES, LANES)
    scale = HD**-0.5
    c = scale * LOG2E
    sel, spare = head_lanes(length, parity)
    row = lax.broadcasted_iota(jnp.int32, (length, LANES), 0)
    k = qkv_ref[:, pl.ds(columns + col, LANES)].astype(f32)
    bias = jnp.where(row < count_ref[0], 0.0, -1e30)
    kaug[...] = jnp.where(sel, k, jnp.where(spare, bias, 0.0)).astype(bf16)
    q = qkv_ref[:, pl.ds(col, LANES)].astype(f32)
    qaug[...] = jnp.where(sel, q, jnp.where(spare, 1.0, 0.0)).astype(bf16)
    do = jnp.where(sel, do_all[:, pl.ds(col, LANES)].astype(f32), 0.0)
    dom[...] = do.astype(bf16)
    prod = do * o_ref[:, pl.ds(col, LANES)].astype(f32)
    hi = prod.astype(bf16)
    lo = (prod - hi.astype(f32)).astype(bf16)
    ones = jnp.ones((8, LANES), bf16)
    delta = (dot(ones, hi, NT) + dot(ones, lo, NT))[0:1]
    lse = lse_ref[pl.ds(h, 1), :]
    sel_b, _ = head_lanes(block, parity)
    ki = lax.broadcasted_iota(jnp.int32, (block, block), 0)
    qi = lax.broadcasted_iota(jnp.int32, (block, block), 1)
    dq[...] = jnp.zeros_like(dq)
    for j in range(length // block):
        first = j * block
        last = first + block
        kj = kaug[first:last]
        vj = qkv_ref[first:last, pl.ds(2 * columns + col, LANES)]

        def part(a, b, diag):
            s = dot(kj, qaug[a:b], NT)
            if diag:
                s = jnp.where(ki <= qi, s, -1e30)
            p = jnp.exp2(s * c - lse[:, a:b])
            dp = dot(vj, dom[a:b], NT)
            ds = (p * (dp - delta[:, a:b])).astype(bf16)
            dv = dot(p.astype(bf16), dom[a:b])
            dk = dot(ds, qaug[a:b])
            dq[a:b] += dot(ds, kj, TN)
            return dv, dk

        dv, dk = part(first, last, True)
        if last < length:
            dv2, dk2 = part(last, length, False)
            dv = dv + dv2
            dk = dk + dk2
        for idx, val in ((1, dk * scale), (2, dv)):
            out = pl.ds(idx * columns + col, LANES)
            g_ref[first:last, out] = jnp.where(sel_b, val.astype(bf16), g_ref[first:last, out])
    out = pl.ds(col, LANES)
    g_ref[:, out] = jnp.where(sel, (dq[...] * scale).astype(bf16), g_ref[:, out])


def attn_bwd(me, count, qkv, d_list, o, lse, block=256):
    length, three = qkv.shape
    columns = three // 3
    heads = columns // HD
    each = length // 4
    return pl.pallas_call(
        functools.partial(attn_bwd_kernel, length=length, columns=columns, block=block),
        grid=(heads,),
        out_shape=shaped((length, three), bf16),
        in_specs=[smem(), smem(), whole(length, three)] + [whole(each, columns)] * 4 + [whole(length, columns), whole(heads, length)],
        out_specs=whole(length, three),
        scratch_shapes=[pltpu.VMEM((length, columns), bf16)] + [pltpu.VMEM((length, LANES), bf16)] * 3 + [pltpu.VMEM((length, LANES), f32)],
        compiler_params=params(),
        cost_estimate=cost(20 * length * length * columns, 2 * length * columns * 8, length * length * heads // 2),
        name="attn_bwd",
    )(me, count, qkv, *d_list, o, lse)


def middle_kernel(x_ref, a0, a1, a2, a3, w0, w1, w2, w3, gain_ref, mid_ref, normed_ref):
    total = x_ref[...].astype(f32)
    acc = dot(a0[...], w0[...]) + dot(a1[...], w1[...]) + dot(a2[...], w2[...]) + dot(a3[...], w3[...])
    total = total + acc
    mid_ref[...] = total
    r = lax.rsqrt(jnp.mean(total * total, axis=1, keepdims=True) + EPS)
    normed_ref[...] = (total * r * gain_ref[...]).astype(bf16)


def middle_of(tokens, a_list, w_list, gain):
    rows, width = tokens.shape
    cols = a_list[0].shape[1]
    step = 128
    block = pl.BlockSpec((step, width), lambda i: (i, 0))
    block_a = pl.BlockSpec((step, cols), lambda i: (i, 0))
    return pl.pallas_call(
        middle_kernel,
        grid=(rows // step,),
        in_specs=[block] + [block_a] * 4 + [whole(cols, width)] * 4 + [whole(1, width)],
        out_specs=[block, block],
        out_shape=[shaped((rows, width), f32), shaped((rows, width), bf16)],
        compiler_params=params(),
        cost_estimate=cost(2 * rows * width * width, rows * width * 10 + 2 * width * width),
        name="middle",
    )(tokens, *a_list, *w_list, gain)


def ffn_kernel(na, nb, ca, cb, wg, wu, wd, hid_ref, gg_ref, gu_ref, pda, pdb, pga, pgb, xs, cs, *, half):
    i = pl.program_id(0)

    @pl.when(i < half)
    def _():
        xs[...] = na[...]
        cs[...] = ca[...]

    @pl.when(i >= half)
    def _():
        xs[...] = nb[...]
        cs[...] = cb[...]

    x = xs[...]
    gate = dot(x, wg[...])
    up = dot(x, wu[...])
    sig = jax.nn.sigmoid(gate)
    silu = gate * sig
    hidden = (silu * up).astype(bf16)
    hid_ref[...] = hidden
    grad_hidden = dot(cs[...], wd[...], NT)
    gg = (grad_hidden * up * sig * (1.0 + gate * (1.0 - sig))).astype(bf16)
    gu = (grad_hidden * silu).astype(bf16)
    gg_ref[...] = gg
    gu_ref[...] = gu
    down = dot(hidden, wd[...]).astype(bf16)
    grad_normed = (dot(gg, wg[...], NT) + dot(gu, wu[...], NT)).astype(bf16)

    @pl.when(i < half)
    def _():
        pda[...] = down
        pga[...] = grad_normed

    @pl.when(i >= half)
    def _():
        pdb[...] = down
        pgb[...] = grad_normed


def ffn(na, nb, ca, cb, wg, wu, wd):
    rows, width = na.shape
    hid = wg.shape[1]
    step = 256
    half = rows // step
    first = pl.BlockSpec((step, width), lambda i: (jnp.minimum(i, half - 1), 0))
    second = pl.BlockSpec((step, width), lambda i: (jnp.maximum(i - half, 0), 0))
    block_h = pl.BlockSpec((step, hid), lambda i: (i, 0))
    return pl.pallas_call(
        functools.partial(ffn_kernel, half=half),
        grid=(2 * half,),
        in_specs=[first, second, first, second, whole(width, hid), whole(width, hid), whole(hid, width)],
        out_specs=[block_h] * 3 + [first, second] * 2,
        out_shape=[shaped((2 * rows, hid), bf16)] * 3 + [shaped((rows, width), bf16)] * 4,
        scratch_shapes=[pltpu.VMEM((step, width), bf16)] * 2,
        compiler_params=params(),
        cost_estimate=cost(24 * rows * width * hid, 12 * rows * (width + hid), 2 * rows * hid),
        name="ffn",
    )(na, nb, ca, cb, wg, wu, wd)


def grad_middle_kernel(cot, mid, g0, g1, g2, gain, w0, w1, w2, w3, gm_ref, gml_ref, o0, o1, o2, o3, gg_ref):
    dn = g0[...].astype(f32) + g1[...].astype(f32) + g2[...].astype(f32)
    x = mid[...]
    r = lax.rsqrt(jnp.mean(x * x, axis=1, keepdims=True) + EPS)
    e = dn * gain[...]
    gm = cot[...].astype(f32) + r * e - x * (r * r * r * jnp.mean(e * x, axis=1, keepdims=True))
    gm_ref[...] = gm
    low = gm.astype(bf16)
    gml_ref[...] = low
    for w, o in ((w0, o0), (w1, o1), (w2, o2), (w3, o3)):
        o[...] = dot(low, w[...], NT).astype(bf16)
    part = jnp.sum(dn * x * r, axis=0, keepdims=True)

    @pl.when(pl.program_id(0) == 0)
    def _():
        gg_ref[...] = part

    @pl.when(pl.program_id(0) > 0)
    def _():
        gg_ref[...] += part


def grad_middle_of(cot, mid, parts, gain, w_list):
    rows, width = cot.shape
    cols = w_list[0].shape[0]
    step = 128
    block = pl.BlockSpec((step, width), lambda i: (i, 0))
    block_a = pl.BlockSpec((step, cols), lambda i: (i, 0))
    return pl.pallas_call(
        grad_middle_kernel,
        grid=(rows // step,),
        in_specs=[block] * 5 + [whole(1, width)] + [whole(cols, width)] * 4,
        out_specs=[block, block] + [block_a] * 4 + [whole(1, width)],
        out_shape=[shaped((rows, width), f32), shaped((rows, width), bf16)] + [shaped((rows, cols), bf16)] * 4 + [shaped((1, width), f32)],
        compiler_params=params(),
        cost_estimate=cost(2 * rows * width * width, rows * width * 20 + 2 * width * width),
        name="grad_middle",
    )(cot, mid, *parts, gain, *w_list)


def grad_tokens_kernel(gm, tok, g0, g1, g2, gain, out_ref, gg_ref):
    dn = g0[...].astype(f32) + g1[...].astype(f32) + g2[...].astype(f32)
    x = tok[...].astype(f32)
    r = lax.rsqrt(jnp.mean(x * x, axis=1, keepdims=True) + EPS)
    e = dn * gain[...]
    out_ref[...] = gm[...] + r * e - x * (r * r * r * jnp.mean(e * x, axis=1, keepdims=True))
    part = jnp.sum(dn * x * r, axis=0, keepdims=True)

    @pl.when(pl.program_id(0) == 0)
    def _():
        gg_ref[...] = part

    @pl.when(pl.program_id(0) > 0)
    def _():
        gg_ref[...] += part


def grad_tokens_of(gm, tokens, parts, gain):
    rows, width = gm.shape
    step = 128
    block = pl.BlockSpec((step, width), lambda i: (i, 0))
    return pl.pallas_call(
        grad_tokens_kernel,
        grid=(rows // step,),
        in_specs=[block] * 5 + [whole(1, width)],
        out_specs=[block, whole(1, width)],
        out_shape=[shaped((rows, width), f32), shaped((1, width), f32)],
        compiler_params=params(),
        cost_estimate=cost(rows * width * 20, rows * width * 20),
        name="grad_tokens",
    )(gm, tokens, *parts, gain)


def qkv_dgrad_kernel(me_ref, g_ref, w_ref, oa_ref, ob_ref, *, ka, kb):
    each = oa_ref.shape[0]
    me = me_ref[0]
    for k, o in ((ka, oa_ref), (kb, ob_ref)):
        rows = pl.ds(pl.multiple_of((me ^ k) * each, each), each)
        o[...] = dot(g_ref[rows, :], w_ref[...], NT).astype(bf16)


def qkv_dgrad(me, grad, w, ka, kb):
    length, three = grad.shape
    width = w.shape[0]
    each = length // 4
    return pl.pallas_call(
        functools.partial(qkv_dgrad_kernel, ka=ka, kb=kb),
        in_specs=[smem(), pl.BlockSpec(memory_space=pltpu.VMEM), pl.BlockSpec(memory_space=pltpu.VMEM)],
        out_specs=[pl.BlockSpec(memory_space=pltpu.VMEM)] * 2,
        out_shape=[shaped((each, width), bf16)] * 2,
        compiler_params=params(),
        cost_estimate=cost(4 * each * width * three, 2 * (length * three + width * three + 2 * each * width)),
        name="qkv_dgrad",
    )(me, grad, w)


def place(block, me):
    rel = block ^ me
    return (rel & 1) * 4 + ((rel >> 1) & 1) * 2 + (rel >> 2)


def unplace(position, me):
    rel = (position >> 2) | (((position >> 1) & 1) << 1) | ((position & 1) << 2)
    return rel ^ me


def wgrad_down_kernel(dp_ref, ha, hb, c0, c1, c2, c3, o_ref, acc, *, each):
    acc[...] = dot(ha[:each], c0[...], TN)
    acc[...] += dot(ha[each:], c1[...], TN)
    acc[...] += dot(hb[:each], c2[...], TN)
    acc[...] += dot(hb[each:], c3[...], TN)
    wide = o_ref.shape[2]
    for b in range(8):
        o_ref[place(b, dp_ref[0])] = acc[:, b * wide : (b + 1) * wide].astype(bf16)


def wgrad_down(dp, ha, hb, c_list):
    hid = ha.shape[1]
    each, width = c_list[0].shape
    vm = pl.BlockSpec(memory_space=pltpu.VMEM)
    return pl.pallas_call(
        functools.partial(wgrad_down_kernel, each=each),
        in_specs=[smem()] + [vm] * 6,
        out_specs=vm,
        out_shape=shaped((8, hid, width // 8), bf16),
        scratch_shapes=[pltpu.VMEM((hid, width), f32)],
        compiler_params=params(),
        cost_estimate=cost(8 * each * width * hid, 8 * each * (width + hid) + 2 * width * hid),
        name="wgrad_down",
    )(dp, ha, hb, *c_list)


def wgrad_gate_up_kernel(dp_ref, ga, gb, ua, ub, n0, n1, n2, n3, o_ref, acc, *, each):
    tall = o_ref.shape[2]
    for idx, (a, b) in enumerate(((ga, gb), (ua, ub))):
        acc[...] = dot(n0[...], a[:each], TN)
        acc[...] += dot(n1[...], a[each:], TN)
        acc[...] += dot(n2[...], b[:each], TN)
        acc[...] += dot(n3[...], b[each:], TN)
        for blk in range(8):
            o_ref[place(blk, dp_ref[0]), idx] = acc[blk * tall : (blk + 1) * tall].astype(bf16)


def wgrad_gate_up(dp, ga, gb, ua, ub, n_list):
    hid = ga.shape[1]
    each, width = n_list[0].shape
    vm = pl.BlockSpec(memory_space=pltpu.VMEM)
    return pl.pallas_call(
        functools.partial(wgrad_gate_up_kernel, each=each),
        in_specs=[smem()] + [vm] * 8,
        out_specs=vm,
        out_shape=shaped((8, 2, width // 8, hid), bf16),
        scratch_shapes=[pltpu.VMEM((width, hid), f32)],
        compiler_params=params(),
        cost_estimate=cost(16 * each * width * hid, 8 * each * (width + 2 * hid) + 4 * width * hid),
        name="wgrad_gate_up",
    )(dp, ga, gb, ua, ub, *n_list)


def wgrad_out_kernel(gml, a0, a1, a2, a3, o0, o1, o2, o3):
    for a, o in ((a0, o0), (a1, o1), (a2, o2), (a3, o3)):
        o[...] = dot(gml[...], a[...], TN).astype(bf16)


def wgrad_out(gml, a_list):
    each, width = gml.shape
    cols = a_list[0].shape[1]
    vm = pl.BlockSpec(memory_space=pltpu.VMEM)
    return pl.pallas_call(
        wgrad_out_kernel,
        in_specs=[vm] * 5,
        out_specs=[vm] * 4,
        out_shape=[shaped((width, cols), bf16)] * 4,
        compiler_params=params(),
        cost_estimate=cost(8 * each * width * cols, 4 * each * width + 2 * width * width),
        name="wgrad_out",
    )(gml, *a_list)


def wgrad_qkv_kernel(me_ref, dp_ref, g_ref, n0, n1, n2, n3, w0, w1, w2, o_ref, acc, *, each):
    me = me_ref[0]
    for k, n in enumerate((n0, n1, n2, n3)):
        rows = pl.ds(pl.multiple_of((me ^ k) * each, each), each)
        term = dot(n[...], g_ref[rows, :], TN)
        if k:
            acc[...] += term
        else:
            acc[...] = term
    tall = o_ref.shape[1]
    three = g_ref.shape[1]
    for blk in range(8):
        rows = slice(blk * tall, (blk + 1) * tall)
        spot = place(blk, dp_ref[0])
        o_ref[spot, :, :three] = acc[rows].astype(bf16)
        out = w0[rows].astype(f32) + w1[rows].astype(f32) + w2[rows].astype(f32)
        o_ref[spot, :, three:] = out.astype(bf16)


def wgrad_qkv(me, dp, grad, n_list, w_parts):
    length, three = grad.shape
    each, width = n_list[0].shape
    cols = w_parts[0].shape[1]
    vm = pl.BlockSpec(memory_space=pltpu.VMEM)
    return pl.pallas_call(
        functools.partial(wgrad_qkv_kernel, each=each),
        in_specs=[smem(), smem()] + [vm] * 8,
        out_specs=vm,
        out_shape=shaped((8, width // 8, three + cols), bf16),
        scratch_shapes=[pltpu.VMEM((width, three), f32)],
        compiler_params=params(),
        cost_estimate=cost(2 * length * width * three, 2 * length * (width + three) + 2 * width * (three + 4 * cols)),
        name="wgrad_qkv",
    )(me, dp, grad, *n_list, *w_parts)


def reduce_dp(value):
    if lax.axis_size("dp") != 8:
        total = lax.psum(value, "dp")
        return total[0:1], total[1:2], total[2:4], total[4:8]
    kept = value[:4]
    got = swap(value[4:], 1, "dp")
    kept, sent = add_low(kept[:2], got[:2]), add_low(kept[2:], got[2:])
    got = swap(sent, 2, "dp")
    kept, sent = add_low(kept[:1], got[:1]), add_low(kept[1:], got[1:])
    got = swap(sent, 4, "dp")
    own = add_low(kept, got)
    one = swap(own, 4, "dp")
    pair = jnp.concatenate([own, one], axis=0)
    two = swap(pair, 2, "dp")
    four = swap(jnp.concatenate([pair, two], axis=0), 1, "dp")
    return own, one, two, four


def pieces(refs):
    position = 0
    for ref in refs:
        for i in range(ref.shape[0]):
            yield position, ref, i
            position += 1


def finish_down_kernel(dp_ref, p0, p1, p2, p4, o_ref):
    wide = p0.shape[2]
    for position, ref, i in pieces((p0, p1, p2, p4)):
        b = unplace(position, dp_ref[0])
        o_ref[:, pl.ds(pl.multiple_of(b * wide, wide), wide)] = ref[i].astype(f32)


def finish_gate_up_kernel(dp_ref, p0, p1, p2, p4, o_ref):
    tall = p0.shape[2]
    for position, ref, i in pieces((p0, p1, p2, p4)):
        b = unplace(position, dp_ref[0])
        rows = pl.ds(pl.multiple_of(b * tall, tall), tall)
        for idx in range(2):
            o_ref[rows, idx, :] = ref[i, idx].astype(f32)


def finish_qkv_kernel(dp_ref, p0, p1, p2, p4, o_ref, out_ref):
    tall = p0.shape[1]
    cols = out_ref.shape[0]
    for position, ref, i in pieces((p0, p1, p2, p4)):
        b = unplace(position, dp_ref[0])
        rows = pl.ds(pl.multiple_of(b * tall, tall), tall)
        for idx in range(3):
            o_ref[rows, idx, :] = ref[i, :, idx * cols : (idx + 1) * cols].astype(f32)
        out_ref[:, rows] = jnp.transpose(ref[i, :, 3 * cols :].astype(f32))


def finish(kernel, dp, parts, shapes, name):
    vm = pl.BlockSpec(memory_space=pltpu.VMEM)
    return pl.pallas_call(
        kernel,
        in_specs=[smem()] + [vm] * 4,
        out_specs=[vm] * len(shapes),
        out_shape=[shaped(s, f32) for s in shapes],
        compiler_params=params(),
        cost_estimate=cost(1e6, 6 * sum(p.size for p in parts)),
        name=name,
    )(dp, *parts)


def sum_all(value):
    for axis in ("mp", "dp"):
        size = lax.axis_size(axis)
        bit = 1
        while bit < size:
            value = value + swap(value, bit, axis)
            bit *= 2
    return value


def rms_scale(values, gain):
    return values * lax.rsqrt(jnp.mean(values * values, axis=-1, keepdims=True) + EPS) * gain


def on_device(tokens, counts, gain_attn, gain_ffn, w_qkv, w_out, w_gate_up, w_down, cotangent):
    rows, width = tokens.shape
    columns = w_qkv.shape[2]
    hid = w_gate_up.shape[2]
    me = lax.axis_index("mp").astype(jnp.int32).reshape(1)
    dp = jnp.zeros((1,), jnp.int32)
    if lax.axis_size("dp") == 8:
        dp = lax.axis_index("dp").astype(jnp.int32).reshape(1)
    gain_a = gain_attn.reshape(1, width)
    gain_f = gain_ffn.reshape(1, width)
    qkv_w = w_qkv.reshape(width, 3 * columns)
    gate_w = w_gate_up[:, 0, :]
    up_w = w_gate_up[:, 1, :]

    normed = rms_scale(tokens.astype(f32), gain_attn).astype(bf16)
    n = gather_rel(normed)
    p0, p1 = project(n[0], n[1], qkv_w)
    out_w = gather_rel(after(w_out, n[2]))
    cot = gather_rel(after(cotangent, out_w[2]))
    qkv, attended, lse, *a = attn_fwd(me, counts, p0, p1, n[2], n[3], qkv_w)
    a = exchange_rel(a)
    middle, normed_ffn = middle_of(tokens, a, out_w, gain_f)
    m = gather_rel(normed_ffn)
    hid_a, gg_a, gu_a, d0, d1, g0, g1 = ffn(m[0], m[1], cot[0], cot[1], gate_w, up_w, w_down)
    hid_b, gg_b, gu_b, d2, d3, g2, g3 = ffn(m[2], m[3], cot[2], cot[3], gate_w, up_w, w_down)
    s = scatter_rel((g0, g1, g2, g3))
    down = wgrad_down(dp, hid_a, hid_b, cot)
    down = reduce_dp(down)
    gate_up = reduce_dp(wgrad_gate_up(dp, gg_a, gg_b, gu_a, gu_b, m))
    grad_middle, low, *ga, gain_f_part = grad_middle_of(cotangent, middle, s, gain_f, out_w)
    d_list = exchange_rel(ga)
    lat = scatter_rel([after(v, d_list[2], d_list[3]) for v in (d0, d1, d2, d3)])
    latents = middle + lat[0].astype(f32) + lat[1].astype(f32) + lat[2].astype(f32)
    w_parts = scatter_rel(wgrad_out(low, a))
    grad = attn_bwd(me, counts, qkv, d_list, attended, lse)
    t2, t3 = qkv_dgrad(me, grad, qkv_w, 2, 3)
    t0, t1 = qkv_dgrad(me, grad, qkv_w, 0, 1)
    t = scatter_rel((t0, t1, t2, t3))
    last = reduce_dp(wgrad_qkv(me, dp, grad, n, w_parts))
    grad_tokens, gain_a_part = grad_tokens_of(grad_middle, tokens, t, gain_a)
    gains = sum_all(jnp.concatenate([gain_a_part, gain_f_part], axis=0))
    (grad_w_down,) = finish(finish_down_kernel, dp, down, [(hid, width)], "finish_down")
    (grad_w_gate_up,) = finish(finish_gate_up_kernel, dp, gate_up, [(width, 2, hid)], "finish_gate_up")
    grad_w_qkv, grad_w_out = finish(finish_qkv_kernel, dp, last, [(width, 3, columns), (columns, width)], "finish_qkv")
    return (
        latents,
        grad_tokens,
        gains[0],
        gains[1],
        grad_w_qkv,
        grad_w_out,
        grad_w_gate_up,
        grad_w_down,
    )


def solution(mesh):
    placed = (
        P(("dp", "mp"), None),
        P("dp"),
        P(),
        P(),
        P(None, None, "mp"),
        P("mp", None),
        P(None, None, "mp"),
        P("mp", None),
        P(("dp", "mp"), None),
    )
    return jax.shard_map(
        on_device,
        mesh=mesh,
        in_specs=placed,
        out_specs=(
            P(("dp", "mp"), None),
            P(("dp", "mp"), None),
            P(),
            P(),
            P(None, None, "mp"),
            P("mp", None),
            P(None, None, "mp"),
            P("mp", None),
        ),
        check_vma=False,
    )
```

```python
import functools

import jax
import jax.numpy as jnp
from jax import lax
from jax.experimental import pallas as pl
from jax.experimental.pallas import tpu as pltpu
from jax.sharding import PartitionSpec as P

HD = 64
EPS = 1e-05
LANES = 128
LOG2E = 1.4426950408889634
NN = (((1,), (0,)), ((), ()))
NT = (((1,), (1,)), ((), ()))
TN = (((0,), (0,)), ((), ()))
f32 = jnp.float32
bf16 = jnp.bfloat16
VMEM_LIMIT = 60 << 20
SHARE = 1


def dot(a, b, dims=NN):
    return lax.dot_general(a, b, dims, preferred_element_type=f32)


def whole(*shape):
    return pl.BlockSpec(shape, lambda *_: (0,) * len(shape))


def smem():
    return pl.BlockSpec(memory_space=pltpu.SMEM)


def shaped(shape, dtype):
    return jax.ShapeDtypeStruct(shape, dtype)


def params():
    return pltpu.CompilerParams(vmem_limit_bytes=VMEM_LIMIT)


def cost(flops, bytes_accessed, transcendentals=0):
    return pl.CostEstimate(
        flops=int(flops * SHARE), bytes_accessed=int(bytes_accessed * SHARE), transcendentals=int(transcendentals * SHARE)
    )


def swap(value, bit, axis="mp"):
    size = lax.axis_size(axis)
    return lax.ppermute(value, axis, [(i, i ^ bit) for i in range(size)])


def after(value, *others):
    return lax.optimization_barrier((value,) + others)[0]


def join(*values):
    return lax.optimization_barrier(values)


def far_of(value):
    return swap(value, 2)


def exchange_rel(parts):
    return [parts[0]] + [swap(parts[k], k) for k in (1, 2, 3)]


def add_low(a, b):
    return (a.astype(f32) + b.astype(f32)).astype(bf16)


def head_lanes(rows, parity):
    lane = lax.broadcasted_iota(jnp.int32, (rows, LANES), 1)
    return (lane // HD) == parity, lane == (1 - parity) * HD


def norm_kernel(x_ref, gain_ref, o_ref):
    x = x_ref[...].astype(f32)
    r = lax.rsqrt(jnp.mean(x * x, axis=1, keepdims=True) + EPS)
    o_ref[...] = (x * r * gain_ref[...]).astype(bf16)


def norm(x, gain):
    rows, width = x.shape
    step = 128
    block = pl.BlockSpec((step, width), lambda i: (i, 0))
    return pl.pallas_call(
        norm_kernel,
        grid=(rows // step,),
        in_specs=[block, whole(1, width)],
        out_specs=block,
        out_shape=shaped((rows, width), bf16),
        compiler_params=params(),
        cost_estimate=cost(rows * width * 8, rows * width * 4),
        name="norm",
    )(x, gain)


def project_kernel(a_ref, b_ref, w_ref, oa_ref, ob_ref):
    cols = w_ref.shape[2]
    for x, o in ((a_ref, oa_ref), (b_ref, ob_ref)):
        for i in range(3):
            o[:, i * cols : (i + 1) * cols] = dot(x[...], w_ref[i]).astype(bf16)


def project(a, b, w):
    rows, width = a.shape
    cols = w.shape[2]
    step = 256
    block = pl.BlockSpec((step, width), lambda i: (i, 0))
    block_out = pl.BlockSpec((step, 3 * cols), lambda i: (i, 0))
    return pl.pallas_call(
        project_kernel,
        grid=(rows // step,),
        in_specs=[block, block, whole(3, width, cols)],
        out_specs=[block_out, block_out],
        out_shape=[shaped((rows, 3 * cols), bf16)] * 2,
        compiler_params=params(),
        cost_estimate=cost(12 * rows * width * cols, 4 * rows * (width + 3 * cols)),
        name="project",
    )(a, b, w)


def attn_fwd_kernel(me_ref, count_ref, p0_ref, p1_ref, n2_ref, n3_ref, w_ref, qkv_ref, o_ref, lse_ref, a0_ref, a1_ref, a2_ref, a3_ref, kaug, *, length, columns, block):
    h = pl.program_id(0)
    rows_each = length // 4
    me = me_ref[0]

    def spot(k):
        return pl.ds(pl.multiple_of((me ^ k) * rows_each, rows_each), rows_each)

    @pl.when(h == 0)
    def _():
        qkv_ref[spot(0), :] = p0_ref[...]
        qkv_ref[spot(1), :] = p1_ref[...]
        for k, n in ((2, n2_ref), (3, n3_ref)):
            for i in range(3):
                qkv_ref[spot(k), i * columns : (i + 1) * columns] = dot(n[...], w_ref[i]).astype(bf16)

    parity = lax.rem(h, 2)
    col = pl.multiple_of((h // 2) * LANES, LANES)
    c = HD**-0.5 * LOG2E
    sel, spare = head_lanes(length, parity)
    row = lax.broadcasted_iota(jnp.int32, (length, LANES), 0)
    k = qkv_ref[:, pl.ds(columns + col, LANES)].astype(f32)
    bias = jnp.where(row < count_ref[0], 0.0, -1e30)
    kaug[...] = jnp.where(sel, k, jnp.where(spare, bias, 0.0)).astype(bf16)
    sel_b, spare_b = head_lanes(block, parity)
    ri = lax.broadcasted_iota(jnp.int32, (block, block), 0)
    ci = lax.broadcasted_iota(jnp.int32, (block, block), 1)
    for i in range(length // block):
        first = i * block
        n = first + block
        rows = pl.ds(first, block)
        q = qkv_ref[rows, pl.ds(col, LANES)].astype(f32)
        q = jnp.where(sel_b, q, jnp.where(spare_b, 1.0, 0.0)).astype(bf16)
        s_d = dot(q, kaug[first:n], NT)
        s_d = jnp.where(ci <= ri, s_d, -1e30)
        m = jnp.max(s_d, axis=1, keepdims=True)
        if first:
            s_o = dot(q, kaug[:first], NT)
            m = jnp.maximum(m, jnp.max(s_o, axis=1, keepdims=True))
        mc = m * c
        p_d = jnp.exp2(s_d * c - mc)
        total = jnp.sum(p_d, axis=1, keepdims=True)
        o = dot(p_d.astype(bf16), qkv_ref[first:n, pl.ds(2 * columns + col, LANES)])
        if first:
            p_o = jnp.exp2(s_o * c - mc)
            total = total + jnp.sum(p_o, axis=1, keepdims=True)
            o = o + dot(p_o.astype(bf16), qkv_ref[:first, pl.ds(2 * columns + col, LANES)])
        o = (o / total).astype(bf16)
        out = pl.ds(col, LANES)
        o_ref[rows, out] = jnp.where(sel_b, o, o_ref[rows, out])
        lse = mc + jnp.log2(total)
        lse_ref[pl.ds(h, 1), first:n] = jnp.transpose(jnp.broadcast_to(lse, (block, LANES)))[0:1]

    @pl.when(h == pl.num_programs(0) - 1)
    def _():
        for k, ref in enumerate((a0_ref, a1_ref, a2_ref, a3_ref)):
            ref[...] = o_ref[spot(k), :]


def attn_fwd(me, count, p0, p1, n2, n3, w, block=256):
    each, width = n2.shape
    length = 4 * each
    columns = w.shape[2]
    three = 3 * columns
    heads = columns // HD
    return pl.pallas_call(
        functools.partial(attn_fwd_kernel, length=length, columns=columns, block=block),
        grid=(heads,),
        out_shape=[shaped((length, three), bf16), shaped((length, columns), bf16), shaped((heads, length), f32)]
        + [shaped((each, columns), bf16)] * 4,
        in_specs=[smem(), smem(), whole(each, three), whole(each, three), whole(each, width), whole(each, width), whole(3, width, columns)],
        out_specs=[whole(length, three), whole(length, columns), whole(heads, length)] + [whole(each, columns)] * 4,
        scratch_shapes=[pltpu.VMEM((length, LANES), bf16)],
        compiler_params=params(),
        cost_estimate=cost(10 * length * length * columns, 2 * length * columns * 8, length * length * heads // 2),
        name="attn_fwd",
    )(me, count, p0, p1, n2, n3, w)


def attn_bwd_kernel(me_ref, count_ref, q_ref, k_ref, v_ref, d0_ref, d1_ref, d2_ref, d3_ref, o_ref, lse_ref, *rest, length, block, pair):
    g_ref, do_all, kaug, qaug, dom, dq = rest[-6:]
    parity = pl.program_id(0)
    rows_each = length // 4
    me = me_ref[0]

    @pl.when(parity == 0)
    def _():
        for k, ref in enumerate((d0_ref, d1_ref, d2_ref, d3_ref)):
            do_all[pl.ds(pl.multiple_of((me ^ k) * rows_each, rows_each), rows_each), :] = ref[...]

    scale = HD**-0.5
    c = scale * LOG2E
    sel, spare = head_lanes(length, parity)
    row = lax.broadcasted_iota(jnp.int32, (length, LANES), 0)
    bias = jnp.where(row < count_ref[0], 0.0, -1e30)
    kaug[...] = jnp.where(sel, k_ref[...].astype(f32), jnp.where(spare, bias, 0.0)).astype(bf16)
    qaug[...] = jnp.where(sel, q_ref[...].astype(f32), jnp.where(spare, 1.0, 0.0)).astype(bf16)
    do = jnp.where(sel, do_all[...].astype(f32), 0.0)
    dom[...] = do.astype(bf16)
    prod = do * o_ref[...].astype(f32)
    hi = prod.astype(bf16)
    lo = (prod - hi.astype(f32)).astype(bf16)
    ones = jnp.ones((8, LANES), bf16)
    delta = (dot(ones, hi, NT) + dot(ones, lo, NT))[0:1]
    lse = lse_ref[pl.ds(2 * pair + parity, 1), :]
    sel_b, _ = head_lanes(block, parity)
    ki = lax.broadcasted_iota(jnp.int32, (block, block), 0)
    qi = lax.broadcasted_iota(jnp.int32, (block, block), 1)
    dq[...] = jnp.zeros_like(dq)
    for j in range(length // block):
        first = j * block
        last = first + block
        kj = kaug[first:last]
        vj = v_ref[first:last]

        def part(a, b, diag):
            s = dot(kj, qaug[a:b], NT)
            if diag:
                s = jnp.where(ki <= qi, s, -1e30)
            p = jnp.exp2(s * c - lse[:, a:b])
            dp = dot(vj, dom[a:b], NT)
            ds = (p * (dp - delta[:, a:b])).astype(bf16)
            dv = dot(p.astype(bf16), dom[a:b])
            dk = dot(ds, qaug[a:b])
            dq[a:b] += dot(ds, kj, TN)
            return dv, dk

        dv, dk = part(first, last, True)
        if last < length:
            dv2, dk2 = part(last, length, False)
            dv = dv + dv2
            dk = dk + dk2
        for idx, val in ((1, dk * scale), (2, dv)):
            out = slice(idx * LANES, (idx + 1) * LANES)
            g_ref[first:last, out] = jnp.where(sel_b, val.astype(bf16), g_ref[first:last, out])
    g_ref[:, :LANES] = jnp.where(sel, (dq[...] * scale).astype(bf16), g_ref[:, :LANES])


def attn_bwd(me, count, qkv, d_list, o, lse, pair, deps=(), block=256):
    length, three = qkv.shape
    columns = three // 3
    heads = columns // HD
    pairs = columns // LANES
    each = length // 4

    def part(rows, col):
        return pl.BlockSpec((rows, LANES), lambda i: (0, col))

    return pl.pallas_call(
        functools.partial(attn_bwd_kernel, length=length, block=block, pair=pair),
        grid=(2,),
        out_shape=shaped((length, 3 * LANES), bf16),
        in_specs=[smem(), smem()]
        + [part(length, i * pairs + pair) for i in range(3)]
        + [part(each, pair)] * 4
        + [part(length, pair), whole(heads, length)]
        + [pl.BlockSpec(memory_space=pl.ANY)] * len(deps),
        out_specs=whole(length, 3 * LANES),
        scratch_shapes=[pltpu.VMEM((length, LANES), bf16)] * 4 + [pltpu.VMEM((length, LANES), f32)],
        compiler_params=params(),
        cost_estimate=cost(20 * length * length * LANES, 2 * length * LANES * 8, length * length),
        name="attn_bwd",
    )(me, count, qkv, qkv, qkv, *d_list, o, lse, *deps)


def middle_kernel(x_ref, a0, a1, a2, a3, w0, w1, w2, w3, gain_ref, mid_ref, normed_ref):
    total = x_ref[...].astype(f32)
    acc = dot(a0[...], w0[...]) + dot(a1[...], w1[...]) + dot(a2[...], w2[...]) + dot(a3[...], w3[...])
    total = total + acc
    mid_ref[...] = total
    r = lax.rsqrt(jnp.mean(total * total, axis=1, keepdims=True) + EPS)
    normed_ref[...] = (total * r * gain_ref[...]).astype(bf16)


def middle_of(tokens, a_list, w_list, gain):
    rows, width = tokens.shape
    cols = a_list[0].shape[1]
    step = 256
    block = pl.BlockSpec((step, width), lambda i: (i, 0))
    block_a = pl.BlockSpec((step, cols), lambda i: (i, 0))
    return pl.pallas_call(
        middle_kernel,
        grid=(rows // step,),
        in_specs=[block] + [block_a] * 4 + [whole(cols, width)] * 4 + [whole(1, width)],
        out_specs=[block, block],
        out_shape=[shaped((rows, width), f32), shaped((rows, width), bf16)],
        compiler_params=params(),
        cost_estimate=cost(2 * rows * width * width, rows * width * 10 + 2 * width * width),
        name="middle",
    )(tokens, *a_list, *w_list, gain)


def ffn_kernel(na, nb, ca, cb, w, wd, hid_ref, gg_ref, gu_ref, pda, pdb, pga, pgb, xs, cs, *, half):
    i = pl.program_id(0)

    @pl.when(i < half)
    def _():
        xs[...] = na[...]
        cs[...] = ca[...]

    @pl.when(i >= half)
    def _():
        xs[...] = nb[...]
        cs[...] = cb[...]

    x = xs[...]
    gate = dot(x, w[0], NT)
    up = dot(x, w[1], NT)
    grad_hidden = dot(cs[...], wd[...], NT)
    sig = jax.nn.sigmoid(gate)
    silu = gate * sig
    hidden = (silu * up).astype(bf16)
    hid_ref[...] = hidden
    gg = (grad_hidden * up * (sig * (1.0 + gate * (1.0 - sig)))).astype(bf16)
    gu = (grad_hidden * silu).astype(bf16)
    gg_ref[...] = gg
    gu_ref[...] = gu
    down = dot(hidden, wd[...]).astype(bf16)
    grad_normed = (dot(gg, w[0]) + dot(gu, w[1])).astype(bf16)

    @pl.when(i < half)
    def _():
        pda[...] = down
        pga[...] = grad_normed

    @pl.when(i >= half)
    def _():
        pdb[...] = down
        pgb[...] = grad_normed


def ffn(na, nb, ca, cb, w, wd):
    rows, width = na.shape
    hid = wd.shape[0]
    step = 256
    half = rows // step
    first = pl.BlockSpec((step, width), lambda i: (jnp.minimum(i, half - 1), 0))
    second = pl.BlockSpec((step, width), lambda i: (jnp.maximum(i - half, 0), 0))
    block_h = pl.BlockSpec((step, hid), lambda i: (i, 0))
    return pl.pallas_call(
        functools.partial(ffn_kernel, half=half),
        grid=(2 * half,),
        in_specs=[first, second, first, second, whole(2, hid, width), whole(hid, width)],
        out_specs=[block_h] * 3 + [first, second] * 2,
        out_shape=[shaped((2 * rows, hid), bf16)] * 3 + [shaped((rows, width), bf16)] * 4,
        scratch_shapes=[pltpu.VMEM((step, width), bf16)] * 2,
        compiler_params=params(),
        cost_estimate=cost(24 * rows * width * hid, 12 * rows * (width + hid), 2 * rows * hid),
        name="ffn",
    )(na, nb, ca, cb, w, wd)


def grad_middle_kernel(cot, mid, g0, g1, g2, gain, w0, w1, w2, w3, gm_ref, gml_ref, o0, o1, o2, o3):
    dn = g0[...].astype(f32) + g1[...].astype(f32) + g2[...].astype(f32)
    x = mid[...]
    r = lax.rsqrt(jnp.mean(x * x, axis=1, keepdims=True) + EPS)
    e = dn * gain[...]
    gm = cot[...].astype(f32) + r * e - x * (r * r * r * jnp.mean(e * x, axis=1, keepdims=True))
    gm_ref[...] = gm
    low = gm.astype(bf16)
    gml_ref[...] = low
    for w, o in ((w0, o0), (w1, o1), (w2, o2), (w3, o3)):
        o[...] = dot(low, w[...], NT).astype(bf16)


def grad_middle_of(cot, mid, parts, gain, w_list):
    rows, width = cot.shape
    cols = w_list[0].shape[0]
    step = 256
    block = pl.BlockSpec((step, width), lambda i: (i, 0))
    block_a = pl.BlockSpec((step, cols), lambda i: (i, 0))
    return pl.pallas_call(
        grad_middle_kernel,
        grid=(rows // step,),
        in_specs=[block] * 5 + [whole(1, width)] + [whole(cols, width)] * 4,
        out_specs=[block, block] + [block_a] * 4,
        out_shape=[shaped((rows, width), f32), shaped((rows, width), bf16)] + [shaped((rows, cols), bf16)] * 4,
        compiler_params=params(),
        cost_estimate=cost(2 * rows * width * width, rows * width * 20 + 2 * width * width),
        name="grad_middle",
    )(cot, mid, *parts, gain, *w_list)


def grad_tokens_kernel(gm, tok, g0, g1, g2, gain, out_ref):
    dn = g0[...].astype(f32) + g1[...].astype(f32) + g2[...].astype(f32)
    x = tok[...].astype(f32)
    r = lax.rsqrt(jnp.mean(x * x, axis=1, keepdims=True) + EPS)
    e = dn * gain[...]
    out_ref[...] = gm[...] + r * e - x * (r * r * r * jnp.mean(e * x, axis=1, keepdims=True))


def grad_tokens_of(gm, tokens, parts, gain):
    rows, width = gm.shape
    step = 128
    block = pl.BlockSpec((step, width), lambda i: (i, 0))
    return pl.pallas_call(
        grad_tokens_kernel,
        grid=(rows // step,),
        in_specs=[block] * 5 + [whole(1, width)],
        out_specs=block,
        out_shape=shaped((rows, width), f32),
        compiler_params=params(),
        cost_estimate=cost(rows * width * 20, rows * width * 20),
        name="grad_tokens",
    )(gm, tokens, *parts, gain)


def qkv_dgrad_kernel(me_ref, g0_ref, g1_ref, w_ref, oa_ref, ob_ref, *, ka, kb):
    each = oa_ref.shape[0]
    me = me_ref[0]
    for k, o in ((ka, oa_ref), (kb, ob_ref)):
        rows = pl.ds(pl.multiple_of((me ^ k) * each, each), each)
        total = None
        for i in range(3):
            cols = slice(i * LANES, (i + 1) * LANES)
            g = jnp.concatenate([g0_ref[rows, cols], g1_ref[rows, cols]], axis=1)
            term = dot(g, w_ref[i], NT)
            total = term if total is None else total + term
        o[...] = total.astype(bf16)


def qkv_dgrad(me, g0, g1, w, ka, kb):
    length, three = g0.shape
    width = w.shape[1]
    each = length // 4
    vm = pl.BlockSpec(memory_space=pltpu.VMEM)
    return pl.pallas_call(
        functools.partial(qkv_dgrad_kernel, ka=ka, kb=kb),
        in_specs=[smem()] + [vm] * 3,
        out_specs=[vm] * 2,
        out_shape=[shaped((each, width), bf16)] * 2,
        compiler_params=params(),
        cost_estimate=cost(8 * each * width * three, 2 * (2 * length * three + 2 * width * three + 2 * each * width)),
        name="qkv_dgrad",
    )(me, g0, g1, w)


def block_of(y, z, me):
    return (2 * z + y) ^ me


def spot_of(y, z, lead):
    if lead == "y":
        return y, (z & 1) * 2 + (z >> 1)
    return z & 1, y * 2 + (z >> 1)


def wgrad_cols_kernel(dp_ref, ha, hb, c0, c1, c2, c3, *rest, each, lead):
    acc = rest[-1]
    halves = rest[-3:-1]
    acc[...] = dot(ha[:each], c0[...], TN)
    acc[...] += dot(ha[each:], c1[...], TN)
    acc[...] += dot(hb[:each], c2[...], TN)
    acc[...] += dot(hb[each:], c3[...], TN)
    wide = halves[0].shape[2]
    for z in range(4):
        for y in range(2):
            b = block_of(y, z, dp_ref[0])
            half, spot = spot_of(y, z, lead)
            halves[half][spot] = acc[:, pl.ds(pl.multiple_of(b * wide, wide), wide)].astype(bf16)
    if len(rest) > 3:
        w_ref, part_ref = rest[:2]
        part_ref[...] = jnp.sum(acc[...] * w_ref[0].astype(f32), axis=0, keepdims=True)


def wgrad_cols(dp, ha, hb, c_list, w=None, index=0, lead="y"):
    hid = ha.shape[1]
    each, width = c_list[0].shape
    extra = 0 if w is None else 1
    half = shaped((4, hid, width // 8), bf16)
    return pl.pallas_call(
        functools.partial(wgrad_cols_kernel, each=each, lead=lead),
        grid=(1,),
        in_specs=[smem(), whole(*ha.shape), whole(*hb.shape)] + [whole(each, width)] * 4 + [pl.BlockSpec((1, hid, width), lambda i: (index, 0, 0))] * extra,
        out_specs=[whole(1, width)] * extra + [whole(*half.shape)] * 2,
        out_shape=[shaped((1, width), f32)] * extra + [half] * 2,
        scratch_shapes=[pltpu.VMEM((hid, width), f32)],
        compiler_params=params(),
        cost_estimate=cost(8 * each * width * hid, 8 * each * (width + hid) + 2 * width * hid),
        name="wgrad_cols",
    )(dp, ha, hb, *c_list, *([w] * extra))


def wgrad_out_kernel(gml, a0, a1, a2, a3, o0, o1, o2, o3):
    for a, o in ((a0, o0), (a1, o1), (a2, o2), (a3, o3)):
        o[...] = dot(a[...], gml[...], TN).astype(bf16)


def wgrad_out(gml, a_list):
    each, width = gml.shape
    cols = a_list[0].shape[1]
    vm = pl.BlockSpec(memory_space=pltpu.VMEM)
    return pl.pallas_call(
        wgrad_out_kernel,
        in_specs=[vm] * 5,
        out_specs=[vm] * 4,
        out_shape=[shaped((cols, width), bf16)] * 4,
        compiler_params=params(),
        cost_estimate=cost(8 * each * width * cols, 4 * each * width + 2 * width * width),
        name="wgrad_out",
    )(gml, *a_list)


def wgrad_qkv_kernel(me_ref, dp_ref, g_ref, w_ref, n0, n1, n2, n3, *rest, each, pair):
    part_ref, keep_ref, send_ref, acc = rest[-4:]
    me = me_ref[0]
    for k, n in enumerate((n0, n1, n2, n3)):
        rows = pl.ds(pl.multiple_of((me ^ k) * each, each), each)
        term = dot(n[...], g_ref[rows, :], TN)
        if k:
            acc[...] += term
        else:
            acc[...] = term
    tall = keep_ref.shape[1]
    three = g_ref.shape[1]
    for z in range(4):
        for y in range(2):
            b = block_of(y, z, dp_ref[0])
            half, spot = spot_of(y, z, "y")
            o = (keep_ref, send_ref)[half]
            rows = pl.ds(pl.multiple_of(b * tall, tall), tall)
            grad = acc[rows, :]
            o[spot, :, :three] = grad.astype(bf16)
            total = None
            for i in range(3):
                cols = slice(i * LANES, (i + 1) * LANES)
                term = grad[:, cols] * w_ref[i, rows, pair * LANES : (pair + 1) * LANES].astype(f32)
                total = term if total is None else total + term
            total = jnp.sum(total, axis=1, keepdims=True)
            part_ref[:, rows] = jnp.transpose(jnp.broadcast_to(total, (tall, LANES)))[0:1]
            if len(rest) > 4:
                out = rest[0][:, rows].astype(f32) + rest[1][:, rows].astype(f32) + rest[2][:, rows].astype(f32)
                for i in range(out.shape[0] // tall):
                    o[spot, :, three + i * tall : three + (i + 1) * tall] = out[i * tall : (i + 1) * tall].astype(bf16)


def wgrad_qkv(me, dp, grad, w, n_list, pair, w_parts=()):
    length, three = grad.shape
    each, width = n_list[0].shape
    extra = w_parts[0].shape[0] if w_parts else 0
    vm = pl.BlockSpec(memory_space=pltpu.VMEM)
    return pl.pallas_call(
        functools.partial(wgrad_qkv_kernel, each=each, pair=pair),
        in_specs=[smem(), smem()] + [vm] * (6 + len(w_parts)),
        out_specs=[vm] * 3,
        out_shape=[shaped((1, width), f32)] + [shaped((4, width // 8, three + extra), bf16)] * 2,
        scratch_shapes=[pltpu.VMEM((width, three), f32)],
        compiler_params=params(),
        cost_estimate=cost(2 * length * width * three, 2 * length * (width + three) + 2 * width * (three + 4 * extra)),
        name="wgrad_qkv",
    )(me, dp, grad, w, *n_list, *w_parts)


def add_split_kernel(a_ref, b_ref, o0, o1):
    half = o0.shape[0]
    o0[...] = (a_ref[:half].astype(f32) + b_ref[:half].astype(f32)).astype(bf16)
    o1[...] = (a_ref[half:].astype(f32) + b_ref[half:].astype(f32)).astype(bf16)


def add_split(a, b):
    vm = pl.BlockSpec(memory_space=pltpu.VMEM)
    half = (a.shape[0] // 2,) + a.shape[1:]
    return pl.pallas_call(
        add_split_kernel,
        in_specs=[vm] * 2,
        out_specs=[vm] * 2,
        out_shape=[shaped(half, bf16)] * 2,
        compiler_params=params(),
        cost_estimate=cost(a.size, 6 * a.size),
        name="add_split",
    )(a, b)


class Chain:
    def __init__(self, kept, sent, lead="y"):
        self.single = lax.axis_size("dp") != 8
        self.steps = 0
        self.kept = kept
        if self.single:
            self.parts = (lax.psum(kept, "dp"), lax.psum(sent, "dp"))
            return
        self.bits = (1, 2, 4, 2, 1) if lead == "y" else (2, 1, 4, 1, 2)
        self.flying = swap(sent, self.bits[0], "dp")

    def close(self, *others):
        if self.single:
            return (self.kept,)
        self.flying = join(self.flying, *others)[0]
        return (self.flying,)

    def step(self, *others):
        if self.single:
            return (self.kept,)
        self.steps += 1
        got = join(self.flying, *others)[0]
        if self.steps == 1:
            self.kept, sent = add_split(self.kept, got)
        elif self.steps == 2:
            self.kept = sent = add_low(self.kept, got)
        elif self.steps == 3:
            self.kept = sent = add_low(self.kept, got[::-1])
        elif self.steps == 4:
            self.kept = sent = jnp.concatenate([self.kept, got], axis=0)
        else:
            self.parts = (self.kept, got)
            return (got,)
        self.flying = swap(sent, self.bits[self.steps], "dp")
        return (sent,)

    def finish(self, *others):
        while not self.single and self.steps < 5:
            self.step(*others)
        return self.parts


def pieces(refs, lead="y"):
    for y in range(2):
        for z in range(4):
            half, spot = spot_of(y, z, lead)
            yield y, z, refs[half], spot


def finish_cols_kernel(dp_ref, k_ref, s_ref, *rest, lead):
    o_ref = rest[-1]
    wide = k_ref.shape[2]
    for y, z, ref, spot in pieces((k_ref, s_ref), lead):
        cols = pl.ds(pl.multiple_of(block_of(y, z, dp_ref[0]) * wide, wide), wide)
        o_ref[0, :, cols] = ref[spot].astype(f32)


def finish_cols(dp, parts, count, index, into=None, lead="y"):
    _, hid, wide = parts[0].shape
    width = 8 * wide
    extra = () if into is None else (into,)
    return pl.pallas_call(
        functools.partial(finish_cols_kernel, lead=lead),
        grid=(1,),
        in_specs=[smem(), whole(*parts[0].shape), whole(*parts[1].shape)] + [pl.BlockSpec(memory_space=pl.ANY)] * len(extra),
        out_specs=pl.BlockSpec((1, hid, width), lambda i: (index, 0, 0)),
        out_shape=shaped((count, hid, width), f32),
        input_output_aliases={3: 0} if extra else {},
        compiler_params=params(),
        cost_estimate=cost(4 * hid * width, 8 * hid * width),
        name="finish_cols",
    )(dp, *parts, *extra)


def finish_qkv_kernel(dp_ref, ak, sk, bk, bs, o_ref, out_ref):
    tall = ak.shape[1]
    cols = out_ref.shape[0]
    three = 3 * LANES
    for (y, z, a, spot), (_, _, b, _) in zip(pieces((ak, sk)), pieces((bk, bs))):
        rows = pl.ds(pl.multiple_of(block_of(y, z, dp_ref[0]) * tall, tall), tall)
        for idx in range(3):
            part = slice(idx * LANES, (idx + 1) * LANES)
            o_ref[idx, rows, :LANES] = a[spot, :, part].astype(f32)
            o_ref[idx, rows, LANES:] = b[spot, :, part].astype(f32)
        for k in range(cols // tall):
            out_ref[k * tall : (k + 1) * tall, rows] = a[spot, :, three + k * tall : three + (k + 1) * tall].astype(f32)


def finish_qkv(dp, first, second, cols):
    vm = pl.BlockSpec(memory_space=pltpu.VMEM)
    width = 8 * first[0].shape[1]
    return pl.pallas_call(
        finish_qkv_kernel,
        in_specs=[smem()] + [vm] * 4,
        out_specs=[vm] * 2,
        out_shape=[shaped((3, width, cols), f32), shaped((cols, width), f32)],
        compiler_params=params(),
        cost_estimate=cost(8 * cols * width, 24 * cols * width),
        name="finish_qkv",
    )(dp, *first, *second)


def on_device(tokens, counts, gain_attn, gain_ffn, w_qkv, w_out, w_gate_up, w_down, cotangent):
    rows, width = tokens.shape
    columns = w_qkv.shape[2]
    hid = w_gate_up.shape[2]
    me = lax.axis_index("mp").astype(jnp.int32).reshape(1)
    dp = jnp.zeros((1,), jnp.int32)
    if lax.axis_size("dp") == 8:
        dp = lax.axis_index("dp").astype(jnp.int32).reshape(1)
    gain_a = gain_attn.reshape(1, width)
    gain_f = gain_ffn.reshape(1, width)
    qkv_w = jnp.transpose(w_qkv, (1, 0, 2))
    gate_up_w = jnp.transpose(w_gate_up, (1, 2, 0))

    n0 = norm(tokens, gain_a)
    n2 = far_of(n0)
    n1 = swap(n0, 1)
    p0, p1 = project(n0, n1, qkv_w)
    n2, p0, p1 = join(n2, p0, p1)
    n = [n0, n1, n2, swap(n2, 1)]
    out2 = far_of(after(w_out, n2))
    cot2 = far_of(after(cotangent, n2))
    qkv, attended, lse, *a = attn_fwd(me, counts, p0, p1, n[2], n[3], qkv_w)
    out2, *a = join(out2, *a)
    out_w = [w_out, swap(w_out, 1), out2, swap(out2, 1)]
    a = exchange_rel(a)
    cot2, *a = join(cot2, *a)
    cot = [cotangent, swap(cotangent, 1), cot2, swap(cot2, 1)]
    middle, m0 = middle_of(tokens, a, out_w, gain_f)
    m2 = far_of(m0)
    m1 = swap(m0, 1)
    hid_a, gg_a, gu_a, d0, d1, g0, g1 = ffn(m0, m1, cot[0], cot[1], gate_up_w, w_down)
    m2, hid_a, gg_a, gu_a, d0, d1, g0, g1 = join(m2, hid_a, gg_a, gu_a, d0, d1, g0, g1)
    m = [m0, m1, m2, swap(m2, 1)]
    g1, d1 = swap(g1, 1), swap(d1, 1)
    hid_b, gg_b, gu_b, d2, d3, g2, g3 = ffn(m[2], m[3], cot[2], cot[3], gate_up_w, w_down)
    g1, d1, g2, g3 = join(g1, d1, g2, g3)
    sent = add_low(g2, swap(g3, 1))
    s2 = far_of(sent)
    d3 = swap(after(d3, sent), 1)
    down = Chain(*wgrad_cols(dp, after(hid_a, sent), hid_b, cot))
    part_u, *parts = wgrad_cols(dp, after(gu_a, down.kept), gu_b, m, gate_up_w, 1)
    up = Chain(*parts)
    part_g, *parts = wgrad_cols(dp, after(gg_a, up.kept), gg_b, m, gate_up_w, 0, "z")
    gate = Chain(*parts, "z")
    lat_sent = add_low(d2, d3)
    x = down.step(gate.kept)
    s2 = join(s2, lat_sent, *x)[0]
    grad_middle, low, *ga = grad_middle_of(cotangent, middle, (g0, g1, s2), gain_f, out_w)
    d_list = exchange_rel(ga)
    w0, w1, w2, w3 = wgrad_out(low, a)
    x = up.step(w0) + down.step(w0) + gate.step(w0)
    d_list = join(*d_list, *x)[:4]
    w1, w3 = join(swap(w1, 1), swap(w3, 1), *d_list)[:2]
    w_sent = add_low(w2, w3)
    w2 = far_of(w_sent)
    grad0 = attn_bwd(me, counts, qkv, d_list, attended, lse, 0, (w_sent,))
    w2 = join(w2, grad0)[0]
    x = down.step(grad0) + up.step(grad0) + gate.step(grad0)
    part_0, *parts = wgrad_qkv(me, dp, after(grad0, *x), qkv_w, n, 0, (w0, w1, w2))
    first = Chain(*parts)
    lat2 = far_of(after(lat_sent, first.kept))
    grad1 = attn_bwd(me, counts, qkv, d_list, attended, lse, 1, (first.kept,))
    x = down.step(grad1) + up.step(grad1) + gate.step(grad1) + first.close(grad1) + (lat2,)
    t2, t3 = qkv_dgrad(me, grad0, after(grad1, *x), qkv_w, 2, 3)
    t3 = swap(t3, 1)
    t0, t1 = qkv_dgrad(me, grad0, after(grad1, t2), qkv_w, 0, 1)
    t3 = join(t3, t0)[0]
    sent = add_low(t2, t3)
    t2 = far_of(sent)
    t1 = swap(after(t1, sent), 1)
    x = first.step(sent)
    part_1, *parts = wgrad_qkv(me, dp, after(grad1, *x), qkv_w, n, 1)
    second = Chain(*parts)
    latents = middle + d0.astype(f32) + d1.astype(f32) + after(lat2, t1, second.kept).astype(f32)
    x = up.step(latents)
    x = first.step(*x)
    x = gate.step(*x)
    x = second.step(*x)
    grad_w_down = finish_cols(dp, down.finish(*x), 1, 0)
    gains = jnp.concatenate([(part_0 + part_1) / gain_a, (part_u + part_g) / gain_f], axis=0)
    gains = gains + swap(after(gains, grad_w_down), 1)
    x = first.step(grad_w_down)
    x = second.step(*x)
    gains = gains + swap(after(gains, *x), 2)
    t0, t1, t2 = join(t0, t1, t2, *x)[:3]
    grad_tokens = grad_tokens_of(grad_middle, tokens, (t0, t1, t2), gain_a)
    x = first.step(grad_tokens)
    x = second.step(*x)
    x = second.step(*x)
    grad_w_gate_up = finish_cols(dp, gate.finish(*x), 2, 0, None, "z")
    grad_w_gate_up = finish_cols(dp, up.finish(grad_w_gate_up), 2, 1, grad_w_gate_up)
    bit = 1
    while bit < lax.axis_size("dp"):
        gains = gains + swap(gains, bit, "dp")
        bit *= 2
    grad_w_qkv, grad_w_out = finish_qkv(dp, first.finish(grad_w_gate_up), second.finish(grad_w_gate_up), columns)
    grad_w_down = grad_w_down.reshape(hid, width)
    grad_w_qkv = jnp.transpose(grad_w_qkv, (1, 0, 2))
    grad_w_gate_up = jnp.transpose(grad_w_gate_up, (2, 0, 1))
    return (
        latents,
        grad_tokens,
        gains[0],
        gains[1],
        grad_w_qkv,
        grad_w_out,
        grad_w_gate_up,
        grad_w_down,
    )


def solution(mesh):
    placed = (
        P(("dp", "mp"), None),
        P("dp"),
        P(),
        P(),
        P(None, None, "mp"),
        P("mp", None),
        P(None, None, "mp"),
        P("mp", None),
        P(("dp", "mp"), None),
    )
    return jax.shard_map(
        on_device,
        mesh=mesh,
        in_specs=placed,
        out_specs=(
            P(("dp", "mp"), None),
            P(("dp", "mp"), None),
            P(),
            P(),
            P(None, None, "mp"),
            P("mp", None),
            P(None, None, "mp"),
            P("mp", None),
        ),
        check_vma=False,
    )
```

```python
import functools

import jax
import jax.numpy as jnp
from jax import lax
from jax.experimental import pallas as pl
from jax.experimental.pallas import tpu as pltpu
from jax.sharding import PartitionSpec as P

HD = 64
EPS = 1e-05
LANES = 128
LOG2E = 1.4426950408889634
NN = (((1,), (0,)), ((), ()))
NT = (((1,), (1,)), ((), ()))
TN = (((0,), (0,)), ((), ()))
f32 = jnp.float32
bf16 = jnp.bfloat16
VMEM_LIMIT = 60 << 20
SHARE = 1


def dot(a, b, dims=NN):
    return lax.dot_general(a, b, dims, preferred_element_type=f32)


def whole(*shape):
    return pl.BlockSpec(shape, lambda *_: (0,) * len(shape))


def smem():
    return pl.BlockSpec(memory_space=pltpu.SMEM)


def shaped(shape, dtype):
    return jax.ShapeDtypeStruct(shape, dtype)


def params():
    return pltpu.CompilerParams(vmem_limit_bytes=VMEM_LIMIT)


def cost(flops, bytes_accessed, transcendentals=0):
    return pl.CostEstimate(
        flops=int(flops * SHARE), bytes_accessed=int(bytes_accessed * SHARE), transcendentals=int(transcendentals * SHARE)
    )


def swap(value, bit, axis="mp"):
    size = lax.axis_size(axis)
    return lax.ppermute(value, axis, [(i, i ^ bit) for i in range(size)])


def after(value, *others):
    return lax.optimization_barrier((value,) + others)[0]


def join(*values):
    return lax.optimization_barrier(values)


def far_of(value):
    return swap(value, 2)


def exchange_rel(parts):
    return [parts[0]] + [swap(parts[k], k) for k in (1, 2, 3)]


def add_low(a, b):
    return (a.astype(f32) + b.astype(f32)).astype(bf16)


def head_lanes(rows, parity):
    lane = lax.broadcasted_iota(jnp.int32, (rows, LANES), 1)
    return (lane // HD) == parity, lane == (1 - parity) * HD


def norm_kernel(x_ref, gain_ref, o_ref):
    x = x_ref[...].astype(f32)
    r = lax.rsqrt(jnp.mean(x * x, axis=1, keepdims=True) + EPS)
    o_ref[...] = (x * r * gain_ref[...]).astype(bf16)


def norm(x, gain):
    rows, width = x.shape
    step = 256
    block = pl.BlockSpec((step, width), lambda i: (i, 0))
    return pl.pallas_call(
        norm_kernel,
        grid=(rows // step,),
        in_specs=[block, whole(1, width)],
        out_specs=block,
        out_shape=shaped((rows, width), bf16),
        compiler_params=params(),
        cost_estimate=cost(rows * width * 8, rows * width * 4),
        name="norm",
    )(x, gain)


def project_kernel(a_ref, b_ref, w_ref, oa_ref, ob_ref):
    cols = w_ref.shape[2]
    for x, o in ((a_ref, oa_ref), (b_ref, ob_ref)):
        for i in range(3):
            o[:, i * cols : (i + 1) * cols] = dot(x[...], w_ref[i]).astype(bf16)


def project(a, b, w):
    rows, width = a.shape
    cols = w.shape[2]
    step = 256
    block = pl.BlockSpec((step, width), lambda i: (i, 0))
    block_out = pl.BlockSpec((step, 3 * cols), lambda i: (i, 0))
    return pl.pallas_call(
        project_kernel,
        grid=(rows // step,),
        in_specs=[block, block, whole(3, width, cols)],
        out_specs=[block_out, block_out],
        out_shape=[shaped((rows, 3 * cols), bf16)] * 2,
        compiler_params=params(),
        cost_estimate=cost(12 * rows * width * cols, 4 * rows * (width + 3 * cols)),
        name="project",
    )(a, b, w)


def attn_fwd_kernel(me_ref, count_ref, p0_ref, p1_ref, n2_ref, n3_ref, w_ref, qkv_ref, o_ref, lse_ref, a0_ref, a1_ref, a2_ref, a3_ref, kaug, *, length, columns, block):
    h = pl.program_id(0)
    rows_each = length // 4
    me = me_ref[0]

    def spot(k):
        return pl.ds(pl.multiple_of((me ^ k) * rows_each, rows_each), rows_each)

    @pl.when(h == 0)
    def _():
        qkv_ref[spot(0), :] = p0_ref[...]
        qkv_ref[spot(1), :] = p1_ref[...]
        for k, n in ((2, n2_ref), (3, n3_ref)):
            for i in range(3):
                qkv_ref[spot(k), i * columns : (i + 1) * columns] = dot(n[...], w_ref[i]).astype(bf16)

    parity = lax.rem(h, 2)
    col = pl.multiple_of((h // 2) * LANES, LANES)
    c = HD**-0.5 * LOG2E
    sel, spare = head_lanes(length, parity)
    row = lax.broadcasted_iota(jnp.int32, (length, LANES), 0)
    k = qkv_ref[:, pl.ds(columns + col, LANES)].astype(f32)
    bias = jnp.where(row < count_ref[0], 0.0, -1e30)
    kaug[...] = jnp.where(sel, k, jnp.where(spare, bias, 0.0)).astype(bf16)
    sel_b, spare_b = head_lanes(block, parity)
    ri = lax.broadcasted_iota(jnp.int32, (block, block), 0)
    ci = lax.broadcasted_iota(jnp.int32, (block, block), 1)
    for i in range(length // block):
        first = i * block
        n = first + block
        rows = pl.ds(first, block)
        q = qkv_ref[rows, pl.ds(col, LANES)].astype(f32)
        q = jnp.where(sel_b, q, jnp.where(spare_b, 1.0, 0.0)).astype(bf16)
        s_d = dot(q, kaug[first:n], NT)
        s_d = jnp.where(ci <= ri, s_d, -1e30)
        m = jnp.max(s_d, axis=1, keepdims=True)
        if first:
            s_o = dot(q, kaug[:first], NT)
            m = jnp.maximum(m, jnp.max(s_o, axis=1, keepdims=True))
        mc = m * c
        p_d = jnp.exp2(s_d * c - mc)
        total = jnp.sum(p_d, axis=1, keepdims=True)
        o = dot(p_d.astype(bf16), qkv_ref[first:n, pl.ds(2 * columns + col, LANES)])
        if first:
            p_o = jnp.exp2(s_o * c - mc)
            total = total + jnp.sum(p_o, axis=1, keepdims=True)
            o = o + dot(p_o.astype(bf16), qkv_ref[:first, pl.ds(2 * columns + col, LANES)])
        o = (o / total).astype(bf16)
        out = pl.ds(col, LANES)
        o_ref[rows, out] = jnp.where(sel_b, o, o_ref[rows, out])
        lse = mc + jnp.log2(total)
        lse_ref[pl.ds(h, 1), first:n] = jnp.transpose(jnp.broadcast_to(lse, (block, LANES)))[0:1]

    @pl.when(h == pl.num_programs(0) - 1)
    def _():
        for k, ref in enumerate((a0_ref, a1_ref, a2_ref, a3_ref)):
            ref[...] = o_ref[spot(k), :]


def attn_fwd(me, count, p0, p1, n2, n3, w, block=512):
    each, width = n2.shape
    length = 4 * each
    columns = w.shape[2]
    three = 3 * columns
    heads = columns // HD
    return pl.pallas_call(
        functools.partial(attn_fwd_kernel, length=length, columns=columns, block=block),
        grid=(heads,),
        out_shape=[shaped((length, three), bf16), shaped((length, columns), bf16), shaped((heads, length), f32)]
        + [shaped((each, columns), bf16)] * 4,
        in_specs=[smem(), smem(), whole(each, three), whole(each, three), whole(each, width), whole(each, width), whole(3, width, columns)],
        out_specs=[whole(length, three), whole(length, columns), whole(heads, length)] + [whole(each, columns)] * 4,
        scratch_shapes=[pltpu.VMEM((length, LANES), bf16)],
        compiler_params=params(),
        cost_estimate=cost(10 * length * length * columns, 2 * length * columns * 8, length * length * heads // 2),
        name="attn_fwd",
    )(me, count, p0, p1, n2, n3, w)


def attn_bwd_kernel(me_ref, count_ref, q_ref, k_ref, v_ref, d0_ref, d1_ref, d2_ref, d3_ref, o_ref, lse_ref, *rest, length, block, pair):
    g_ref, do_all, kaug, qaug, dom, dq = rest[-6:]
    parity = pl.program_id(0)
    rows_each = length // 4
    me = me_ref[0]

    @pl.when(parity == 0)
    def _():
        for k, ref in enumerate((d0_ref, d1_ref, d2_ref, d3_ref)):
            do_all[pl.ds(pl.multiple_of((me ^ k) * rows_each, rows_each), rows_each), :] = ref[...]

    scale = HD**-0.5
    c = scale * LOG2E
    sel, spare = head_lanes(length, parity)
    row = lax.broadcasted_iota(jnp.int32, (length, LANES), 0)
    bias = jnp.where(row < count_ref[0], 0.0, -1e30)
    kaug[...] = jnp.where(sel, k_ref[...].astype(f32), jnp.where(spare, bias, 0.0)).astype(bf16)
    qaug[...] = jnp.where(sel, q_ref[...].astype(f32), jnp.where(spare, 1.0, 0.0)).astype(bf16)
    do = jnp.where(sel, do_all[...].astype(f32), 0.0)
    dom[...] = do.astype(bf16)
    prod = do * o_ref[...].astype(f32)
    hi = prod.astype(bf16)
    lo = (prod - hi.astype(f32)).astype(bf16)
    ones = jnp.ones((8, LANES), bf16)
    delta = (dot(ones, hi, NT) + dot(ones, lo, NT))[0:1]
    lse = lse_ref[pl.ds(2 * pair + parity, 1), :]
    sel_b, _ = head_lanes(block, parity)
    ki = lax.broadcasted_iota(jnp.int32, (block, block), 0)
    qi = lax.broadcasted_iota(jnp.int32, (block, block), 1)
    dq[...] = jnp.zeros_like(dq)
    for j in range(length // block):
        first = j * block
        last = first + block
        kj = kaug[first:last]
        vj = v_ref[first:last]

        def part(a, b, diag):
            s = dot(kj, qaug[a:b], NT)
            if diag:
                s = jnp.where(ki <= qi, s, -1e30)
            p = jnp.exp2(s * c - lse[:, a:b])
            dp = dot(vj, dom[a:b], NT)
            ds = (p * (dp - delta[:, a:b])).astype(bf16)
            dv = dot(p.astype(bf16), dom[a:b])
            dk = dot(ds, qaug[a:b])
            dq[a:b] += dot(ds, kj, TN)
            return dv, dk

        dv, dk = part(first, last, True)
        if last < length:
            dv2, dk2 = part(last, length, False)
            dv = dv + dv2
            dk = dk + dk2
        for idx, val in ((1, dk * scale), (2, dv)):
            out = slice(idx * LANES, (idx + 1) * LANES)
            g_ref[first:last, out] = jnp.where(sel_b, val.astype(bf16), g_ref[first:last, out])
    g_ref[:, :LANES] = jnp.where(sel, (dq[...] * scale).astype(bf16), g_ref[:, :LANES])


def attn_bwd(me, count, qkv, d_list, o, lse, pair, deps=(), block=512):
    length, three = qkv.shape
    columns = three // 3
    heads = columns // HD
    pairs = columns // LANES
    each = length // 4

    def part(rows, col):
        return pl.BlockSpec((rows, LANES), lambda i: (0, col))

    return pl.pallas_call(
        functools.partial(attn_bwd_kernel, length=length, block=block, pair=pair),
        grid=(2,),
        out_shape=shaped((length, 3 * LANES), bf16),
        in_specs=[smem(), smem()]
        + [part(length, i * pairs + pair) for i in range(3)]
        + [part(each, pair)] * 4
        + [part(length, pair), whole(heads, length)]
        + [pl.BlockSpec(memory_space=pl.ANY)] * len(deps),
        out_specs=whole(length, 3 * LANES),
        scratch_shapes=[pltpu.VMEM((length, LANES), bf16)] * 4 + [pltpu.VMEM((length, LANES), f32)],
        compiler_params=params(),
        cost_estimate=cost(20 * length * length * LANES, 2 * length * LANES * 8, length * length),
        name="attn_bwd",
    )(me, count, qkv, qkv, qkv, *d_list, o, lse, *deps)


def middle_kernel(x_ref, a0, a1, a2, a3, w0, w1, w2, w3, gain_ref, mid_ref, normed_ref):
    total = x_ref[...].astype(f32)
    acc = dot(a0[...], w0[...]) + dot(a1[...], w1[...]) + dot(a2[...], w2[...]) + dot(a3[...], w3[...])
    total = total + acc
    mid_ref[...] = total
    r = lax.rsqrt(jnp.mean(total * total, axis=1, keepdims=True) + EPS)
    normed_ref[...] = (total * r * gain_ref[...]).astype(bf16)


def middle_of(tokens, a_list, w_list, gain):
    rows, width = tokens.shape
    cols = a_list[0].shape[1]
    step = 256
    block = pl.BlockSpec((step, width), lambda i: (i, 0))
    block_a = pl.BlockSpec((step, cols), lambda i: (i, 0))
    return pl.pallas_call(
        middle_kernel,
        grid=(rows // step,),
        in_specs=[block] + [block_a] * 4 + [whole(cols, width)] * 4 + [whole(1, width)],
        out_specs=[block, block],
        out_shape=[shaped((rows, width), f32), shaped((rows, width), bf16)],
        compiler_params=params(),
        cost_estimate=cost(2 * rows * width * width, rows * width * 10 + 2 * width * width),
        name="middle",
    )(tokens, *a_list, *w_list, gain)


def ffn_kernel(na, nb, ca, cb, w, wd, hid_ref, gg_ref, gu_ref, pda, pdb, pga, pgb, xs, cs, *, half):
    i = pl.program_id(0)

    @pl.when(i < half)
    def _():
        xs[...] = na[...]
        cs[...] = ca[...]

    @pl.when(i >= half)
    def _():
        xs[...] = nb[...]
        cs[...] = cb[...]

    x = xs[...]
    gate = dot(x, w[0], NT)
    up = dot(x, w[1], NT)
    grad_hidden = dot(cs[...], wd[...], NT)
    sig = jax.nn.sigmoid(gate)
    silu = gate * sig
    hidden = (silu * up).astype(bf16)
    hid_ref[...] = hidden
    gg = (grad_hidden * up * (sig * (1.0 + gate * (1.0 - sig)))).astype(bf16)
    gu = (grad_hidden * silu).astype(bf16)
    gg_ref[...] = gg
    gu_ref[...] = gu
    down = dot(hidden, wd[...]).astype(bf16)
    grad_normed = (dot(gg, w[0]) + dot(gu, w[1])).astype(bf16)

    @pl.when(i < half)
    def _():
        pda[...] = down
        pga[...] = grad_normed

    @pl.when(i >= half)
    def _():
        pdb[...] = down
        pgb[...] = grad_normed


def ffn(na, nb, ca, cb, w, wd):
    rows, width = na.shape
    hid = wd.shape[0]
    step = 256
    half = rows // step
    first = pl.BlockSpec((step, width), lambda i: (jnp.minimum(i, half - 1), 0))
    second = pl.BlockSpec((step, width), lambda i: (jnp.maximum(i - half, 0), 0))
    block_h = pl.BlockSpec((step, hid), lambda i: (i, 0))
    return pl.pallas_call(
        functools.partial(ffn_kernel, half=half),
        grid=(2 * half,),
        in_specs=[first, second, first, second, whole(2, hid, width), whole(hid, width)],
        out_specs=[block_h] * 3 + [first, second] * 2,
        out_shape=[shaped((2 * rows, hid), bf16)] * 3 + [shaped((rows, width), bf16)] * 4,
        scratch_shapes=[pltpu.VMEM((step, width), bf16)] * 2,
        compiler_params=params(),
        cost_estimate=cost(24 * rows * width * hid, 12 * rows * (width + hid), 2 * rows * hid),
        name="ffn",
    )(na, nb, ca, cb, w, wd)


def grad_middle_kernel(cot, mid, g0, g1, g2, gain, w0, w1, w2, w3, gm_ref, gml_ref, o0, o1, o2, o3):
    dn = g0[...].astype(f32) + g1[...].astype(f32) + g2[...].astype(f32)
    x = mid[...]
    r = lax.rsqrt(jnp.mean(x * x, axis=1, keepdims=True) + EPS)
    e = dn * gain[...]
    gm = cot[...].astype(f32) + r * e - x * (r * r * r * jnp.mean(e * x, axis=1, keepdims=True))
    gm_ref[...] = gm
    low = gm.astype(bf16)
    gml_ref[...] = low
    for w, o in ((w0, o0), (w1, o1), (w2, o2), (w3, o3)):
        o[...] = dot(low, w[...], NT).astype(bf16)


def grad_middle_of(cot, mid, parts, gain, w_list):
    rows, width = cot.shape
    cols = w_list[0].shape[0]
    step = 256
    block = pl.BlockSpec((step, width), lambda i: (i, 0))
    block_a = pl.BlockSpec((step, cols), lambda i: (i, 0))
    return pl.pallas_call(
        grad_middle_kernel,
        grid=(rows // step,),
        in_specs=[block] * 5 + [whole(1, width)] + [whole(cols, width)] * 4,
        out_specs=[block, block] + [block_a] * 4,
        out_shape=[shaped((rows, width), f32), shaped((rows, width), bf16)] + [shaped((rows, cols), bf16)] * 4,
        compiler_params=params(),
        cost_estimate=cost(2 * rows * width * width, rows * width * 20 + 2 * width * width),
        name="grad_middle",
    )(cot, mid, *parts, gain, *w_list)


def grad_tokens_kernel(gm, tok, g0, g1, g2, gain, out_ref):
    dn = g0[...].astype(f32) + g1[...].astype(f32) + g2[...].astype(f32)
    x = tok[...].astype(f32)
    r = lax.rsqrt(jnp.mean(x * x, axis=1, keepdims=True) + EPS)
    e = dn * gain[...]
    out_ref[...] = gm[...] + r * e - x * (r * r * r * jnp.mean(e * x, axis=1, keepdims=True))


def grad_tokens_of(gm, tokens, parts, gain):
    rows, width = gm.shape
    step = 256
    block = pl.BlockSpec((step, width), lambda i: (i, 0))
    return pl.pallas_call(
        grad_tokens_kernel,
        grid=(rows // step,),
        in_specs=[block] * 5 + [whole(1, width)],
        out_specs=block,
        out_shape=shaped((rows, width), f32),
        compiler_params=params(),
        cost_estimate=cost(rows * width * 20, rows * width * 20),
        name="grad_tokens",
    )(gm, tokens, *parts, gain)


def qkv_dgrad_kernel(me_ref, g0_ref, g1_ref, w_ref, oa_ref, ob_ref, *, ka, kb):
    each = oa_ref.shape[0]
    me = me_ref[0]
    for k, o in ((ka, oa_ref), (kb, ob_ref)):
        rows = pl.ds(pl.multiple_of((me ^ k) * each, each), each)
        total = None
        for i in range(3):
            cols = slice(i * LANES, (i + 1) * LANES)
            g = jnp.concatenate([g0_ref[rows, cols], g1_ref[rows, cols]], axis=1)
            term = dot(g, w_ref[i], NT)
            total = term if total is None else total + term
        o[...] = total.astype(bf16)


def qkv_dgrad(me, g0, g1, w, ka, kb):
    length, three = g0.shape
    width = w.shape[1]
    each = length // 4
    vm = pl.BlockSpec(memory_space=pltpu.VMEM)
    return pl.pallas_call(
        functools.partial(qkv_dgrad_kernel, ka=ka, kb=kb),
        in_specs=[smem()] + [vm] * 3,
        out_specs=[vm] * 2,
        out_shape=[shaped((each, width), bf16)] * 2,
        compiler_params=params(),
        cost_estimate=cost(8 * each * width * three, 2 * (2 * length * three + 2 * width * three + 2 * each * width)),
        name="qkv_dgrad",
    )(me, g0, g1, w)


def block_of(y, z, me):
    return (2 * z + y) ^ me


def spot_of(y, z, lead):
    if lead == "y":
        return y, (z & 1) * 2 + (z >> 1)
    return z & 1, y * 2 + (z >> 1)


def wgrad_cols_kernel(dp_ref, ha, hb, c0, c1, c2, c3, *rest, each, lead):
    acc = rest[-1]
    halves = rest[-3:-1]
    acc[...] = dot(ha[:each], c0[...], TN)
    acc[...] += dot(ha[each:], c1[...], TN)
    acc[...] += dot(hb[:each], c2[...], TN)
    acc[...] += dot(hb[each:], c3[...], TN)
    wide = halves[0].shape[2]
    for z in range(4):
        for y in range(2):
            b = block_of(y, z, dp_ref[0])
            half, spot = spot_of(y, z, lead)
            halves[half][spot] = acc[:, pl.ds(pl.multiple_of(b * wide, wide), wide)].astype(bf16)


def wgrad_cols(dp, ha, hb, c_list, lead="y"):
    hid = ha.shape[1]
    each, width = c_list[0].shape
    vm = pl.BlockSpec(memory_space=pltpu.VMEM)
    return pl.pallas_call(
        functools.partial(wgrad_cols_kernel, each=each, lead=lead),
        in_specs=[smem()] + [vm] * 6,
        out_specs=[vm] * 2,
        out_shape=[shaped((4, hid, width // 8), bf16)] * 2,
        scratch_shapes=[pltpu.VMEM((hid, width), f32)],
        compiler_params=params(),
        cost_estimate=cost(8 * each * width * hid, 8 * each * (width + hid) + 2 * width * hid),
        name="wgrad_cols",
    )(dp, ha, hb, *c_list)


def wgrad_out_kernel(gml, a0, a1, a2, a3, o0, o1, o2, o3):
    for a, o in ((a0, o0), (a1, o1), (a2, o2), (a3, o3)):
        o[...] = dot(a[...], gml[...], TN).astype(bf16)


def wgrad_out(gml, a_list):
    each, width = gml.shape
    cols = a_list[0].shape[1]
    vm = pl.BlockSpec(memory_space=pltpu.VMEM)
    return pl.pallas_call(
        wgrad_out_kernel,
        in_specs=[vm] * 5,
        out_specs=[vm] * 4,
        out_shape=[shaped((cols, width), bf16)] * 4,
        compiler_params=params(),
        cost_estimate=cost(8 * each * width * cols, 4 * each * width + 2 * width * width),
        name="wgrad_out",
    )(gml, *a_list)


def wgrad_qkv_kernel(me_ref, dp_ref, g_ref, n0, n1, n2, n3, *rest, each):
    keep_ref, send_ref, acc = rest[-3:]
    me = me_ref[0]
    for k, n in enumerate((n0, n1, n2, n3)):
        rows = pl.ds(pl.multiple_of((me ^ k) * each, each), each)
        term = dot(n[...], g_ref[rows, :], TN)
        if k:
            acc[...] += term
        else:
            acc[...] = term
    tall = keep_ref.shape[1]
    three = g_ref.shape[1]
    for z in range(4):
        for y in range(2):
            b = block_of(y, z, dp_ref[0])
            half, spot = spot_of(y, z, "y")
            o = (keep_ref, send_ref)[half]
            rows = pl.ds(pl.multiple_of(b * tall, tall), tall)
            o[spot, :, :three] = acc[rows, :].astype(bf16)
            if len(rest) > 3:
                out = rest[0][:, rows].astype(f32) + rest[1][:, rows].astype(f32) + rest[2][:, rows].astype(f32)
                for i in range(out.shape[0] // tall):
                    o[spot, :, three + i * tall : three + (i + 1) * tall] = out[i * tall : (i + 1) * tall].astype(bf16)


def wgrad_qkv(me, dp, grad, n_list, w_parts=()):
    length, three = grad.shape
    each, width = n_list[0].shape
    extra = w_parts[0].shape[0] if w_parts else 0
    vm = pl.BlockSpec(memory_space=pltpu.VMEM)
    return pl.pallas_call(
        functools.partial(wgrad_qkv_kernel, each=each),
        in_specs=[smem(), smem()] + [vm] * (5 + len(w_parts)),
        out_specs=[vm] * 2,
        out_shape=[shaped((4, width // 8, three + extra), bf16)] * 2,
        scratch_shapes=[pltpu.VMEM((width, three), f32)],
        compiler_params=params(),
        cost_estimate=cost(2 * length * width * three, 2 * length * (width + three) + 2 * width * (three + 4 * extra)),
        name="wgrad_qkv",
    )(me, dp, grad, *n_list, *w_parts)


def add_split_kernel(a_ref, b_ref, o0, o1):
    half = o0.shape[0]
    o0[...] = (a_ref[:half].astype(f32) + b_ref[:half].astype(f32)).astype(bf16)
    o1[...] = (a_ref[half:].astype(f32) + b_ref[half:].astype(f32)).astype(bf16)


def add_split(a, b):
    vm = pl.BlockSpec(memory_space=pltpu.VMEM)
    half = (a.shape[0] // 2,) + a.shape[1:]
    return pl.pallas_call(
        add_split_kernel,
        in_specs=[vm] * 2,
        out_specs=[vm] * 2,
        out_shape=[shaped(half, bf16)] * 2,
        compiler_params=params(),
        cost_estimate=cost(a.size, 6 * a.size),
        name="add_split",
    )(a, b)


class Chain:
    def __init__(self, kept, sent, lead="y"):
        self.single = lax.axis_size("dp") != 8
        self.steps = 0
        self.kept = kept
        if self.single:
            self.parts = (lax.psum(kept, "dp"), lax.psum(sent, "dp"))
            return
        self.bits = (1, 2, 4, 2, 1) if lead == "y" else (2, 1, 4, 1, 2)
        self.flying = swap(sent, self.bits[0], "dp")

    def close(self, *others):
        if self.single:
            return (self.kept,)
        self.flying = join(self.flying, *others)[0]
        return (self.flying,)

    def step(self, *others):
        if self.single:
            return (self.kept,)
        self.steps += 1
        got = join(self.flying, *others)[0]
        if self.steps == 1:
            self.kept, sent = add_split(self.kept, got)
        elif self.steps == 2:
            self.kept = sent = add_low(self.kept, got)
        elif self.steps == 3:
            self.kept = sent = add_low(self.kept, got[::-1])
        elif self.steps == 4:
            self.kept = sent = jnp.concatenate([self.kept, got], axis=0)
        else:
            self.parts = (self.kept, got)
            return (got,)
        self.flying = swap(sent, self.bits[self.steps], "dp")
        return (sent,)

    def finish(self, *others):
        while not self.single and self.steps < 5:
            self.step(*others)
        return self.parts


def pieces(refs, lead="y"):
    for y in range(2):
        for z in range(4):
            half, spot = spot_of(y, z, lead)
            yield y, z, refs[half], spot


def finish_down_kernel(dp_ref, k_ref, s_ref, o_ref):
    wide = k_ref.shape[2]
    for y, z, ref, spot in pieces((k_ref, s_ref)):
        cols = pl.ds(pl.multiple_of(block_of(y, z, dp_ref[0]) * wide, wide), wide)
        o_ref[:, cols] = ref[spot].astype(f32)


def finish_down(dp, parts, shape):
    vm = pl.BlockSpec(memory_space=pltpu.VMEM)
    return pl.pallas_call(
        finish_down_kernel,
        in_specs=[smem()] + [vm] * 2,
        out_specs=vm,
        out_shape=shaped(shape, f32),
        compiler_params=params(),
        cost_estimate=cost(shape[0] * shape[1], 6 * shape[0] * shape[1]),
        name="finish_down",
    )(dp, *parts)


def finish_cols_kernel(dp_ref, k_ref, s_ref, w_ref, gain_ref, *rest, lead):
    o_ref, part_ref = rest[-2:]
    wide = k_ref.shape[2]
    for y, z, ref, spot in pieces((k_ref, s_ref), lead):
        cols = pl.ds(pl.multiple_of(block_of(y, z, dp_ref[0]) * wide, wide), wide)
        grad = ref[spot].astype(f32)
        o_ref[0, :, cols] = grad
        part_ref[:, cols] = jnp.sum(grad * w_ref[0, :, cols].astype(f32), axis=0, keepdims=True) / gain_ref[:, cols]


def finish_cols(dp, parts, w, gain, index, into=None, lead="y"):
    two, hid, width = w.shape
    one = pl.BlockSpec((1, hid, width), lambda i: (index, 0, 0))
    extra = () if into is None else (into,)
    return pl.pallas_call(
        functools.partial(finish_cols_kernel, lead=lead),
        grid=(1,),
        in_specs=[smem(), whole(*parts[0].shape), whole(*parts[1].shape), one, whole(1, width)] + [pl.BlockSpec(memory_space=pl.ANY)] * len(extra),
        out_specs=[one, whole(1, width)],
        out_shape=[shaped(w.shape, f32), shaped((1, width), f32)],
        input_output_aliases={5: 0} if extra else {},
        compiler_params=params(),
        cost_estimate=cost(4 * hid * width, 8 * hid * width),
        name="finish_cols",
    )(dp, *parts, w, gain, *extra)


def half_gain_kernel(dp_ref, a_ref, b_ref, w_ref, gain_ref, o_ref, *, y):
    tall = a_ref.shape[1]
    o_ref[...] = jnp.zeros_like(o_ref)
    for z in range(4):
        _, spot = spot_of(y, z, "y")
        rows = pl.ds(pl.multiple_of(block_of(y, z, dp_ref[0]) * tall, tall), tall)
        total = None
        for idx in range(3):
            part = slice(idx * LANES, (idx + 1) * LANES)
            for pair, ref in enumerate((a_ref, b_ref)):
                term = ref[spot, :, part].astype(f32) * w_ref[idx, rows, pair * LANES : (pair + 1) * LANES].astype(f32)
                total = term if total is None else total + term
        total = jnp.sum(total, axis=1, keepdims=True)
        o_ref[:, rows] = jnp.transpose(jnp.broadcast_to(total, (tall, LANES)))[0:1] / gain_ref[:, rows]


def half_gain(dp, first, second, w, gain, y):
    vm = pl.BlockSpec(memory_space=pltpu.VMEM)
    width = w.shape[1]
    return pl.pallas_call(
        functools.partial(half_gain_kernel, y=y),
        in_specs=[smem()] + [vm] * 4,
        out_specs=vm,
        out_shape=shaped((1, width), f32),
        compiler_params=params(),
        cost_estimate=cost(2 * w.size, 4 * w.size),
        name="half_gain",
    )(dp, first, second, w, gain)


def finish_qkv_kernel(dp_ref, ak, sk, bk, bs, o_ref, out_ref):
    tall = ak.shape[1]
    cols = out_ref.shape[0]
    three = 3 * LANES
    for (y, z, a, spot), (_, _, b, _) in zip(pieces((ak, sk)), pieces((bk, bs))):
        rows = pl.ds(pl.multiple_of(block_of(y, z, dp_ref[0]) * tall, tall), tall)
        for idx in range(3):
            part = slice(idx * LANES, (idx + 1) * LANES)
            o_ref[idx, rows, :LANES] = a[spot, :, part].astype(f32)
            o_ref[idx, rows, LANES:] = b[spot, :, part].astype(f32)
        for k in range(cols // tall):
            out_ref[k * tall : (k + 1) * tall, rows] = a[spot, :, three + k * tall : three + (k + 1) * tall].astype(f32)


def finish_qkv(dp, first, second, cols):
    vm = pl.BlockSpec(memory_space=pltpu.VMEM)
    width = 8 * first[0].shape[1]
    return pl.pallas_call(
        finish_qkv_kernel,
        in_specs=[smem()] + [vm] * 4,
        out_specs=[vm] * 2,
        out_shape=[shaped((3, width, cols), f32), shaped((cols, width), f32)],
        compiler_params=params(),
        cost_estimate=cost(8 * cols * width, 24 * cols * width),
        name="finish_qkv",
    )(dp, *first, *second)


def on_device(tokens, counts, gain_attn, gain_ffn, w_qkv, w_out, w_gate_up, w_down, cotangent):
    rows, width = tokens.shape
    columns = w_qkv.shape[2]
    hid = w_gate_up.shape[2]
    me = lax.axis_index("mp").astype(jnp.int32).reshape(1)
    dp = jnp.zeros((1,), jnp.int32)
    if lax.axis_size("dp") == 8:
        dp = lax.axis_index("dp").astype(jnp.int32).reshape(1)
    gain_a = gain_attn.reshape(1, width)
    gain_f = gain_ffn.reshape(1, width)
    qkv_w = jnp.transpose(w_qkv, (1, 0, 2))
    gate_up_w = jnp.transpose(w_gate_up, (1, 2, 0))

    n0 = norm(tokens, gain_a)
    n2 = far_of(n0)
    n1 = swap(n0, 1)
    p0, p1 = project(n0, n1, qkv_w)
    n2, p0, p1 = join(n2, p0, p1)
    n = [n0, n1, n2, swap(n2, 1)]
    out2 = far_of(after(w_out, n2))
    cot2 = far_of(after(cotangent, *n[2:]))
    qkv, attended, lse, *a = attn_fwd(me, counts, p0, p1, n[2], n[3], qkv_w)
    out2, *a = join(out2, *a)
    out_w = [w_out, swap(w_out, 1), out2, swap(out2, 1)]
    a = exchange_rel(a)
    cot2, *a = join(cot2, *a)
    cot = [cotangent, swap(cotangent, 1), cot2, swap(cot2, 1)]
    middle, m0 = middle_of(tokens, a, out_w, gain_f)
    m2 = far_of(m0)
    m1 = swap(m0, 1)
    hid_a, gg_a, gu_a, d0, d1, g0, g1 = ffn(m0, m1, cot[0], cot[1], gate_up_w, w_down)
    m2, hid_a, gg_a, gu_a, d0, d1, g0, g1 = join(m2, hid_a, gg_a, gu_a, d0, d1, g0, g1)
    m = [m0, m1, m2, swap(m2, 1)]
    g1, d1 = swap(g1, 1), swap(d1, 1)
    hid_b, gg_b, gu_b, d2, d3, g2, g3 = ffn(m[2], m[3], cot[2], cot[3], gate_up_w, w_down)
    g1, d1, g2, g3 = join(g1, d1, g2, g3)
    sent = add_low(g2, swap(g3, 1))
    s2 = far_of(sent)
    d3 = swap(after(d3, sent), 1)
    down = Chain(*wgrad_cols(dp, after(hid_a, sent), hid_b, cot))
    parts = wgrad_cols(dp, after(gu_a, down.kept), gu_b, m)
    up = Chain(*parts)
    parts = wgrad_cols(dp, after(gg_a, up.kept), gg_b, m, "z")
    gate_kept, gate_sent = parts
    lat_sent = add_low(d2, d3)
    x = down.step(gate_kept)
    s2 = join(s2, lat_sent, *x)[0]
    grad_middle, low, *ga = grad_middle_of(cotangent, middle, (g0, g1, s2), gain_f, out_w)
    d_list = exchange_rel(ga)
    gate = Chain(gate_kept, after(gate_sent, low), "z")
    w0, w1, w2, w3 = wgrad_out(low, a)
    x = up.step(w0) + down.step(w0)
    d_list = join(*d_list, *x)[:4]
    w1, w3 = join(swap(w1, 1), swap(w3, 1), *d_list)[:2]
    w_sent = add_low(w2, w3)
    w2 = far_of(w_sent)
    grad0 = attn_bwd(me, counts, qkv, d_list, attended, lse, 0, (w_sent,))
    w2 = join(w2, grad0)[0]
    x = down.step(grad0) + up.step(grad0) + gate.step(grad0)
    parts = wgrad_qkv(me, dp, after(grad0, *x), n, (w0, w1, w2))
    first = Chain(*parts)
    lat2 = far_of(after(lat_sent, first.kept))
    grad1 = attn_bwd(me, counts, qkv, d_list, attended, lse, 1, (first.kept,))
    x = down.step(grad1) + up.step(grad1) + gate.step(grad1) + first.close(grad1) + (lat2,)
    t2, t3 = qkv_dgrad(me, grad0, after(grad1, *x), qkv_w, 2, 3)
    t3 = swap(t3, 1)
    t0, t1 = qkv_dgrad(me, grad0, after(grad1, t2), qkv_w, 0, 1)
    t3 = join(t3, t0)[0]
    sent = add_low(t2, t3)
    t2 = far_of(sent)
    x = first.step(sent)
    parts = wgrad_qkv(me, dp, after(grad1, *x), n)
    second = Chain(*parts)
    latents = middle + d0.astype(f32) + d1.astype(f32) + after(lat2, second.kept).astype(f32)
    t1 = swap(after(t1, latents), 1)
    x = up.step(latents)
    x = first.step(*x)
    x = gate.step(*x)
    x = second.step(*x)
    grad_w_down = finish_down(dp, down.finish(*x), (hid, width))
    x = first.step(grad_w_down)
    x = second.step(*x)
    t0, t1, t2 = join(t0, t1, t2, *x)[:3]
    grad_tokens = grad_tokens_of(grad_middle, tokens, (t0, t1, t2), gain_a)
    x = first.step(grad_tokens)
    x = second.step(*x)
    grad_w_gate_up, part_u = finish_cols(dp, up.finish(*x), gate_up_w, gain_f, 1)
    x = second.step(grad_w_gate_up)
    if lax.axis_size("dp") == 8:
        gain_1 = half_gain(dp, first.kept, after(second.kept, *x), qkv_w, gain_a, 0)
        gain_1 = gain_1 + swap(gain_1, 1) + swap(gain_1, 2) + swap(gain_1, 3)
        gain_1 = gain_1 + swap(gain_1, 1, "dp")
    else:
        parts = [half_gain(dp, first.parts[y], second.parts[y], qkv_w, gain_a, y) for y in range(2)]
        gain_1 = parts[0] + parts[1]
        gain_1 = gain_1 + swap(gain_1, 1) + swap(gain_1, 2) + swap(gain_1, 3)
    grad_w_gate_up, part_g = finish_cols(dp, gate.finish(*x), gate_up_w, gain_f, 0, grad_w_gate_up, "z")
    gain_2 = part_u + part_g
    gain_2 = gain_2 + swap(gain_2, 1) + swap(gain_2, 2) + swap(gain_2, 3)
    grad_w_qkv, grad_w_out = finish_qkv(dp, first.finish(grad_w_gate_up), second.finish(grad_w_gate_up), columns)
    gains = (gain_1, gain_2)
    grad_w_qkv = jnp.transpose(grad_w_qkv, (1, 0, 2))
    grad_w_gate_up = jnp.transpose(grad_w_gate_up, (2, 0, 1))
    return (
        latents,
        grad_tokens,
        gains[0].reshape(width),
        gains[1].reshape(width),
        grad_w_qkv,
        grad_w_out,
        grad_w_gate_up,
        grad_w_down,
    )


def solution(mesh):
    placed = (
        P(("dp", "mp"), None),
        P("dp"),
        P(),
        P(),
        P(None, None, "mp"),
        P("mp", None),
        P(None, None, "mp"),
        P("mp", None),
        P(("dp", "mp"), None),
    )
    return jax.shard_map(
        on_device,
        mesh=mesh,
        in_specs=placed,
        out_specs=(
            P(("dp", "mp"), None),
            P(("dp", "mp"), None),
            P(),
            P(),
            P(None, None, "mp"),
            P("mp", None),
            P(None, None, "mp"),
            P("mp", None),
        ),
        check_vma=False,
    )
```

```python
import functools

import jax
import jax.numpy as jnp
from jax import lax
from jax.experimental import pallas as pl
from jax.experimental.pallas import tpu as pltpu
from jax.sharding import PartitionSpec as P

HD = 64
EPS = 1e-05
LANES = 128
LOG2E = 1.4426950408889634
NN = (((1,), (0,)), ((), ()))
NT = (((1,), (1,)), ((), ()))
TN = (((0,), (0,)), ((), ()))
f32 = jnp.float32
bf16 = jnp.bfloat16
VMEM_LIMIT = 28 << 20
SHARE = 1


def dot(a, b, dims=NN):
    return lax.dot_general(a, b, dims, preferred_element_type=f32)


def whole(*shape):
    return pl.BlockSpec(shape, lambda *_: (0,) * len(shape))


def smem():
    return pl.BlockSpec(memory_space=pltpu.SMEM)


def shaped(shape, dtype):
    return jax.ShapeDtypeStruct(shape, dtype)


def params():
    return pltpu.CompilerParams(vmem_limit_bytes=VMEM_LIMIT)


def cost(flops, bytes_accessed, transcendentals=0):
    return pl.CostEstimate(
        flops=int(flops * SHARE), bytes_accessed=int(bytes_accessed * SHARE), transcendentals=int(transcendentals * SHARE)
    )


def swap(value, bit, axis="mp"):
    size = lax.axis_size(axis)
    return lax.ppermute(value, axis, [(i, i ^ bit) for i in range(size)])


def after(value, *others):
    return lax.optimization_barrier((value,) + others)[0]


def join(*values):
    return lax.optimization_barrier(values)


def far_of(value):
    return swap(value, 2)


def exchange_rel(parts):
    return [parts[0]] + [swap(parts[k], k) for k in (1, 2, 3)]


def add_low(a, b):
    return (a.astype(f32) + b.astype(f32)).astype(bf16)


def head_lanes(rows, parity):
    lane = lax.broadcasted_iota(jnp.int32, (rows, LANES), 1)
    return (lane // HD) == parity, lane == (1 - parity) * HD


def norm_kernel(x_ref, gain_ref, o_ref):
    x = x_ref[...].astype(f32)
    r = lax.rsqrt(jnp.mean(x * x, axis=1, keepdims=True) + EPS)
    o_ref[...] = (x * r * gain_ref[...]).astype(bf16)


def norm(x, gain):
    rows, width = x.shape
    step = 256
    block = pl.BlockSpec((step, width), lambda i: (i, 0))
    return pl.pallas_call(
        norm_kernel,
        grid=(rows // step,),
        in_specs=[block, whole(1, width)],
        out_specs=block,
        out_shape=shaped((rows, width), bf16),
        compiler_params=params(),
        cost_estimate=cost(rows * width * 8, rows * width * 4),
        name="norm",
    )(x, gain)


def project_kernel(a_ref, b_ref, w_ref, oa_ref, ob_ref):
    cols = w_ref.shape[2]
    for x, o in ((a_ref, oa_ref), (b_ref, ob_ref)):
        for i in range(3):
            o[:, i * cols : (i + 1) * cols] = dot(x[...], w_ref[i]).astype(bf16)


def project(a, b, w):
    rows, width = a.shape
    cols = w.shape[2]
    step = 256
    block = pl.BlockSpec((step, width), lambda i: (i, 0))
    block_out = pl.BlockSpec((step, 3 * cols), lambda i: (i, 0))
    return pl.pallas_call(
        project_kernel,
        grid=(rows // step,),
        in_specs=[block, block, whole(3, width, cols)],
        out_specs=[block_out, block_out],
        out_shape=[shaped((rows, 3 * cols), bf16)] * 2,
        compiler_params=params(),
        cost_estimate=cost(12 * rows * width * cols, 4 * rows * (width + 3 * cols)),
        name="project",
    )(a, b, w)


def attn_fwd_kernel(me_ref, count_ref, p0_ref, p1_ref, n2_ref, n3_ref, w_ref, qkv_ref, o_ref, lse_ref, a0_ref, a1_ref, a2_ref, a3_ref, kaug, *, length, columns, block):
    h = pl.program_id(0)
    rows_each = length // 4
    me = me_ref[0]

    def spot(k):
        return pl.ds(pl.multiple_of((me ^ k) * rows_each, rows_each), rows_each)

    @pl.when(h == 0)
    def _():
        qkv_ref[spot(0), :] = p0_ref[...]
        qkv_ref[spot(1), :] = p1_ref[...]
        for k, n in ((2, n2_ref), (3, n3_ref)):
            for i in range(3):
                qkv_ref[spot(k), i * columns : (i + 1) * columns] = dot(n[...], w_ref[i]).astype(bf16)

    parity = lax.rem(h, 2)
    col = pl.multiple_of((h // 2) * LANES, LANES)
    c = HD**-0.5 * LOG2E
    sel, spare = head_lanes(length, parity)
    row = lax.broadcasted_iota(jnp.int32, (length, LANES), 0)
    k = qkv_ref[:, pl.ds(columns + col, LANES)].astype(f32)
    bias = jnp.where(row < count_ref[0], 0.0, -1e30)
    kaug[...] = jnp.where(sel, k, jnp.where(spare, bias, 0.0)).astype(bf16)
    sel_b, spare_b = head_lanes(block, parity)
    ri = lax.broadcasted_iota(jnp.int32, (block, block), 0)
    ci = lax.broadcasted_iota(jnp.int32, (block, block), 1)
    for i in range(length // block):
        first = i * block
        n = first + block
        rows = pl.ds(first, block)
        q = qkv_ref[rows, pl.ds(col, LANES)].astype(f32)
        q = jnp.where(sel_b, q, jnp.where(spare_b, 1.0, 0.0)).astype(bf16)
        s_d = dot(q, kaug[first:n], NT)
        s_d = jnp.where(ci <= ri, s_d, -1e30)
        m = jnp.max(s_d, axis=1, keepdims=True)
        if first:
            s_o = dot(q, kaug[:first], NT)
            m = jnp.maximum(m, jnp.max(s_o, axis=1, keepdims=True))
        mc = m * c
        p_d = jnp.exp2(s_d * c - mc)
        total = jnp.sum(p_d, axis=1, keepdims=True)
        o = dot(p_d.astype(bf16), qkv_ref[first:n, pl.ds(2 * columns + col, LANES)])
        if first:
            p_o = jnp.exp2(s_o * c - mc)
            total = total + jnp.sum(p_o, axis=1, keepdims=True)
            o = o + dot(p_o.astype(bf16), qkv_ref[:first, pl.ds(2 * columns + col, LANES)])
        o = (o / total).astype(bf16)
        out = pl.ds(col, LANES)
        o_ref[rows, out] = jnp.where(sel_b, o, o_ref[rows, out])
        lse = mc + jnp.log2(total)
        lse_ref[pl.ds(h, 1), first:n] = jnp.transpose(jnp.broadcast_to(lse, (block, LANES)))[0:1]

    @pl.when(h == pl.num_programs(0) - 1)
    def _():
        for k, ref in enumerate((a0_ref, a1_ref, a2_ref, a3_ref)):
            ref[...] = o_ref[spot(k), :]


def attn_fwd(me, count, p0, p1, n2, n3, w, block=512):
    each, width = n2.shape
    length = 4 * each
    columns = w.shape[2]
    three = 3 * columns
    heads = columns // HD
    return pl.pallas_call(
        functools.partial(attn_fwd_kernel, length=length, columns=columns, block=block),
        grid=(heads,),
        out_shape=[shaped((length, three), bf16), shaped((length, columns), bf16), shaped((heads, length), f32)]
        + [shaped((each, columns), bf16)] * 4,
        in_specs=[smem(), smem(), whole(each, three), whole(each, three), whole(each, width), whole(each, width), whole(3, width, columns)],
        out_specs=[whole(length, three), whole(length, columns), whole(heads, length)] + [whole(each, columns)] * 4,
        scratch_shapes=[pltpu.VMEM((length, LANES), bf16)],
        compiler_params=params(),
        cost_estimate=cost(10 * length * length * columns, 2 * length * columns * 8, length * length * heads // 2),
        name="attn_fwd",
    )(me, count, p0, p1, n2, n3, w)


def attn_bwd_kernel(me_ref, count_ref, q_ref, k_ref, v_ref, d0_ref, d1_ref, d2_ref, d3_ref, o_ref, lse_ref, *rest, length, block, pair):
    g_ref, do_all, kaug, qaug, dom, dq = rest[-6:]
    parity = pl.program_id(0)
    rows_each = length // 4
    me = me_ref[0]

    @pl.when(parity == 0)
    def _():
        for k, ref in enumerate((d0_ref, d1_ref, d2_ref, d3_ref)):
            do_all[pl.ds(pl.multiple_of((me ^ k) * rows_each, rows_each), rows_each), :] = ref[...]

    scale = HD**-0.5
    c = scale * LOG2E
    sel, spare = head_lanes(length, parity)
    row = lax.broadcasted_iota(jnp.int32, (length, LANES), 0)
    bias = jnp.where(row < count_ref[0], 0.0, -1e30)
    kaug[...] = jnp.where(sel, k_ref[...].astype(f32), jnp.where(spare, bias, 0.0)).astype(bf16)
    qaug[...] = jnp.where(sel, q_ref[...].astype(f32), jnp.where(spare, 1.0, 0.0)).astype(bf16)
    do = jnp.where(sel, do_all[...].astype(f32), 0.0)
    dom[...] = do.astype(bf16)
    prod = do * o_ref[...].astype(f32)
    hi = prod.astype(bf16)
    lo = (prod - hi.astype(f32)).astype(bf16)
    ones = jnp.ones((8, LANES), bf16)
    delta = (dot(ones, hi, NT) + dot(ones, lo, NT))[0:1]
    lse = lse_ref[pl.ds(2 * pair + parity, 1), :]
    sel_b, _ = head_lanes(block, parity)
    ki = lax.broadcasted_iota(jnp.int32, (block, block), 0)
    qi = lax.broadcasted_iota(jnp.int32, (block, block), 1)
    dq[...] = jnp.zeros_like(dq)
    for j in range(length // block):
        first = j * block
        last = first + block
        kj = kaug[first:last]
        vj = v_ref[first:last]

        def part(a, b, diag):
            s = dot(kj, qaug[a:b], NT)
            if diag:
                s = jnp.where(ki <= qi, s, -1e30)
            p = jnp.exp2(s * c - lse[:, a:b])
            dp = dot(vj, dom[a:b], NT)
            ds = (p * (dp - delta[:, a:b])).astype(bf16)
            dv = dot(p.astype(bf16), dom[a:b])
            dk = dot(ds, qaug[a:b])
            dq[a:b] += dot(ds, kj, TN)
            return dv, dk

        dv, dk = part(first, last, True)
        if last < length:
            dv2, dk2 = part(last, length, False)
            dv = dv + dv2
            dk = dk + dk2
        for idx, val in ((1, dk * scale), (2, dv)):
            out = slice(idx * LANES, (idx + 1) * LANES)
            g_ref[first:last, out] = jnp.where(sel_b, val.astype(bf16), g_ref[first:last, out])
    g_ref[:, :LANES] = jnp.where(sel, (dq[...] * scale).astype(bf16), g_ref[:, :LANES])


def attn_bwd(me, count, qkv, d_list, o, lse, pair, deps=(), block=512):
    length, three = qkv.shape
    columns = three // 3
    heads = columns // HD
    pairs = columns // LANES
    each = length // 4

    def part(rows, col):
        return pl.BlockSpec((rows, LANES), lambda i: (0, col))

    return pl.pallas_call(
        functools.partial(attn_bwd_kernel, length=length, block=block, pair=pair),
        grid=(2,),
        out_shape=shaped((length, 3 * LANES), bf16),
        in_specs=[smem(), smem()]
        + [part(length, i * pairs + pair) for i in range(3)]
        + [part(each, pair)] * 4
        + [part(length, pair), whole(heads, length)]
        + [pl.BlockSpec(memory_space=pl.ANY)] * len(deps),
        out_specs=whole(length, 3 * LANES),
        scratch_shapes=[pltpu.VMEM((length, LANES), bf16)] * 4 + [pltpu.VMEM((length, LANES), f32)],
        compiler_params=params(),
        cost_estimate=cost(20 * length * length * LANES, 2 * length * LANES * 8, length * length),
        name="attn_bwd",
    )(me, count, qkv, qkv, qkv, *d_list, o, lse, *deps)


def middle_kernel(x_ref, a0, a1, a2, a3, w0, w1, w2, w3, gain_ref, mid_ref, normed_ref):
    total = x_ref[...].astype(f32)
    acc = dot(a0[...], w0[...]) + dot(a1[...], w1[...]) + dot(a2[...], w2[...]) + dot(a3[...], w3[...])
    total = total + acc
    mid_ref[...] = total
    r = lax.rsqrt(jnp.mean(total * total, axis=1, keepdims=True) + EPS)
    normed_ref[...] = (total * r * gain_ref[...]).astype(bf16)


def middle_of(tokens, a_list, w_list, gain):
    rows, width = tokens.shape
    cols = a_list[0].shape[1]
    step = 256
    block = pl.BlockSpec((step, width), lambda i: (i, 0))
    block_a = pl.BlockSpec((step, cols), lambda i: (i, 0))
    return pl.pallas_call(
        middle_kernel,
        grid=(rows // step,),
        in_specs=[block] + [block_a] * 4 + [whole(cols, width)] * 4 + [whole(1, width)],
        out_specs=[block, block],
        out_shape=[shaped((rows, width), f32), shaped((rows, width), bf16)],
        compiler_params=params(),
        cost_estimate=cost(2 * rows * width * width, rows * width * 10 + 2 * width * width),
        name="middle",
    )(tokens, *a_list, *w_list, gain)


def ffn_kernel(na, nb, ca, cb, w, wd, hid_ref, gg_ref, gu_ref, pda, pdb, pga, pgb, xs, cs, *, half):
    i = pl.program_id(0)

    @pl.when(i < half)
    def _():
        xs[...] = na[...]
        cs[...] = ca[...]

    @pl.when(i >= half)
    def _():
        xs[...] = nb[...]
        cs[...] = cb[...]

    x = xs[...]
    gate = dot(x, w[0], NT)
    up = dot(x, w[1], NT)
    grad_hidden = dot(cs[...], wd[...], NT)
    sig = jax.nn.sigmoid(gate)
    silu = gate * sig
    hidden = (silu * up).astype(bf16)
    hid_ref[...] = hidden
    gg = (grad_hidden * up * (sig * (1.0 + gate * (1.0 - sig)))).astype(bf16)
    gu = (grad_hidden * silu).astype(bf16)
    gg_ref[...] = gg
    gu_ref[...] = gu
    down = dot(hidden, wd[...]).astype(bf16)
    grad_normed = (dot(gg, w[0]) + dot(gu, w[1])).astype(bf16)

    @pl.when(i < half)
    def _():
        pda[...] = down
        pga[...] = grad_normed

    @pl.when(i >= half)
    def _():
        pdb[...] = down
        pgb[...] = grad_normed


def ffn(na, nb, ca, cb, w, wd):
    rows, width = na.shape
    hid = wd.shape[0]
    step = 256
    half = rows // step
    first = pl.BlockSpec((step, width), lambda i: (jnp.minimum(i, half - 1), 0))
    second = pl.BlockSpec((step, width), lambda i: (jnp.maximum(i - half, 0), 0))
    block_h = pl.BlockSpec((step, hid), lambda i: (i, 0))
    return pl.pallas_call(
        functools.partial(ffn_kernel, half=half),
        grid=(2 * half,),
        in_specs=[first, second, first, second, whole(2, hid, width), whole(hid, width)],
        out_specs=[block_h] * 3 + [first, second] * 2,
        out_shape=[shaped((2 * rows, hid), bf16)] * 3 + [shaped((rows, width), bf16)] * 4,
        scratch_shapes=[pltpu.VMEM((step, width), bf16)] * 2,
        compiler_params=params(),
        cost_estimate=cost(24 * rows * width * hid, 12 * rows * (width + hid), 2 * rows * hid),
        name="ffn",
    )(na, nb, ca, cb, w, wd)


def grad_middle_kernel(cot, mid, g0, g1, g2, gain, w0, w1, w2, w3, gm_ref, gml_ref, o0, o1, o2, o3):
    dn = g0[...].astype(f32) + g1[...].astype(f32) + g2[...].astype(f32)
    x = mid[...]
    r = lax.rsqrt(jnp.mean(x * x, axis=1, keepdims=True) + EPS)
    e = dn * gain[...]
    gm = cot[...].astype(f32) + r * e - x * (r * r * r * jnp.mean(e * x, axis=1, keepdims=True))
    gm_ref[...] = gm
    low = gm.astype(bf16)
    gml_ref[...] = low
    for w, o in ((w0, o0), (w1, o1), (w2, o2), (w3, o3)):
        o[...] = dot(low, w[...], NT).astype(bf16)


def grad_middle_of(cot, mid, parts, gain, w_list):
    rows, width = cot.shape
    cols = w_list[0].shape[0]
    step = 256
    block = pl.BlockSpec((step, width), lambda i: (i, 0))
    block_a = pl.BlockSpec((step, cols), lambda i: (i, 0))
    return pl.pallas_call(
        grad_middle_kernel,
        grid=(rows // step,),
        in_specs=[block] * 5 + [whole(1, width)] + [whole(cols, width)] * 4,
        out_specs=[block, block] + [block_a] * 4,
        out_shape=[shaped((rows, width), f32), shaped((rows, width), bf16)] + [shaped((rows, cols), bf16)] * 4,
        compiler_params=params(),
        cost_estimate=cost(2 * rows * width * width, rows * width * 20 + 2 * width * width),
        name="grad_middle",
    )(cot, mid, *parts, gain, *w_list)


def grad_tokens_kernel(gm, tok, g0, g1, g2, gain, out_ref):
    dn = g0[...].astype(f32) + g1[...].astype(f32) + g2[...].astype(f32)
    x = tok[...].astype(f32)
    r = lax.rsqrt(jnp.mean(x * x, axis=1, keepdims=True) + EPS)
    e = dn * gain[...]
    out_ref[...] = gm[...] + r * e - x * (r * r * r * jnp.mean(e * x, axis=1, keepdims=True))


def grad_tokens_of(gm, tokens, parts, gain):
    rows, width = gm.shape
    step = 256
    block = pl.BlockSpec((step, width), lambda i: (i, 0))
    return pl.pallas_call(
        grad_tokens_kernel,
        grid=(rows // step,),
        in_specs=[block] * 5 + [whole(1, width)],
        out_specs=block,
        out_shape=shaped((rows, width), f32),
        compiler_params=params(),
        cost_estimate=cost(rows * width * 20, rows * width * 20),
        name="grad_tokens",
    )(gm, tokens, *parts, gain)


def qkv_dgrad_kernel(me_ref, g0_ref, g1_ref, w_ref, oa_ref, ob_ref, *, ka, kb):
    each = oa_ref.shape[0]
    me = me_ref[0]
    for k, o in ((ka, oa_ref), (kb, ob_ref)):
        rows = pl.ds(pl.multiple_of((me ^ k) * each, each), each)
        total = None
        for i in range(3):
            cols = slice(i * LANES, (i + 1) * LANES)
            g = jnp.concatenate([g0_ref[rows, cols], g1_ref[rows, cols]], axis=1)
            term = dot(g, w_ref[i], NT)
            total = term if total is None else total + term
        o[...] = total.astype(bf16)


def qkv_dgrad(me, g0, g1, w, ka, kb):
    length, three = g0.shape
    width = w.shape[1]
    each = length // 4
    vm = pl.BlockSpec(memory_space=pltpu.VMEM)
    return pl.pallas_call(
        functools.partial(qkv_dgrad_kernel, ka=ka, kb=kb),
        in_specs=[smem()] + [vm] * 3,
        out_specs=[vm] * 2,
        out_shape=[shaped((each, width), bf16)] * 2,
        compiler_params=params(),
        cost_estimate=cost(8 * each * width * three, 2 * (2 * length * three + 2 * width * three + 2 * each * width)),
        name="qkv_dgrad",
    )(me, g0, g1, w)


def block_of(y, z, me):
    return (2 * z + y) ^ me


def spot_of(y, z, lead):
    if lead == "y":
        return y, (z & 1) * 2 + (z >> 1)
    return z & 1, y * 2 + (z >> 1)


def wgrad_cols_kernel(dp_ref, ha, hb, c0, c1, c2, c3, *rest, each, lead):
    acc = rest[-1]
    halves = rest[-3:-1]
    acc[...] = dot(ha[:each], c0[...], TN)
    acc[...] += dot(ha[each:], c1[...], TN)
    acc[...] += dot(hb[:each], c2[...], TN)
    acc[...] += dot(hb[each:], c3[...], TN)
    wide = halves[0].shape[2]
    for z in range(4):
        for y in range(2):
            b = block_of(y, z, dp_ref[0])
            half, spot = spot_of(y, z, lead)
            halves[half][spot] = acc[:, pl.ds(pl.multiple_of(b * wide, wide), wide)].astype(bf16)


def wgrad_cols(dp, ha, hb, c_list, lead="y"):
    hid = ha.shape[1]
    each, width = c_list[0].shape
    vm = pl.BlockSpec(memory_space=pltpu.VMEM)
    return pl.pallas_call(
        functools.partial(wgrad_cols_kernel, each=each, lead=lead),
        in_specs=[smem()] + [vm] * 6,
        out_specs=[vm] * 2,
        out_shape=[shaped((4, hid, width // 8), bf16)] * 2,
        scratch_shapes=[pltpu.VMEM((hid, width), f32)],
        compiler_params=params(),
        cost_estimate=cost(8 * each * width * hid, 8 * each * (width + hid) + 2 * width * hid),
        name="wgrad_cols",
    )(dp, ha, hb, *c_list)


def wgrad_out_kernel(gml, a0, a1, a2, a3, o0, o1, o2, o3):
    for a, o in ((a0, o0), (a1, o1), (a2, o2), (a3, o3)):
        o[...] = dot(a[...], gml[...], TN).astype(bf16)


def wgrad_out(gml, a_list):
    each, width = gml.shape
    cols = a_list[0].shape[1]
    vm = pl.BlockSpec(memory_space=pltpu.VMEM)
    return pl.pallas_call(
        wgrad_out_kernel,
        in_specs=[vm] * 5,
        out_specs=[vm] * 4,
        out_shape=[shaped((cols, width), bf16)] * 4,
        compiler_params=params(),
        cost_estimate=cost(8 * each * width * cols, 4 * each * width + 2 * width * width),
        name="wgrad_out",
    )(gml, *a_list)


def wgrad_qkv_kernel(me_ref, dp_ref, g_ref, n0, n1, n2, n3, *rest, each):
    keep_ref, send_ref, acc = rest[-3:]
    me = me_ref[0]
    for k, n in enumerate((n0, n1, n2, n3)):
        rows = pl.ds(pl.multiple_of((me ^ k) * each, each), each)
        term = dot(n[...], g_ref[rows, :], TN)
        if k:
            acc[...] += term
        else:
            acc[...] = term
    tall = keep_ref.shape[1]
    three = g_ref.shape[1]
    for z in range(4):
        for y in range(2):
            b = block_of(y, z, dp_ref[0])
            half, spot = spot_of(y, z, "y")
            o = (keep_ref, send_ref)[half]
            rows = pl.ds(pl.multiple_of(b * tall, tall), tall)
            o[spot, :, :three] = acc[rows, :].astype(bf16)
            if len(rest) > 3:
                out = rest[0][:, rows].astype(f32) + rest[1][:, rows].astype(f32) + rest[2][:, rows].astype(f32)
                for i in range(out.shape[0] // tall):
                    o[spot, :, three + i * tall : three + (i + 1) * tall] = out[i * tall : (i + 1) * tall].astype(bf16)


def wgrad_qkv(me, dp, grad, n_list, w_parts=()):
    length, three = grad.shape
    each, width = n_list[0].shape
    extra = w_parts[0].shape[0] if w_parts else 0
    vm = pl.BlockSpec(memory_space=pltpu.VMEM)
    return pl.pallas_call(
        functools.partial(wgrad_qkv_kernel, each=each),
        in_specs=[smem(), smem()] + [vm] * (5 + len(w_parts)),
        out_specs=[vm] * 2,
        out_shape=[shaped((4, width // 8, three + extra), bf16)] * 2,
        scratch_shapes=[pltpu.VMEM((width, three), f32)],
        compiler_params=params(),
        cost_estimate=cost(2 * length * width * three, 2 * length * (width + three) + 2 * width * (three + 4 * extra)),
        name="wgrad_qkv",
    )(me, dp, grad, *n_list, *w_parts)


def add_split_kernel(a_ref, b_ref, o0, o1):
    half = o0.shape[0]
    o0[...] = (a_ref[:half].astype(f32) + b_ref[:half].astype(f32)).astype(bf16)
    o1[...] = (a_ref[half:].astype(f32) + b_ref[half:].astype(f32)).astype(bf16)


def add_split(a, b):
    vm = pl.BlockSpec(memory_space=pltpu.VMEM)
    half = (a.shape[0] // 2,) + a.shape[1:]
    return pl.pallas_call(
        add_split_kernel,
        in_specs=[vm] * 2,
        out_specs=[vm] * 2,
        out_shape=[shaped(half, bf16)] * 2,
        compiler_params=params(),
        cost_estimate=cost(a.size, 6 * a.size),
        name="add_split",
    )(a, b)


class Chain:
    def __init__(self, kept, sent, lead="y"):
        self.single = lax.axis_size("dp") != 8
        self.steps = 0
        self.kept = kept
        if self.single:
            self.parts = (lax.psum(kept, "dp"), lax.psum(sent, "dp"))
            return
        self.bits = (1, 2, 4, 2, 1) if lead == "y" else (2, 1, 4, 1, 2)
        self.flying = swap(sent, self.bits[0], "dp")

    def close(self, *others):
        if self.single:
            return (self.kept,)
        self.flying = join(self.flying, *others)[0]
        return (self.flying,)

    def step(self, *others):
        if self.single:
            return (self.kept,)
        self.steps += 1
        got = join(self.flying, *others)[0]
        if self.steps == 1:
            self.kept, sent = add_split(self.kept, got)
        elif self.steps == 2:
            self.kept = sent = add_low(self.kept, got)
        elif self.steps == 3:
            self.kept = sent = add_low(self.kept, got[::-1])
        elif self.steps == 4:
            self.kept = sent = jnp.concatenate([self.kept, got], axis=0)
        else:
            self.parts = (self.kept, got)
            return (got,)
        self.flying = swap(sent, self.bits[self.steps], "dp")
        return (sent,)

    def finish(self, *others):
        while not self.single and self.steps < 5:
            self.step(*others)
        return self.parts


def pieces(refs, lead="y"):
    for y in range(2):
        for z in range(4):
            half, spot = spot_of(y, z, lead)
            yield y, z, refs[half], spot


def finish_down_kernel(dp_ref, k_ref, s_ref, o_ref):
    wide = k_ref.shape[2]
    for y, z, ref, spot in pieces((k_ref, s_ref)):
        cols = pl.ds(pl.multiple_of(block_of(y, z, dp_ref[0]) * wide, wide), wide)
        o_ref[:, cols] = ref[spot].astype(f32)


def finish_down(dp, parts, shape):
    vm = pl.BlockSpec(memory_space=pltpu.VMEM)
    return pl.pallas_call(
        finish_down_kernel,
        in_specs=[smem()] + [vm] * 2,
        out_specs=vm,
        out_shape=shaped(shape, f32),
        compiler_params=params(),
        cost_estimate=cost(shape[0] * shape[1], 6 * shape[0] * shape[1]),
        name="finish_down",
    )(dp, *parts)


def finish_cols_kernel(dp_ref, k_ref, s_ref, w_ref, gain_ref, *rest, lead):
    o_ref, part_ref = rest[-2:]
    wide = k_ref.shape[2]
    for y, z, ref, spot in pieces((k_ref, s_ref), lead):
        cols = pl.ds(pl.multiple_of(block_of(y, z, dp_ref[0]) * wide, wide), wide)
        grad = ref[spot].astype(f32)
        o_ref[0, :, cols] = grad
        part_ref[:, cols] = jnp.sum(grad * w_ref[0, :, cols].astype(f32), axis=0, keepdims=True) / gain_ref[:, cols]


def finish_cols(dp, parts, w, gain, index, into=None, lead="y"):
    two, hid, width = w.shape
    one = pl.BlockSpec((1, hid, width), lambda i: (index, 0, 0))
    extra = () if into is None else (into,)
    return pl.pallas_call(
        functools.partial(finish_cols_kernel, lead=lead),
        grid=(1,),
        in_specs=[smem(), whole(*parts[0].shape), whole(*parts[1].shape), one, whole(1, width)] + [pl.BlockSpec(memory_space=pl.ANY)] * len(extra),
        out_specs=[one, whole(1, width)],
        out_shape=[shaped(w.shape, f32), shaped((1, width), f32)],
        input_output_aliases={5: 0} if extra else {},
        compiler_params=params(),
        cost_estimate=cost(4 * hid * width, 8 * hid * width),
        name="finish_cols",
    )(dp, *parts, w, gain, *extra)


def half_gain_kernel(dp_ref, a_ref, b_ref, w_ref, gain_ref, o_ref, *, y):
    tall = a_ref.shape[1]
    o_ref[...] = jnp.zeros_like(o_ref)
    for z in range(4):
        _, spot = spot_of(y, z, "y")
        rows = pl.ds(pl.multiple_of(block_of(y, z, dp_ref[0]) * tall, tall), tall)
        total = None
        for idx in range(3):
            part = slice(idx * LANES, (idx + 1) * LANES)
            for pair, ref in enumerate((a_ref, b_ref)):
                term = ref[spot, :, part].astype(f32) * w_ref[idx, rows, pair * LANES : (pair + 1) * LANES].astype(f32)
                total = term if total is None else total + term
        total = jnp.sum(total, axis=1, keepdims=True)
        o_ref[:, rows] = jnp.transpose(jnp.broadcast_to(total, (tall, LANES)))[0:1] / gain_ref[:, rows]


def half_gain(dp, first, second, w, gain, y):
    vm = pl.BlockSpec(memory_space=pltpu.VMEM)
    width = w.shape[1]
    return pl.pallas_call(
        functools.partial(half_gain_kernel, y=y),
        in_specs=[smem()] + [vm] * 4,
        out_specs=vm,
        out_shape=shaped((1, width), f32),
        compiler_params=params(),
        cost_estimate=cost(2 * w.size, 4 * w.size),
        name="half_gain",
    )(dp, first, second, w, gain)


def finish_qkv_kernel(dp_ref, ak, sk, bk, bs, o_ref, out_ref):
    tall = ak.shape[1]
    cols = out_ref.shape[0]
    three = 3 * LANES
    for (y, z, a, spot), (_, _, b, _) in zip(pieces((ak, sk)), pieces((bk, bs))):
        rows = pl.ds(pl.multiple_of(block_of(y, z, dp_ref[0]) * tall, tall), tall)
        for idx in range(3):
            part = slice(idx * LANES, (idx + 1) * LANES)
            o_ref[idx, rows, :LANES] = a[spot, :, part].astype(f32)
            o_ref[idx, rows, LANES:] = b[spot, :, part].astype(f32)
        for k in range(cols // tall):
            out_ref[k * tall : (k + 1) * tall, rows] = a[spot, :, three + k * tall : three + (k + 1) * tall].astype(f32)


def finish_qkv(dp, first, second, cols):
    vm = pl.BlockSpec(memory_space=pltpu.VMEM)
    width = 8 * first[0].shape[1]
    return pl.pallas_call(
        finish_qkv_kernel,
        in_specs=[smem()] + [vm] * 4,
        out_specs=[vm] * 2,
        out_shape=[shaped((3, width, cols), f32), shaped((cols, width), f32)],
        compiler_params=params(),
        cost_estimate=cost(8 * cols * width, 24 * cols * width),
        name="finish_qkv",
    )(dp, *first, *second)


def on_device(tokens, counts, gain_attn, gain_ffn, w_qkv, w_out, w_gate_up, w_down, cotangent):
    rows, width = tokens.shape
    columns = w_qkv.shape[2]
    hid = w_gate_up.shape[2]
    me = lax.axis_index("mp").astype(jnp.int32).reshape(1)
    dp = jnp.zeros((1,), jnp.int32)
    if lax.axis_size("dp") == 8:
        dp = lax.axis_index("dp").astype(jnp.int32).reshape(1)
    gain_a = gain_attn.reshape(1, width)
    gain_f = gain_ffn.reshape(1, width)
    qkv_w = jnp.transpose(w_qkv, (1, 0, 2))
    gate_up_w = jnp.transpose(w_gate_up, (1, 2, 0))

    n0 = norm(tokens, gain_a)
    n2 = far_of(n0)
    n1 = swap(n0, 1)
    p0, p1 = project(n0, n1, qkv_w)
    n2, p0, p1 = join(n2, p0, p1)
    n = [n0, n1, n2, swap(n2, 1)]
    out2 = far_of(after(w_out, n2))
    cot2 = far_of(after(cotangent, *n[2:]))
    qkv, attended, lse, *a = attn_fwd(me, counts, p0, p1, n[2], n[3], qkv_w)
    out2, *a = join(out2, *a)
    out_w = [w_out, swap(w_out, 1), out2, swap(out2, 1)]
    a = exchange_rel(a)
    cot2, *a = join(cot2, *a)
    cot = [cotangent, swap(cotangent, 1), cot2, swap(cot2, 1)]
    middle, m0 = middle_of(tokens, a, out_w, gain_f)
    m2 = far_of(m0)
    m1 = swap(m0, 1)
    hid_a, gg_a, gu_a, d0, d1, g0, g1 = ffn(m0, m1, cot[0], cot[1], gate_up_w, w_down)
    m2, hid_a, gg_a, gu_a, d0, d1, g0, g1 = join(m2, hid_a, gg_a, gu_a, d0, d1, g0, g1)
    m = [m0, m1, m2, swap(m2, 1)]
    g1, d1 = swap(g1, 1), swap(d1, 1)
    hid_b, gg_b, gu_b, d2, d3, g2, g3 = ffn(m[2], m[3], cot[2], cot[3], gate_up_w, w_down)
    g1, d1, g2, g3 = join(g1, d1, g2, g3)
    sent = add_low(g2, swap(g3, 1))
    s2 = far_of(sent)
    d3 = swap(after(d3, sent), 1)
    down = Chain(*wgrad_cols(dp, after(hid_a, sent), hid_b, cot))
    parts = wgrad_cols(dp, after(gu_a, down.kept), gu_b, m)
    up = Chain(*parts)
    parts = wgrad_cols(dp, after(gg_a, up.kept), gg_b, m, "z")
    gate_kept, gate_sent = parts
    lat_sent = add_low(d2, d3)
    x = down.step(gate_kept)
    s2 = join(s2, lat_sent, *x)[0]
    grad_middle, low, *ga = grad_middle_of(cotangent, middle, (g0, g1, s2), gain_f, out_w)
    d_list = exchange_rel(ga)
    gate = Chain(gate_kept, after(gate_sent, low), "z")
    w0, w1, w2, w3 = wgrad_out(low, a)
    x = up.step(w0) + down.step(w0)
    d_list = join(*d_list, *x)[:4]
    w1, w3 = join(swap(w1, 1), swap(w3, 1), *d_list)[:2]
    w_sent = add_low(w2, w3)
    w2 = far_of(w_sent)
    grad0 = attn_bwd(me, counts, qkv, d_list, attended, lse, 0, (w_sent,))
    w2 = join(w2, grad0)[0]
    x = down.step(grad0) + up.step(grad0) + gate.step(grad0)
    parts = wgrad_qkv(me, dp, after(grad0, *x), n, (w0, w1, w2))
    first = Chain(*parts)
    lat2 = far_of(after(lat_sent, first.kept))
    grad1 = attn_bwd(me, counts, qkv, d_list, attended, lse, 1, (first.kept,))
    x = down.step(grad1) + up.step(grad1) + gate.step(grad1) + first.close(grad1) + (lat2,)
    t2, t3 = qkv_dgrad(me, grad0, after(grad1, *x), qkv_w, 2, 3)
    t3 = swap(t3, 1)
    t0, t1 = qkv_dgrad(me, grad0, after(grad1, t2), qkv_w, 0, 1)
    t3 = join(t3, t0)[0]
    sent = add_low(t2, t3)
    t2 = far_of(sent)
    x = first.step(sent)
    parts = wgrad_qkv(me, dp, after(grad1, *x), n)
    second = Chain(*parts)
    latents = middle + d0.astype(f32) + d1.astype(f32) + after(lat2, second.kept).astype(f32)
    t1 = swap(after(t1, latents), 1)
    x = up.step(latents)
    x = first.step(*x)
    x = gate.step(*x)
    x = second.step(*x)
    grad_w_down = finish_down(dp, down.finish(*x), (hid, width))
    x = first.step(grad_w_down)
    x = second.step(*x)
    t0, t1, t2 = join(t0, t1, t2, *x)[:3]
    grad_tokens = grad_tokens_of(grad_middle, tokens, (t0, t1, t2), gain_a)
    x = first.step(grad_tokens)
    x = second.step(*x)
    grad_w_gate_up, part_u = finish_cols(dp, up.finish(*x), gate_up_w, gain_f, 1)
    x = second.step(grad_w_gate_up)
    if lax.axis_size("dp") == 8:
        gain_1 = half_gain(dp, first.kept, after(second.kept, *x), qkv_w, gain_a, 0)
        gain_1 = gain_1 + swap(gain_1, 1) + swap(gain_1, 2) + swap(gain_1, 3)
        gain_1 = gain_1 + swap(gain_1, 1, "dp")
    else:
        parts = [half_gain(dp, first.parts[y], second.parts[y], qkv_w, gain_a, y) for y in range(2)]
        gain_1 = parts[0] + parts[1]
        gain_1 = gain_1 + swap(gain_1, 1) + swap(gain_1, 2) + swap(gain_1, 3)
    grad_w_gate_up, part_g = finish_cols(dp, gate.finish(*x), gate_up_w, gain_f, 0, grad_w_gate_up, "z")
    gain_2 = part_u + part_g
    gain_2 = gain_2 + swap(gain_2, 1) + swap(gain_2, 2) + swap(gain_2, 3)
    grad_w_qkv, grad_w_out = finish_qkv(dp, first.finish(grad_w_gate_up), second.finish(grad_w_gate_up), columns)
    gains = (gain_1, gain_2)
    grad_w_qkv = jnp.transpose(grad_w_qkv, (1, 0, 2))
    grad_w_gate_up = jnp.transpose(grad_w_gate_up, (2, 0, 1))
    return (
        latents,
        grad_tokens,
        gains[0].reshape(width),
        gains[1].reshape(width),
        grad_w_qkv,
        grad_w_out,
        grad_w_gate_up,
        grad_w_down,
    )


def solution(mesh):
    placed = (
        P(("dp", "mp"), None),
        P("dp"),
        P(),
        P(),
        P(None, None, "mp"),
        P("mp", None),
        P(None, None, "mp"),
        P("mp", None),
        P(("dp", "mp"), None),
    )
    return jax.shard_map(
        on_device,
        mesh=mesh,
        in_specs=placed,
        out_specs=(
            P(("dp", "mp"), None),
            P(("dp", "mp"), None),
            P(),
            P(),
            P(None, None, "mp"),
            P("mp", None),
            P(None, None, "mp"),
            P("mp", None),
        ),
        check_vma=False,
    )
```

```python
import functools

import jax
import jax.numpy as jnp
from jax import lax
from jax.experimental import pallas as pl
from jax.experimental.pallas import tpu as pltpu
from jax.sharding import PartitionSpec as P

HD = 64
EPS = 1e-05
LANES = 128
LOG2E = 1.4426950408889634
NN = (((1,), (0,)), ((), ()))
NT = (((1,), (1,)), ((), ()))
TN = (((0,), (0,)), ((), ()))
f32 = jnp.float32
bf16 = jnp.bfloat16
VMEM_LIMIT = 28 << 20
SHARE = 1


def dot(a, b, dims=NN):
    return lax.dot_general(a, b, dims, preferred_element_type=f32)


def whole(*shape):
    return pl.BlockSpec(shape, lambda *_: (0,) * len(shape))


def smem():
    return pl.BlockSpec(memory_space=pltpu.SMEM)


def shaped(shape, dtype):
    return jax.ShapeDtypeStruct(shape, dtype)


def params():
    return pltpu.CompilerParams(vmem_limit_bytes=VMEM_LIMIT)


def cost(flops, bytes_accessed, transcendentals=0):
    return pl.CostEstimate(
        flops=int(flops * SHARE), bytes_accessed=int(bytes_accessed * SHARE), transcendentals=int(transcendentals * SHARE)
    )


def swap(value, bit, axis="mp"):
    size = lax.axis_size(axis)
    return lax.ppermute(value, axis, [(i, i ^ bit) for i in range(size)])


def after(value, *others):
    return lax.optimization_barrier((value,) + others)[0]


def join(*values):
    return lax.optimization_barrier(values)


def far_of(value):
    return swap(value, 2)


def exchange_rel(parts):
    return [parts[0]] + [swap(parts[k], k) for k in (1, 2, 3)]


def add_low(a, b):
    return (a.astype(f32) + b.astype(f32)).astype(bf16)


def head_lanes(rows, parity):
    lane = lax.broadcasted_iota(jnp.int32, (rows, LANES), 1)
    return (lane // HD) == parity, lane == (1 - parity) * HD


def norm_kernel(x_ref, gain_ref, o_ref):
    x = x_ref[...].astype(f32)
    r = lax.rsqrt(jnp.mean(x * x, axis=1, keepdims=True) + EPS)
    o_ref[...] = (x * r * gain_ref[...]).astype(bf16)


def norm(x, gain):
    rows, width = x.shape
    step = 256
    block = pl.BlockSpec((step, width), lambda i: (i, 0))
    return pl.pallas_call(
        norm_kernel,
        grid=(rows // step,),
        in_specs=[block, whole(1, width)],
        out_specs=block,
        out_shape=shaped((rows, width), bf16),
        compiler_params=params(),
        cost_estimate=cost(rows * width * 8, rows * width * 4),
        name="norm",
    )(x, gain)


def project_kernel(a_ref, b_ref, w_ref, oa_ref, ob_ref):
    cols = w_ref.shape[2]
    for x, o in ((a_ref, oa_ref), (b_ref, ob_ref)):
        for i in range(3):
            o[:, i * cols : (i + 1) * cols] = dot(x[...], w_ref[i]).astype(bf16)


def project(a, b, w):
    rows, width = a.shape
    cols = w.shape[2]
    step = 256
    block = pl.BlockSpec((step, width), lambda i: (i, 0))
    block_out = pl.BlockSpec((step, 3 * cols), lambda i: (i, 0))
    return pl.pallas_call(
        project_kernel,
        grid=(rows // step,),
        in_specs=[block, block, whole(3, width, cols)],
        out_specs=[block_out, block_out],
        out_shape=[shaped((rows, 3 * cols), bf16)] * 2,
        compiler_params=params(),
        cost_estimate=cost(12 * rows * width * cols, 4 * rows * (width + 3 * cols)),
        name="project",
    )(a, b, w)


def attn_fwd_kernel(me_ref, count_ref, p0_ref, p1_ref, n2_ref, n3_ref, w_ref, qkv_ref, o_ref, lse_ref, a0_ref, a1_ref, a2_ref, a3_ref, kaug, *, length, columns, block):
    h = pl.program_id(0)
    rows_each = length // 4
    me = me_ref[0]

    def spot(k):
        return pl.ds(pl.multiple_of((me ^ k) * rows_each, rows_each), rows_each)

    @pl.when(h == 0)
    def _():
        qkv_ref[spot(0), :] = p0_ref[...]
        qkv_ref[spot(1), :] = p1_ref[...]
        for k, n in ((2, n2_ref), (3, n3_ref)):
            for i in range(3):
                qkv_ref[spot(k), i * columns : (i + 1) * columns] = dot(n[...], w_ref[i]).astype(bf16)

    parity = lax.rem(h, 2)
    col = pl.multiple_of((h // 2) * LANES, LANES)
    c = HD**-0.5 * LOG2E
    sel, spare = head_lanes(length, parity)
    row = lax.broadcasted_iota(jnp.int32, (length, LANES), 0)
    k = qkv_ref[:, pl.ds(columns + col, LANES)].astype(f32)
    bias = jnp.where(row < count_ref[0], 0.0, -1e30)
    kaug[...] = jnp.where(sel, k, jnp.where(spare, bias, 0.0)).astype(bf16)
    sel_b, spare_b = head_lanes(block, parity)
    ri = lax.broadcasted_iota(jnp.int32, (block, block), 0)
    ci = lax.broadcasted_iota(jnp.int32, (block, block), 1)
    for i in range(length // block):
        first = i * block
        n = first + block
        rows = pl.ds(first, block)
        q = qkv_ref[rows, pl.ds(col, LANES)].astype(f32)
        q = jnp.where(sel_b, q, jnp.where(spare_b, 1.0, 0.0)).astype(bf16)
        s_d = dot(q, kaug[first:n], NT)
        s_d = jnp.where(ci <= ri, s_d, -1e30)
        m = jnp.max(s_d, axis=1, keepdims=True)
        if first:
            s_o = dot(q, kaug[:first], NT)
            m = jnp.maximum(m, jnp.max(s_o, axis=1, keepdims=True))
        mc = m * c
        p_d = jnp.exp2(s_d * c - mc)
        total = jnp.sum(p_d, axis=1, keepdims=True)
        o = dot(p_d.astype(bf16), qkv_ref[first:n, pl.ds(2 * columns + col, LANES)])
        if first:
            p_o = jnp.exp2(s_o * c - mc)
            total = total + jnp.sum(p_o, axis=1, keepdims=True)
            o = o + dot(p_o.astype(bf16), qkv_ref[:first, pl.ds(2 * columns + col, LANES)])
        o = (o / total).astype(bf16)
        out = pl.ds(col, LANES)
        o_ref[rows, out] = jnp.where(sel_b, o, o_ref[rows, out])
        lse = mc + jnp.log2(total)
        lse_ref[pl.ds(h, 1), first:n] = jnp.transpose(jnp.broadcast_to(lse, (block, LANES)))[0:1]

    @pl.when(h == pl.num_programs(0) - 1)
    def _():
        for k, ref in enumerate((a0_ref, a1_ref, a2_ref, a3_ref)):
            ref[...] = o_ref[spot(k), :]


def attn_fwd(me, count, p0, p1, n2, n3, w, block=512):
    each, width = n2.shape
    length = 4 * each
    columns = w.shape[2]
    three = 3 * columns
    heads = columns // HD
    return pl.pallas_call(
        functools.partial(attn_fwd_kernel, length=length, columns=columns, block=block),
        grid=(heads,),
        out_shape=[shaped((length, three), bf16), shaped((length, columns), bf16), shaped((heads, length), f32)]
        + [shaped((each, columns), bf16)] * 4,
        in_specs=[smem(), smem(), whole(each, three), whole(each, three), whole(each, width), whole(each, width), whole(3, width, columns)],
        out_specs=[whole(length, three), whole(length, columns), whole(heads, length)] + [whole(each, columns)] * 4,
        scratch_shapes=[pltpu.VMEM((length, LANES), bf16)],
        compiler_params=params(),
        cost_estimate=cost(10 * length * length * columns, 2 * length * columns * 8, length * length * heads // 2),
        name="attn_fwd",
    )(me, count, p0, p1, n2, n3, w)


def attn_bwd_kernel(me_ref, count_ref, q_ref, k_ref, v_ref, d0_ref, d1_ref, d2_ref, d3_ref, o_ref, lse_ref, *rest, length, block, pair):
    g_ref, do_all, kaug, qaug, dom, vaug, dq = rest[-7:]
    parity = pl.program_id(0)
    rows_each = length // 4
    me = me_ref[0]

    @pl.when(parity == 0)
    def _():
        for k, ref in enumerate((d0_ref, d1_ref, d2_ref, d3_ref)):
            do_all[pl.ds(pl.multiple_of((me ^ k) * rows_each, rows_each), rows_each), :] = ref[...]

    scale = HD**-0.5
    c = scale * LOG2E
    sel, spare = head_lanes(length, parity)
    row = lax.broadcasted_iota(jnp.int32, (length, LANES), 0)
    bias = jnp.where(row < count_ref[0], 0.0, -1e30)
    offset = lax.broadcasted_iota(jnp.int32, (length, LANES), 1) - (1 - parity) * HD
    extra = (offset >= 1) & (offset <= 3)

    def in_lanes(column):
        high = column.astype(bf16).astype(f32)
        rest_1 = column - high
        middle = rest_1.astype(bf16).astype(f32)
        return jnp.where(offset == 1, high, jnp.where(offset == 2, middle, jnp.where(offset == 3, rest_1 - middle, 0.0)))

    ones = jnp.where(extra, 1.0, 0.0)
    kaug[...] = jnp.where(sel, k_ref[...].astype(f32), jnp.where(spare, bias, ones)).astype(bf16)
    vaug[...] = jnp.where(sel, v_ref[...].astype(f32), ones).astype(bf16)
    lse = lse_ref[pl.ds(2 * pair + parity, 1), :]
    shift = in_lanes(jnp.transpose(jnp.broadcast_to(lse * (-1.0 / c), (LANES, length))))
    qaug[...] = jnp.where(sel, q_ref[...].astype(f32), jnp.where(spare, 1.0, shift)).astype(bf16)
    do = jnp.where(sel, do_all[...].astype(f32), 0.0)
    delta = jnp.sum(do * o_ref[...].astype(f32), axis=1, keepdims=True)
    dom[...] = (do + in_lanes(jnp.broadcast_to(-delta, (length, LANES)))).astype(bf16)
    sel_b, _ = head_lanes(block, parity)
    ki = lax.broadcasted_iota(jnp.int32, (block, block), 0)
    qi = lax.broadcasted_iota(jnp.int32, (block, block), 1)
    dq[...] = jnp.zeros_like(dq)
    for j in range(length // block):
        first = j * block
        last = first + block
        kj = kaug[first:last]
        vj = vaug[first:last]

        def part(a, b, diag):
            s = dot(kj, qaug[a:b], NT)
            if diag:
                s = jnp.where(ki <= qi, s, -1e30)
            p = jnp.exp2(s * c)
            dp = dot(vj, dom[a:b], NT)
            ds = (p * dp).astype(bf16)
            dv = dot(p.astype(bf16), dom[a:b])
            dk = dot(ds, qaug[a:b])
            dq[a:b] += dot(ds, kj, TN)
            return dv, dk

        dv, dk = part(first, last, True)
        if last < length:
            dv2, dk2 = part(last, length, False)
            dv = dv + dv2
            dk = dk + dk2
        for idx, val in ((1, dk * scale), (2, dv)):
            out = slice(idx * LANES, (idx + 1) * LANES)
            g_ref[first:last, out] = jnp.where(sel_b, val.astype(bf16), g_ref[first:last, out])
    g_ref[:, :LANES] = jnp.where(sel, (dq[...] * scale).astype(bf16), g_ref[:, :LANES])


def attn_bwd(me, count, qkv, d_list, o, lse, pair, deps=(), block=512):
    length, three = qkv.shape
    columns = three // 3
    heads = columns // HD
    pairs = columns // LANES
    each = length // 4

    def part(rows, col):
        return pl.BlockSpec((rows, LANES), lambda i: (0, col))

    return pl.pallas_call(
        functools.partial(attn_bwd_kernel, length=length, block=block, pair=pair),
        grid=(2,),
        out_shape=shaped((length, 3 * LANES), bf16),
        in_specs=[smem(), smem()]
        + [part(length, i * pairs + pair) for i in range(3)]
        + [part(each, pair)] * 4
        + [part(length, pair), whole(heads, length)]
        + [pl.BlockSpec(memory_space=pl.ANY)] * len(deps),
        out_specs=whole(length, 3 * LANES),
        scratch_shapes=[pltpu.VMEM((length, LANES), bf16)] * 5 + [pltpu.VMEM((length, LANES), f32)],
        compiler_params=params(),
        cost_estimate=cost(20 * length * length * LANES, 2 * length * LANES * 8, length * length),
        name="attn_bwd",
    )(me, count, qkv, qkv, qkv, *d_list, o, lse, *deps)


def middle_kernel(x_ref, a0, a1, a2, a3, w0, w1, w2, w3, gain_ref, mid_ref, normed_ref):
    total = x_ref[...].astype(f32)
    acc = dot(a0[...], w0[...]) + dot(a1[...], w1[...]) + dot(a2[...], w2[...]) + dot(a3[...], w3[...])
    total = total + acc
    mid_ref[...] = total
    r = lax.rsqrt(jnp.mean(total * total, axis=1, keepdims=True) + EPS)
    normed_ref[...] = (total * r * gain_ref[...]).astype(bf16)


def middle_of(tokens, a_list, w_list, gain):
    rows, width = tokens.shape
    cols = a_list[0].shape[1]
    step = 256
    block = pl.BlockSpec((step, width), lambda i: (i, 0))
    block_a = pl.BlockSpec((step, cols), lambda i: (i, 0))
    return pl.pallas_call(
        middle_kernel,
        grid=(rows // step,),
        in_specs=[block] + [block_a] * 4 + [whole(cols, width)] * 4 + [whole(1, width)],
        out_specs=[block, block],
        out_shape=[shaped((rows, width), f32), shaped((rows, width), bf16)],
        compiler_params=params(),
        cost_estimate=cost(2 * rows * width * width, rows * width * 10 + 2 * width * width),
        name="middle",
    )(tokens, *a_list, *w_list, gain)


def ffn_kernel(na, nb, ca, cb, w, wd, hid_ref, gg_ref, gu_ref, pda, pdb, pga, pgb, xs, cs, *, half):
    i = pl.program_id(0)

    @pl.when(i < half)
    def _():
        xs[...] = na[...]
        cs[...] = ca[...]

    @pl.when(i >= half)
    def _():
        xs[...] = nb[...]
        cs[...] = cb[...]

    x = xs[...]
    gate = dot(x, w[0], NT)
    up = dot(x, w[1], NT)
    grad_hidden = dot(cs[...], wd[...], NT)
    sig = jax.nn.sigmoid(gate)
    silu = gate * sig
    hidden = (silu * up).astype(bf16)
    hid_ref[...] = hidden
    gg = (grad_hidden * up * (sig * (1.0 + gate * (1.0 - sig)))).astype(bf16)
    gu = (grad_hidden * silu).astype(bf16)
    gg_ref[...] = gg
    gu_ref[...] = gu
    down = dot(hidden, wd[...]).astype(bf16)
    grad_normed = (dot(gg, w[0]) + dot(gu, w[1])).astype(bf16)

    @pl.when(i < half)
    def _():
        pda[...] = down
        pga[...] = grad_normed

    @pl.when(i >= half)
    def _():
        pdb[...] = down
        pgb[...] = grad_normed


def ffn(na, nb, ca, cb, w, wd):
    rows, width = na.shape
    hid = wd.shape[0]
    step = 256
    half = rows // step
    first = pl.BlockSpec((step, width), lambda i: (jnp.minimum(i, half - 1), 0))
    second = pl.BlockSpec((step, width), lambda i: (jnp.maximum(i - half, 0), 0))
    block_h = pl.BlockSpec((step, hid), lambda i: (i, 0))
    return pl.pallas_call(
        functools.partial(ffn_kernel, half=half),
        grid=(2 * half,),
        in_specs=[first, second, first, second, whole(2, hid, width), whole(hid, width)],
        out_specs=[block_h] * 3 + [first, second] * 2,
        out_shape=[shaped((2 * rows, hid), bf16)] * 3 + [shaped((rows, width), bf16)] * 4,
        scratch_shapes=[pltpu.VMEM((step, width), bf16)] * 2,
        compiler_params=params(),
        cost_estimate=cost(24 * rows * width * hid, 12 * rows * (width + hid), 2 * rows * hid),
        name="ffn",
    )(na, nb, ca, cb, w, wd)


def grad_middle_kernel(cot, mid, g0, g1, g2, gain, w0, w1, w2, w3, gm_ref, gml_ref, o0, o1, o2, o3):
    dn = g0[...].astype(f32) + g1[...].astype(f32) + g2[...].astype(f32)
    x = mid[...]
    r = lax.rsqrt(jnp.mean(x * x, axis=1, keepdims=True) + EPS)
    e = dn * gain[...]
    gm = cot[...].astype(f32) + r * e - x * (r * r * r * jnp.mean(e * x, axis=1, keepdims=True))
    gm_ref[...] = gm
    low = gm.astype(bf16)
    gml_ref[...] = low
    for w, o in ((w0, o0), (w1, o1), (w2, o2), (w3, o3)):
        o[...] = dot(low, w[...], NT).astype(bf16)


def grad_middle_of(cot, mid, parts, gain, w_list):
    rows, width = cot.shape
    cols = w_list[0].shape[0]
    step = 256
    block = pl.BlockSpec((step, width), lambda i: (i, 0))
    block_a = pl.BlockSpec((step, cols), lambda i: (i, 0))
    return pl.pallas_call(
        grad_middle_kernel,
        grid=(rows // step,),
        in_specs=[block] * 5 + [whole(1, width)] + [whole(cols, width)] * 4,
        out_specs=[block, block] + [block_a] * 4,
        out_shape=[shaped((rows, width), f32), shaped((rows, width), bf16)] + [shaped((rows, cols), bf16)] * 4,
        compiler_params=params(),
        cost_estimate=cost(2 * rows * width * width, rows * width * 20 + 2 * width * width),
        name="grad_middle",
    )(cot, mid, *parts, gain, *w_list)


def grad_tokens_kernel(gm, tok, g0, g1, g2, gain, out_ref):
    dn = g0[...].astype(f32) + g1[...].astype(f32) + g2[...].astype(f32)
    x = tok[...].astype(f32)
    r = lax.rsqrt(jnp.mean(x * x, axis=1, keepdims=True) + EPS)
    e = dn * gain[...]
    out_ref[...] = gm[...] + r * e - x * (r * r * r * jnp.mean(e * x, axis=1, keepdims=True))


def grad_tokens_of(gm, tokens, parts, gain):
    rows, width = gm.shape
    step = 256
    block = pl.BlockSpec((step, width), lambda i: (i, 0))
    return pl.pallas_call(
        grad_tokens_kernel,
        grid=(rows // step,),
        in_specs=[block] * 5 + [whole(1, width)],
        out_specs=block,
        out_shape=shaped((rows, width), f32),
        compiler_params=params(),
        cost_estimate=cost(rows * width * 20, rows * width * 20),
        name="grad_tokens",
    )(gm, tokens, *parts, gain)


def qkv_dgrad_kernel(me_ref, g0_ref, g1_ref, w_ref, oa_ref, ob_ref, *, ka, kb):
    each = oa_ref.shape[0]
    me = me_ref[0]
    for k, o in ((ka, oa_ref), (kb, ob_ref)):
        rows = pl.ds(pl.multiple_of((me ^ k) * each, each), each)
        total = None
        for i in range(3):
            cols = slice(i * LANES, (i + 1) * LANES)
            g = jnp.concatenate([g0_ref[rows, cols], g1_ref[rows, cols]], axis=1)
            term = dot(g, w_ref[i], NT)
            total = term if total is None else total + term
        o[...] = total.astype(bf16)


def qkv_dgrad(me, g0, g1, w, ka, kb):
    length, three = g0.shape
    width = w.shape[1]
    each = length // 4
    vm = pl.BlockSpec(memory_space=pltpu.VMEM)
    return pl.pallas_call(
        functools.partial(qkv_dgrad_kernel, ka=ka, kb=kb),
        in_specs=[smem()] + [vm] * 3,
        out_specs=[vm] * 2,
        out_shape=[shaped((each, width), bf16)] * 2,
        compiler_params=params(),
        cost_estimate=cost(8 * each * width * three, 2 * (2 * length * three + 2 * width * three + 2 * each * width)),
        name="qkv_dgrad",
    )(me, g0, g1, w)


def block_of(y, z, me):
    return (2 * z + y) ^ me


def spot_of(y, z, lead):
    if lead == "y":
        return y, (z & 1) * 2 + (z >> 1)
    return z & 1, y * 2 + (z >> 1)


def wgrad_cols_kernel(dp_ref, ha, hb, c0, c1, c2, c3, *rest, each, lead):
    acc = rest[-1]
    halves = rest[-3:-1]
    acc[...] = dot(ha[:each], c0[...], TN)
    acc[...] += dot(ha[each:], c1[...], TN)
    acc[...] += dot(hb[:each], c2[...], TN)
    acc[...] += dot(hb[each:], c3[...], TN)
    wide = halves[0].shape[2]
    for z in range(4):
        for y in range(2):
            b = block_of(y, z, dp_ref[0])
            half, spot = spot_of(y, z, lead)
            halves[half][spot] = acc[:, pl.ds(pl.multiple_of(b * wide, wide), wide)].astype(bf16)


def wgrad_cols(dp, ha, hb, c_list, lead="y"):
    hid = ha.shape[1]
    each, width = c_list[0].shape
    vm = pl.BlockSpec(memory_space=pltpu.VMEM)
    return pl.pallas_call(
        functools.partial(wgrad_cols_kernel, each=each, lead=lead),
        in_specs=[smem()] + [vm] * 6,
        out_specs=[vm] * 2,
        out_shape=[shaped((4, hid, width // 8), bf16)] * 2,
        scratch_shapes=[pltpu.VMEM((hid, width), f32)],
        compiler_params=params(),
        cost_estimate=cost(8 * each * width * hid, 8 * each * (width + hid) + 2 * width * hid),
        name="wgrad_cols",
    )(dp, ha, hb, *c_list)


def wgrad_out_kernel(gml, a0, a1, a2, a3, o0, o1, o2, o3):
    for a, o in ((a0, o0), (a1, o1), (a2, o2), (a3, o3)):
        o[...] = dot(a[...], gml[...], TN).astype(bf16)


def wgrad_out(gml, a_list):
    each, width = gml.shape
    cols = a_list[0].shape[1]
    vm = pl.BlockSpec(memory_space=pltpu.VMEM)
    return pl.pallas_call(
        wgrad_out_kernel,
        in_specs=[vm] * 5,
        out_specs=[vm] * 4,
        out_shape=[shaped((cols, width), bf16)] * 4,
        compiler_params=params(),
        cost_estimate=cost(8 * each * width * cols, 4 * each * width + 2 * width * width),
        name="wgrad_out",
    )(gml, *a_list)


def wgrad_qkv_kernel(me_ref, dp_ref, g_ref, n0, n1, n2, n3, *rest, each):
    keep_ref, send_ref, acc = rest[-3:]
    me = me_ref[0]
    for k, n in enumerate((n0, n1, n2, n3)):
        rows = pl.ds(pl.multiple_of((me ^ k) * each, each), each)
        term = dot(n[...], g_ref[rows, :], TN)
        if k:
            acc[...] += term
        else:
            acc[...] = term
    tall = keep_ref.shape[1]
    three = g_ref.shape[1]
    for z in range(4):
        for y in range(2):
            b = block_of(y, z, dp_ref[0])
            half, spot = spot_of(y, z, "y")
            o = (keep_ref, send_ref)[half]
            rows = pl.ds(pl.multiple_of(b * tall, tall), tall)
            o[spot, :, :three] = acc[rows, :].astype(bf16)
            if len(rest) > 3:
                out = rest[0][:, rows].astype(f32) + rest[1][:, rows].astype(f32) + rest[2][:, rows].astype(f32)
                for i in range(out.shape[0] // tall):
                    o[spot, :, three + i * tall : three + (i + 1) * tall] = out[i * tall : (i + 1) * tall].astype(bf16)


def wgrad_qkv(me, dp, grad, n_list, w_parts=()):
    length, three = grad.shape
    each, width = n_list[0].shape
    extra = w_parts[0].shape[0] if w_parts else 0
    vm = pl.BlockSpec(memory_space=pltpu.VMEM)
    return pl.pallas_call(
        functools.partial(wgrad_qkv_kernel, each=each),
        in_specs=[smem(), smem()] + [vm] * (5 + len(w_parts)),
        out_specs=[vm] * 2,
        out_shape=[shaped((4, width // 8, three + extra), bf16)] * 2,
        scratch_shapes=[pltpu.VMEM((width, three), f32)],
        compiler_params=params(),
        cost_estimate=cost(2 * length * width * three, 2 * length * (width + three) + 2 * width * (three + 4 * extra)),
        name="wgrad_qkv",
    )(me, dp, grad, *n_list, *w_parts)


def add_split_kernel(a_ref, b_ref, o0, o1):
    half = o0.shape[0]
    o0[...] = (a_ref[:half].astype(f32) + b_ref[:half].astype(f32)).astype(bf16)
    o1[...] = (a_ref[half:].astype(f32) + b_ref[half:].astype(f32)).astype(bf16)


def add_split(a, b):
    vm = pl.BlockSpec(memory_space=pltpu.VMEM)
    half = (a.shape[0] // 2,) + a.shape[1:]
    return pl.pallas_call(
        add_split_kernel,
        in_specs=[vm] * 2,
        out_specs=[vm] * 2,
        out_shape=[shaped(half, bf16)] * 2,
        compiler_params=params(),
        cost_estimate=cost(a.size, 6 * a.size),
        name="add_split",
    )(a, b)


class Chain:
    def __init__(self, kept, sent, lead="y"):
        self.single = lax.axis_size("dp") != 8
        self.steps = 0
        self.kept = kept
        if self.single:
            self.parts = (lax.psum(kept, "dp"), lax.psum(sent, "dp"))
            return
        self.bits = (1, 2, 4, 2, 1) if lead == "y" else (2, 1, 4, 1, 2)
        self.flying = swap(sent, self.bits[0], "dp")

    def close(self, *others):
        if self.single:
            return (self.kept,)
        self.flying = join(self.flying, *others)[0]
        return (self.flying,)

    def step(self, *others):
        if self.single:
            return (self.kept,)
        self.steps += 1
        got = join(self.flying, *others)[0]
        if self.steps == 1:
            self.kept, sent = add_split(self.kept, got)
        elif self.steps == 2:
            self.kept = sent = add_low(self.kept, got)
        elif self.steps == 3:
            self.kept = sent = add_low(self.kept, got[::-1])
        elif self.steps == 4:
            self.kept = sent = jnp.concatenate([self.kept, got], axis=0)
        else:
            self.parts = (self.kept, got)
            return (got,)
        self.flying = swap(sent, self.bits[self.steps], "dp")
        return (sent,)

    def finish(self, *others):
        while not self.single and self.steps < 5:
            self.step(*others)
        return self.parts


def pieces(refs, lead="y"):
    for y in range(2):
        for z in range(4):
            half, spot = spot_of(y, z, lead)
            yield y, z, refs[half], spot


def finish_down_kernel(dp_ref, k_ref, s_ref, o_ref):
    wide = k_ref.shape[2]
    for y, z, ref, spot in pieces((k_ref, s_ref)):
        cols = pl.ds(pl.multiple_of(block_of(y, z, dp_ref[0]) * wide, wide), wide)
        o_ref[:, cols] = ref[spot].astype(f32)


def finish_down(dp, parts, shape):
    vm = pl.BlockSpec(memory_space=pltpu.VMEM)
    return pl.pallas_call(
        finish_down_kernel,
        in_specs=[smem()] + [vm] * 2,
        out_specs=vm,
        out_shape=shaped(shape, f32),
        compiler_params=params(),
        cost_estimate=cost(shape[0] * shape[1], 6 * shape[0] * shape[1]),
        name="finish_down",
    )(dp, *parts)


def finish_cols_kernel(dp_ref, k_ref, s_ref, w_ref, gain_ref, *rest, lead):
    o_ref, part_ref = rest[-2:]
    wide = k_ref.shape[2]
    for y, z, ref, spot in pieces((k_ref, s_ref), lead):
        cols = pl.ds(pl.multiple_of(block_of(y, z, dp_ref[0]) * wide, wide), wide)
        grad = ref[spot].astype(f32)
        o_ref[0, :, cols] = grad
        part_ref[:, cols] = jnp.sum(grad * w_ref[0, :, cols].astype(f32), axis=0, keepdims=True) / gain_ref[:, cols]


def finish_cols(dp, parts, w, gain, index, into=None, lead="y"):
    two, hid, width = w.shape
    one = pl.BlockSpec((1, hid, width), lambda i: (index, 0, 0))
    extra = () if into is None else (into,)
    return pl.pallas_call(
        functools.partial(finish_cols_kernel, lead=lead),
        grid=(1,),
        in_specs=[smem(), whole(*parts[0].shape), whole(*parts[1].shape), one, whole(1, width)] + [pl.BlockSpec(memory_space=pl.ANY)] * len(extra),
        out_specs=[one, whole(1, width)],
        out_shape=[shaped(w.shape, f32), shaped((1, width), f32)],
        input_output_aliases={5: 0} if extra else {},
        compiler_params=params(),
        cost_estimate=cost(4 * hid * width, 8 * hid * width),
        name="finish_cols",
    )(dp, *parts, w, gain, *extra)


def half_gain_kernel(dp_ref, a_ref, b_ref, w_ref, gain_ref, o_ref, *, y):
    tall = a_ref.shape[1]
    o_ref[...] = jnp.zeros_like(o_ref)
    for z in range(4):
        _, spot = spot_of(y, z, "y")
        rows = pl.ds(pl.multiple_of(block_of(y, z, dp_ref[0]) * tall, tall), tall)
        total = None
        for idx in range(3):
            part = slice(idx * LANES, (idx + 1) * LANES)
            for pair, ref in enumerate((a_ref, b_ref)):
                term = ref[spot, :, part].astype(f32) * w_ref[idx, rows, pair * LANES : (pair + 1) * LANES].astype(f32)
                total = term if total is None else total + term
        total = jnp.sum(total, axis=1, keepdims=True)
        o_ref[:, rows] = jnp.transpose(jnp.broadcast_to(total, (tall, LANES)))[0:1] / gain_ref[:, rows]


def half_gain(dp, first, second, w, gain, y):
    vm = pl.BlockSpec(memory_space=pltpu.VMEM)
    width = w.shape[1]
    return pl.pallas_call(
        functools.partial(half_gain_kernel, y=y),
        in_specs=[smem()] + [vm] * 4,
        out_specs=vm,
        out_shape=shaped((1, width), f32),
        compiler_params=params(),
        cost_estimate=cost(2 * w.size, 4 * w.size),
        name="half_gain",
    )(dp, first, second, w, gain)


def finish_qkv_kernel(dp_ref, ak, sk, bk, bs, o_ref, out_ref):
    tall = ak.shape[1]
    cols = out_ref.shape[0]
    three = 3 * LANES
    for (y, z, a, spot), (_, _, b, _) in zip(pieces((ak, sk)), pieces((bk, bs))):
        rows = pl.ds(pl.multiple_of(block_of(y, z, dp_ref[0]) * tall, tall), tall)
        for idx in range(3):
            part = slice(idx * LANES, (idx + 1) * LANES)
            o_ref[idx, rows, :LANES] = a[spot, :, part].astype(f32)
            o_ref[idx, rows, LANES:] = b[spot, :, part].astype(f32)
        for k in range(cols // tall):
            out_ref[k * tall : (k + 1) * tall, rows] = a[spot, :, three + k * tall : three + (k + 1) * tall].astype(f32)


def finish_qkv(dp, first, second, cols):
    vm = pl.BlockSpec(memory_space=pltpu.VMEM)
    width = 8 * first[0].shape[1]
    return pl.pallas_call(
        finish_qkv_kernel,
        in_specs=[smem()] + [vm] * 4,
        out_specs=[vm] * 2,
        out_shape=[shaped((3, width, cols), f32), shaped((cols, width), f32)],
        compiler_params=params(),
        cost_estimate=cost(8 * cols * width, 24 * cols * width),
        name="finish_qkv",
    )(dp, *first, *second)


def on_device(tokens, counts, gain_attn, gain_ffn, w_qkv, w_out, w_gate_up, w_down, cotangent):
    rows, width = tokens.shape
    columns = w_qkv.shape[2]
    hid = w_gate_up.shape[2]
    me = lax.axis_index("mp").astype(jnp.int32).reshape(1)
    dp = jnp.zeros((1,), jnp.int32)
    if lax.axis_size("dp") == 8:
        dp = lax.axis_index("dp").astype(jnp.int32).reshape(1)
    gain_a = gain_attn.reshape(1, width)
    gain_f = gain_ffn.reshape(1, width)
    qkv_w = jnp.transpose(w_qkv, (1, 0, 2))
    gate_up_w = jnp.transpose(w_gate_up, (1, 2, 0))

    n0 = norm(tokens, gain_a)
    n2 = far_of(n0)
    n1 = swap(n0, 1)
    p0, p1 = project(n0, n1, qkv_w)
    n2, p0, p1 = join(n2, p0, p1)
    n = [n0, n1, n2, swap(n2, 1)]
    out2 = far_of(after(w_out, n2))
    cot2 = far_of(after(cotangent, *n[2:]))
    qkv, attended, lse, *a = attn_fwd(me, counts, p0, p1, n[2], n[3], qkv_w)
    out2, *a = join(out2, *a)
    out_w = [w_out, swap(w_out, 1), out2, swap(out2, 1)]
    a = exchange_rel(a)
    cot2, *a = join(cot2, *a)
    cot = [cotangent, swap(cotangent, 1), cot2, swap(cot2, 1)]
    middle, m0 = middle_of(tokens, a, out_w, gain_f)
    m2 = far_of(m0)
    m1 = swap(m0, 1)
    hid_a, gg_a, gu_a, d0, d1, g0, g1 = ffn(m0, m1, cot[0], cot[1], gate_up_w, w_down)
    m2, hid_a, gg_a, gu_a, d0, d1, g0, g1 = join(m2, hid_a, gg_a, gu_a, d0, d1, g0, g1)
    m = [m0, m1, m2, swap(m2, 1)]
    g1, d1 = swap(g1, 1), swap(d1, 1)
    hid_b, gg_b, gu_b, d2, d3, g2, g3 = ffn(m[2], m[3], cot[2], cot[3], gate_up_w, w_down)
    g1, d1, g2, g3 = join(g1, d1, g2, g3)
    sent = add_low(g2, swap(g3, 1))
    s2 = far_of(sent)
    d3 = swap(after(d3, sent), 1)
    down = Chain(*wgrad_cols(dp, after(hid_a, sent), hid_b, cot))
    parts = wgrad_cols(dp, after(gu_a, down.kept), gu_b, m)
    up = Chain(*parts)
    parts = wgrad_cols(dp, after(gg_a, up.kept), gg_b, m, "z")
    gate_kept, gate_sent = parts
    lat_sent = add_low(d2, d3)
    x = down.step(gate_kept)
    s2 = join(s2, lat_sent, *x)[0]
    grad_middle, low, *ga = grad_middle_of(cotangent, middle, (g0, g1, s2), gain_f, out_w)
    d_list = exchange_rel(ga)
    gate = Chain(gate_kept, after(gate_sent, low), "z")
    w0, w1, w2, w3 = wgrad_out(low, a)
    x = up.step(w0) + down.step(w0)
    d_list = join(*d_list, *x)[:4]
    w1, w3 = join(swap(w1, 1), swap(w3, 1), *d_list)[:2]
    w_sent = add_low(w2, w3)
    w2 = far_of(w_sent)
    grad0 = attn_bwd(me, counts, qkv, d_list, attended, lse, 0, (w_sent,))
    w2 = join(w2, grad0)[0]
    x = down.step(grad0) + up.step(grad0) + gate.step(grad0)
    parts = wgrad_qkv(me, dp, after(grad0, *x), n, (w0, w1, w2))
    first = Chain(*parts)
    lat2 = far_of(after(lat_sent, first.kept))
    grad1 = attn_bwd(me, counts, qkv, d_list, attended, lse, 1, (first.kept,))
    x = down.step(grad1) + up.step(grad1) + gate.step(grad1) + first.close(grad1) + (lat2,)
    t2, t3 = qkv_dgrad(me, grad0, after(grad1, *x), qkv_w, 2, 3)
    t3 = swap(t3, 1)
    t0, t1 = qkv_dgrad(me, grad0, after(grad1, t2), qkv_w, 0, 1)
    t3 = join(t3, t0)[0]
    sent = add_low(t2, t3)
    t2 = far_of(sent)
    x = first.step(sent)
    parts = wgrad_qkv(me, dp, after(grad1, *x), n)
    second = Chain(*parts)
    latents = middle + d0.astype(f32) + d1.astype(f32) + after(lat2, second.kept).astype(f32)
    t1 = swap(after(t1, latents), 1)
    x = up.step(latents)
    x = first.step(*x)
    x = gate.step(*x)
    x = second.step(*x)
    grad_w_down = finish_down(dp, down.finish(*x), (hid, width))
    x = first.step(grad_w_down)
    x = second.step(*x)
    t0, t1, t2 = join(t0, t1, t2, *x)[:3]
    grad_tokens = grad_tokens_of(grad_middle, tokens, (t0, t1, t2), gain_a)
    x = first.step(grad_tokens)
    x = second.step(*x)
    grad_w_gate_up, part_u = finish_cols(dp, up.finish(*x), gate_up_w, gain_f, 1)
    x = second.step(grad_w_gate_up)
    if lax.axis_size("dp") == 8:
        gain_1 = half_gain(dp, first.kept, after(second.kept, *x), qkv_w, gain_a, 0)
        gain_1 = gain_1 + swap(gain_1, 1) + swap(gain_1, 2) + swap(gain_1, 3)
        gain_1 = gain_1 + swap(gain_1, 1, "dp")
    else:
        parts = [half_gain(dp, first.parts[y], second.parts[y], qkv_w, gain_a, y) for y in range(2)]
        gain_1 = parts[0] + parts[1]
        gain_1 = gain_1 + swap(gain_1, 1) + swap(gain_1, 2) + swap(gain_1, 3)
    grad_w_gate_up, part_g = finish_cols(dp, gate.finish(*x), gate_up_w, gain_f, 0, grad_w_gate_up, "z")
    gain_2 = part_u + part_g
    gain_2 = gain_2 + swap(gain_2, 1) + swap(gain_2, 2) + swap(gain_2, 3)
    grad_w_qkv, grad_w_out = finish_qkv(dp, first.finish(grad_w_gate_up), second.finish(grad_w_gate_up), columns)
    gains = (gain_1, gain_2)
    grad_w_qkv = jnp.transpose(grad_w_qkv, (1, 0, 2))
    grad_w_gate_up = jnp.transpose(grad_w_gate_up, (2, 0, 1))
    return (
        latents,
        grad_tokens,
        gains[0].reshape(width),
        gains[1].reshape(width),
        grad_w_qkv,
        grad_w_out,
        grad_w_gate_up,
        grad_w_down,
    )


def solution(mesh):
    placed = (
        P(("dp", "mp"), None),
        P("dp"),
        P(),
        P(),
        P(None, None, "mp"),
        P("mp", None),
        P(None, None, "mp"),
        P("mp", None),
        P(("dp", "mp"), None),
    )
    return jax.shard_map(
        on_device,
        mesh=mesh,
        in_specs=placed,
        out_specs=(
            P(("dp", "mp"), None),
            P(("dp", "mp"), None),
            P(),
            P(),
            P(None, None, "mp"),
            P("mp", None),
            P(None, None, "mp"),
            P("mp", None),
        ),
        check_vma=False,
    )
```
